128 devices in a mesh: row: 4 (over y_hi, core), col: 4 (over z), rep: 8 (over x, y_lo).
Axes of the slice: x: 4, y: 4 (y_hi: 2, y_lo: 2; y = y_hi * 2 + y_lo), z: 4, core: 2. Of those that a mesh axis runs over, the one named last changes fastest.
Arguments:
- features: bfloat16 [32768, 512], P(('row', 'col', 'rep')), may hold values from -6 to 6
- weight: bfloat16 [512, 512], replicated, may hold values from -0.25 to 0.25
- tile_values: bfloat16 [24576, 128, 128], P(('row', 'col', 'rep')), as said below
- tile_rows: int32 [24576], P(('row', 'col', 'rep')), may hold values from 0 to 63
- tile_cols: int32 [24576], P(('row', 'col', 'rep')), may hold values from 0 to 7
- tile_count: int32 [128], P(('row', 'col', 'rep')), may hold values from 48 to 192, as said below
- output_grad: bfloat16 [32768, 512], P(('row', 'col', 'rep')), may hold values from -6 to 6
Outputs:
- output: bfloat16 [32768, 512], P(('row', 'col', 'rep'))
- grad_features: bfloat16 [32768, 512], P(('row', 'col', 'rep'))
- grad_weight: float32 [512, 512], replicated
The draws below stay inside these ranges and needn't reach their ends.
Inputs may be any that keep to these rules, and one draw needn't show every extreme that they name: The live tiles of a device are the first tile_count of its 192 slots; in every draw some device has all 192 slots live. `tile_values`: entries are zero or positive.
All inputs are finite; a program needn't handle non-finite values.
Results may differ from the reference program's by a relative error of at most 0.0056.
Values may be sent and summed in bfloat16 or wider, within the bound.
A program may use at most 128 MiB of HBM per device.

```python
import jax
import jax.numpy as jnp
from jax import lax

F = 512
TILE = 128
NODE_DEV = 256
TILES_DEV = 192
NODES = 32768
ROW_TILES = 64
COL_TILES = 8
N_COL = 4
N_REP = 8
DEVICES = 128


def draw_tile_values(key, part):
    key = jax.random.fold_in(key, 11)
    key_mask, key_mag = jax.random.split(key)
    shape = (DEVICES * TILES_DEV, TILE, TILE)
    pattern = jax.random.bernoulli(key_mask, 0.4, shape).astype(jnp.float32)
    scale = (0.25 * TILES_DEV * TILE * TILE / NODE_DEV) ** (-0.5)
    magnitude = jax.random.uniform(key_mag, shape, jnp.float32, 0.5, 1.5)
    return (pattern * magnitude * scale).astype(jnp.bfloat16)


def draw_tile_count(key, part):
    key = jax.random.fold_in(key, 23)
    key_count, key_spot = jax.random.split(key)
    counts = jax.random.randint(key_count, (DEVICES,), TILES_DEV // 4, TILES_DEV + 1)
    spot = jax.random.randint(key_spot, (), 0, DEVICES)
    return counts.at[spot].set(TILES_DEV).astype(jnp.int32)


def set_ends(values, key, smallest, top_value):
    longest = values.shape.index(max(values.shape))
    spots = []
    for shift in (0, 1):
        where = [jax.random.randint(jax.random.fold_in(key, axis), (), 0, length) for axis, length in enumerate(values.shape)]
        where[longest] = (where[longest] + shift) % values.shape[longest]
        spots.append(tuple(where))
    return values.at[spots[0]].set(smallest).at[spots[1]].set(top_value)


def block_scale(own_key, extent, shards, smallest, high):
    factor_of, own = 1.0, jax.random.fold_in(own_key, 6)
    for position, blocks in shards:
        steps = jnp.exp(jax.random.uniform(jax.random.fold_in(own, position), (blocks,), jnp.float32, smallest / len(shards), high / len(shards)))
        factor_of = factor_of * jnp.repeat(steps, extent[position] // blocks).reshape([-1 if axis == position else 1 for axis in range(len(extent))])
    return factor_of


def scatter_about(own_key, extent, scale, reach, pieces=(), held_as=jnp.bfloat16):
    values = scale * jax.random.normal(own_key, extent, jnp.float32)
    if pieces:
        values = values * block_scale(own_key, extent, pieces, -0.22, 0.18)
    return jnp.clip(values, -reach, reach).astype(held_as)


def setup_inputs(seed: int = 0) -> dict:
    splits = jax.random.split(jax.random.key(seed), 8)
    return {
        "features": scatter_about(splits[0], (NODES, F), 1.0, 6.0, ((0, 128),)),
        "weight": scatter_about(splits[1], (F, F), F ** -0.5, 0.25),
        "tile_values": draw_tile_values(jax.random.fold_in(splits[7], 71), 0),
        "tile_rows": set_ends(jax.random.randint(splits[3], (DEVICES * TILES_DEV,), 0, ROW_TILES), jax.random.fold_in(splits[3], 1), 0, ROW_TILES - 1).astype(jnp.int32),
        "tile_cols": set_ends(jax.random.randint(splits[4], (DEVICES * TILES_DEV,), 0, COL_TILES), jax.random.fold_in(splits[4], 1), 0, COL_TILES - 1).astype(jnp.int32),
        "tile_count": draw_tile_count(jax.random.fold_in(splits[7], 71), 0),
        "output_grad": scatter_about(splits[6], (NODES, F), 1.0, 6.0, ((0, 128),)),
    }


def reference(features, weight, tile_values, tile_rows, tile_cols, tile_count, output_grad):
    width = features.shape[1]
    groups = N_COL * N_REP
    per = NODE_DEV // TILE
    node_tiles = NODES // TILE
    projected = jnp.dot(features, weight, preferred_element_type=jnp.float32).astype(jnp.bfloat16)
    slots = jnp.arange(DEVICES * TILES_DEV, dtype=jnp.int32)
    device = (slots // TILES_DEV).astype(jnp.int32)
    live = (slots % TILES_DEV < tile_count[device]).astype(jnp.float32)
    row_tile = (device // groups * ROW_TILES + tile_rows).astype(jnp.int32)
    col_tile = ((tile_cols // per * groups + device % groups) * per + tile_cols % per).astype(jnp.int32)
    values = tile_values.astype(jnp.float32) * live[:, None, None]
    values = values.reshape(DEVICES, TILES_DEV, TILE, TILE)
    row_tile = row_tile.reshape(DEVICES, TILES_DEV)
    col_tile = col_tile.reshape(DEVICES, TILES_DEV)
    source = projected.astype(jnp.float32).reshape(node_tiles, TILE, width)

    def forward(total, item):
        block, rows, cols = item
        prod = jnp.einsum('tij,tjf->tif', block, source[cols], precision=lax.Precision.HIGHEST)
        return (total.at[rows].add(prod), None)
    aggregated, _ = lax.scan(forward, jnp.zeros((node_tiles, TILE, width), jnp.float32), (values, row_tile, col_tile))
    aggregated = aggregated.reshape(NODES, width)
    output, pullback = jax.vjp(jax.nn.gelu, aggregated)
    grad_agg = pullback(output_grad.astype(jnp.float32))[0].astype(jnp.bfloat16)
    grad_source = grad_agg.astype(jnp.float32).reshape(node_tiles, TILE, width)

    def backward(total, item):
        block, rows, cols = item
        prod = jnp.einsum('tij,tif->tjf', block, grad_source[rows], precision=lax.Precision.HIGHEST)
        return (total.at[cols].add(prod), None)
    grad_proj, _ = lax.scan(backward, jnp.zeros((node_tiles, TILE, width), jnp.float32), (values, row_tile, col_tile))
    grad_proj = grad_proj.reshape(NODES, width)
    grad_features = jnp.dot(grad_proj, weight.astype(jnp.float32).T, precision=lax.Precision.HIGHEST).astype(jnp.bfloat16)
    grad_weight = jnp.dot(features.astype(jnp.float32).T, grad_proj, precision=lax.Precision.HIGHEST)
    return (output.astype(jnp.bfloat16), grad_features, grad_weight)
```

```python
import math

import jax
import jax.numpy as jnp
from jax import lax
from jax.experimental import pallas as pl
from jax.experimental.pallas import tpu as pltpu
from jax.sharding import PartitionSpec as P

MESH = pl.DeviceIdType.MESH
F32, BF16 = jnp.float32, jnp.bfloat16
TILE = 128
NODES = 256
HALF = 256
WIDTH = 512
PEERS = 4
CHUNKS = 32
COLS = 1024
LOADS = 8
C0 = math.sqrt(2.0 / math.pi)


def place_kernel(rows, cols, count, values, dense, tiles, block, in_sem, out_sem):
    slots = tiles.shape[0]
    load = pltpu.make_async_copy(values, tiles, in_sem)
    load.start()

    def clear(i, carry):
        block[pl.ds(pl.multiple_of(i * 64, 64), 64), :] = jnp.zeros((64, COLS), BF16)
        return carry

    lax.fori_loop(0, block.shape[0] // 64, clear, 0)
    load.wait()

    def place(t, carry):
        row = pl.ds(pl.multiple_of(rows[t] * TILE, TILE), TILE)
        col = pl.ds(pl.multiple_of(cols[t] * TILE, TILE), TILE)
        block[row, col] = block[row, col] + tiles[t]
        return carry

    lax.fori_loop(0, jnp.minimum(count[0], slots), place, 0)
    store = pltpu.make_async_copy(block, dense, out_sem)
    store.start()
    store.wait()


def place_tiles(values, rows, cols, count):
    slots = values.shape[0]
    smem = pl.BlockSpec(memory_space=pltpu.SMEM)
    return pl.pallas_call(
        place_kernel,
        out_shape=jax.ShapeDtypeStruct((CHUNKS * NODES, COLS), BF16),
        in_specs=[smem, smem, smem, pl.BlockSpec(memory_space=pl.ANY)],
        out_specs=pl.BlockSpec(memory_space=pl.ANY),
        scratch_shapes=[
            pltpu.VMEM((slots, TILE, TILE), BF16),
            pltpu.VMEM((CHUNKS * NODES, COLS), BF16),
            pltpu.SemaphoreType.DMA,
            pltpu.SemaphoreType.DMA,
        ],
        compiler_params=pltpu.CompilerParams(vmem_limit_bytes=40 * 2**20),
        name="place_tiles",
    )(rows, cols, count, values)


def dot(a, b):
    return jnp.dot(a, b, preferred_element_type=F32)


def split(v):
    high = v.astype(BF16)
    return high, (v - high.astype(F32)).astype(BF16)


def layer_kernel(
    features, weight, dense_hbm, output_grad, output, grad_features, grad_weight,
    dense, feats, source, far_out, near_out, far_in, near_in, far2_out, near2_out, far2_in, near2_in,
    pair_out, pair_in, kept, grads, terms, col_out, col_in, col2_out, col2_in,
    wcore_out, wcore_in, wx, wx_out, wx_in, wz, wz_out, wz_in, wy, wy_out, wy_in, ygath, wfull,
    load_sem, a_s, a_r, far_s, far_r, near_s, near_r, far2_s, far2_r, near2_s, near2_r, pair_s, pair_r,
    g_s, g_r, c_s, c_r, c2_s, c2_r, wc_s, wc_r, wx_s, wx_r, wz_s, wz_r, wy_s, wy_r,
    gy_s, gy_r, gz_s, gz_r, gx_s, gx_r, gc_s, gc_r,
):
    row, z, rep = lax.axis_index("row"), lax.axis_index("col"), lax.axis_index("rep")
    high, core = row // 2, row % 2
    x, low = rep // 2, rep % 2

    def at(high_=None, core_=None, z_=None, x_=None, low_=None):
        pick = lambda v, own: own if v is None else v
        return {
            "row": pick(high_, high) * 2 + pick(core_, core),
            "col": pick(z_, z),
            "rep": pick(x_, x) * 2 + pick(low_, low),
        }

    def along(axis, step):
        return at(x_=(x + step) % 4) if axis == "x" else at(z_=(z + step) % 4)

    axes = (("x", "z"), ("z", "x"))
    spots = ((x, z), (z, x))

    def chunk(p, first, second, pair):
        if p == 0:
            return second * 8 + first * 2 + pair
        return first * 8 + second * 2 + pair

    def copy(src, dst, s, r, device):
        return pltpu.make_async_remote_copy(
            src_ref=src, dst_ref=dst, send_sem=s, recv_sem=r, device_id=device, device_id_type=MESH
        )

    cores, pair, across = at(core_=1 - core), at(low_=1 - low), at(high_=1 - high)
    ypeer = (pair, across, at(high_=1 - high, low_=1 - low))

    def loop(n, body):
        def step(i, carry):
            body(i)
            return carry

        lax.fori_loop(0, n, step, 0)

    per_load = CHUNKS * NODES // LOADS

    def load(i):
        span = pl.ds(pl.multiple_of(i * per_load, per_load), per_load)
        return pltpu.make_async_copy(dense_hbm.at[span], dense.at[span], load_sem.at[i])

    loop(LOADS, lambda i: load(i).start())

    barrier = pltpu.get_barrier_semaphore()
    partners = [along(axis, step) for axis in ("x", "z") for step in (1, 2, 3)] + list(ypeer) + [cores]
    for device in partners:
        pl.semaphore_signal(barrier, inc=1, device_id=device, device_id_type=MESH)
    pl.semaphore_wait(barrier, len(partners))

    row_across, row_core, row_last = (1 - high) * 2 + core, high * 2 + 1 - core, (1 - high) * 2 + 1 - core
    gather = (
        lambda r: copy(features, feats.at[r], a_s.at[0], a_r.at[0], across),
        lambda r: copy(features, feats.at[r], a_s.at[1], a_r.at[1], cores),
        lambda r: copy(feats.at[r], feats.at[r], a_s.at[2], a_r.at[2], cores),
    )
    gather[0](row).start()
    gather[1](row).start()
    feats[row] = features[...]

    def project(r):
        span = pl.ds(pl.multiple_of(r * NODES, NODES), NODES)
        source[span, :] = dot(feats[r], weight[...]).astype(BF16)

    project(row)
    gather[1](row_core).wait_recv()
    project(row_core)
    gather[0](row_across).wait_recv()
    gather[2](row_across).start()
    project(row_across)
    gather[2](row_last).wait_recv()
    project(row_last)
    loop(LOADS, lambda i: load(i).wait())

    def partial(p, first, second, pair_):
        start = pl.multiple_of(chunk(p, first, second, pair_) * NODES, NODES)
        return dot(dense[pl.ds(start, NODES), :], source[:, p * HALF:(p + 1) * HALF])

    steps = (3, 1)

    def far(p, o, d):
        return copy(far_out.at[p, o, d], far_in.at[p, o, d], far_s.at[p, o, d], far_r.at[p, o, d], along(axes[p][0], steps[d]))

    def near(p, o, d, y):
        return copy(
            near_out.at[p, o, d, y], near_in.at[p, o, d, y], near_s.at[p, o, d, y], near_r.at[p, o, d, y],
            along(axes[p][0], steps[d]),
        )

    def order(t):
        late = t // 2
        return (1 - late) * (2 - t) + late * 3 * (3 - t)

    def send_far(t):
        o = order(t)
        for p in range(2):
            first, second = spots[p]
            for d in range(2):
                far_out[p, o, d] = partial(p, (first + 2) % 4, (second + o) % 4, d).astype(BF16)
                far(p, o, d).start()

    def send_near(t):
        o = order(t)
        for p in range(2):
            first, second = spots[p]
            for d in range(2):
                near_out[p, o, d, 1 - d] = partial(p, (first + steps[d]) % 4, (second + o) % 4, 1 - d).astype(BF16)
                near(p, o, d, 1 - d).start()

    def send_added(t):
        o = order(t)
        for p in range(2):
            first, second = spots[p]
            for d in range(2):
                value = partial(p, (first + steps[d]) % 4, (second + o) % 4, d)
                far(p, o, d).wait_recv()
                near_out[p, o, d, d] = (value + far_in[p, o, d].astype(F32)).astype(BF16)
                near(p, o, d, d).start()

    loop(4, send_far)
    loop(4, send_near)
    loop(4, send_added)

    def far2(p, d):
        return copy(far2_out.at[p, d], far2_in.at[p, d], far2_s.at[p, d], far2_r.at[p, d], along(axes[p][1], steps[d]))

    def near2(p, d, y):
        return copy(
            near2_out.at[p, d, y], near2_in.at[p, d, y], near2_s.at[p, d, y], near2_r.at[p, d, y], along(axes[p][1], steps[d])
        )

    def first_sum(p, o, y):
        value = partial(p, spots[p][0], (spots[p][1] + o) % 4, y)
        near(p, o, 0, y).wait_recv()
        near(p, o, 1, y).wait_recv()
        return value + near_in[p, o, 0, y].astype(F32) + near_in[p, o, 1, y].astype(F32)

    for p in range(2):
        for d in range(2):
            far2_out[p, d] = first_sum(p, 2, d).astype(BF16)
            far2(p, d).start()
    for o, d in ((1, 1), (3, 0)):
        for p in range(2):
            near2_out[p, d, 1 - d] = first_sum(p, o, 1 - d).astype(BF16)
            near2(p, d, 1 - d).start()
            value = first_sum(p, o, d)
            far2(p, d).wait_recv()
            near2_out[p, d, d] = (value + far2_in[p, d].astype(F32)).astype(BF16)
            near2(p, d, d).start()
    for p in range(2):
        for y in range(2):
            kept[p, y] = first_sum(p, 0, y)

    def pairs(p):
        return copy(pair_out.at[p], pair_in.at[p], pair_s.at[p], pair_r.at[p], pair)

    for p in range(2):
        for y in range(2):
            for d in range(2):
                near2(p, d, y).wait_recv()
            kept[p, y] = kept[p, y] + near2_in[p, 0, y].astype(F32) + near2_in[p, 1, y].astype(F32)
        pair_out[p] = kept[p, 1 - low].astype(BF16)
        pairs(p).start()

    def slot(p, i, j, y):
        back = {1: 3, 3: 1}
        if i == 0:
            device = along(axes[p][1], 1 if (j == 3 or (j == 2 and y == 1)) else 3)
            src = grads.at[p, 0, 0, y] if j != 2 else grads.at[p, 0, 1 if y == 0 else 3, y]
        else:
            device = along(axes[p][0], 1 if (i == 3 or (i == 2 and y == 1)) else 3)
            src = grads.at[p, 0, j, y] if i != 2 else grads.at[p, 1 if y == 0 else 3, j, y]
        return copy(src, grads.at[p, i, j, y], g_s.at[p, i, j, y], g_r.at[p, i, j, y], device)

    def own_block(p, y):
        return copy(grads.at[p, 0, 0, y], grads.at[p, 0, 0, y], g_s.at[p, 0, 0, 0], g_r.at[p, 0, 0, 0], pair)

    for p in range(2):
        pairs(p).wait_recv()
        v = kept[p, low] + pair_in[p].astype(F32)
        span = slice(p * HALF, (p + 1) * HALF)
        t = jnp.tanh(C0 * (v + 0.044715 * (v * v * v)))
        output[:, span] = (0.5 * v * (1.0 + t)).astype(BF16)
        slope = 0.5 * (1.0 + t) + 0.5 * v * (1.0 - t * t) * (C0 * (1.0 + 3.0 * 0.044715 * (v * v)))
        grad = (output_grad[:, span].astype(F32) * slope).astype(BF16)
        grads[p, 0, 0, low] = grad.astype(F32).T.astype(BF16)
        own_block(p, low).start()

    for p in range(2):
        own_block(p, 1 - low).wait_recv()
        for j in (1, 3):
            for y in range(2):
                slot(p, 0, j, y).start()
        for i in (1, 3):
            for y in range(2):
                slot(p, i, 0, y).start()

    def product(p, i, j):
        first, second = spots[p]
        total = None
        for y in range(2):
            start = pl.multiple_of(chunk(p, (first + i) % 4, (second + j) % 4, y) * NODES, NODES)
            term = dot(grads[p, i, j, y], dense[pl.ds(start, NODES), :])
            total = term if total is None else total + term
        return total

    def add(p, i, j, fresh=False):
        total = product(p, i, j)
        for r in range(PEERS):
            part = total[:, r * NODES:(r + 1) * NODES]
            terms[p, r] = part if fresh else terms[p, r] + part

    for p in range(2):
        add(p, 0, 0, fresh=True)

    def arrive_first(j):
        for p in range(2):
            slot(p, 1, j, 0).wait_recv()
            slot(p, 2, j, 0).start()
            slot(p, 3, j, 1).wait_recv()
            slot(p, 2, j, 1).start()

    def use_first(j):
        for p in range(2):
            slot(p, 1, j, 1).wait_recv()
            add(p, 1, j)
            slot(p, 3, j, 0).wait_recv()
            add(p, 3, j)

    for p in range(2):
        slot(p, 0, 1, 0).wait_recv()
        slot(p, 0, 2, 0).start()
        slot(p, 0, 3, 1).wait_recv()
        slot(p, 0, 2, 1).start()
    for p in range(2):
        slot(p, 0, 1, 1).wait_recv()
        slot(p, 0, 3, 0).wait_recv()
        for j in (1, 3):
            for i in (1, 3):
                for y in range(2):
                    slot(p, i, j, y).start()
    arrive_first(0)
    for p in range(2):
        add(p, 0, 1)
        add(p, 0, 3)
    for p in range(2):
        for y in range(2):
            slot(p, 0, 2, y).wait_recv()
        for i in (1, 3):
            for y in range(2):
                slot(p, i, 2, y).start()
    for p in range(2):
        add(p, 0, 2)
    use_first(0)

    def middle(t):
        j = (1 - t // 2) * (2 * t + 1) + (t // 2) * 2
        arrive_first(j)
        use_first(j)

    loop(3, middle)

    def last(j):
        for p in range(2):
            for y in range(2):
                slot(p, 2, j, y).wait_recv()
            add(p, 2, j)

    loop(4, last)

    def cols1(h):
        return copy(col_out.at[h], col_in.at[h], c_s.at[h], c_r.at[h], cores)

    cols2 = copy(col2_out, col2_in, c2_s, c2_r, across)
    for h in range(2):
        for p in range(2):
            col_out[h, p] = terms[p, 2 * h + 1 - core].astype(BF16)
        cols1(h).start()

    def weight_half(p):
        total = jnp.zeros((HALF, WIDTH), F32)
        for r in range(PEERS):
            top, rest = split(terms[p, r])
            total = total + dot(top, feats[r]) + dot(rest, feats[r])
        return total

    weight_core = copy(wcore_out, wcore_in, wc_s, wc_r, cores)
    wcore_out[...] = weight_half(1 - core).astype(BF16)
    weight_core.start()
    wx[...] = weight_half(core).reshape(4, 64, WIDTH)
    weight_core.wait_recv()
    wx[...] = wx[...] + wcore_in[...].astype(F32).reshape(4, 64, WIDTH)

    def weight_x(s):
        return copy(wx_out.at[s], wx_in.at[s], wx_s.at[s], wx_r.at[s], along("x", s + 1))

    for s in range(3):
        wx_out[s] = wx[(x + s + 1) % 4].astype(BF16)
        weight_x(s).start()

    cols1(1 - high).wait_recv()
    for p in range(2):
        col2_out[p] = (terms[p, row_across] + col_in[1 - high, p].astype(F32)).astype(BF16)
    cols2.start()

    for s in range(3):
        weight_x(s).wait_recv()
    wz[...] = (
        wx[x] + wx_in[0].astype(F32) + wx_in[1].astype(F32) + wx_in[2].astype(F32)
    ).reshape(4, 16, WIDTH)

    def weight_z(s):
        return copy(wz_out.at[s], wz_in.at[s], wz_s.at[s], wz_r.at[s], along("z", s + 1))

    for s in range(3):
        wz_out[s] = wz[(z + s + 1) % 4]
        weight_z(s).start()
    cols1(high).wait_recv()
    for s in range(3):
        weight_z(s).wait_recv()
    total = wz[z] + wz_in[0] + wz_in[1] + wz_in[2]
    for s in range(4):
        wy[s] = total[:, s * TILE:(s + 1) * TILE]
    y = high * 2 + low
    yspot = (high * 2 + 1 - low, (1 - high) * 2 + low, (1 - high) * 2 + 1 - low)

    def weight_y(s):
        return copy(wy.at[yspot[s]], wy_in.at[s], wy_s.at[s], wy_r.at[s], ypeer[s])

    for s in range(3):
        weight_y(s).start()

    cols2.wait_recv()
    for p in range(2):
        value = terms[p, row] + col_in[high, p].astype(F32) + col2_in[p].astype(F32)
        kept[p, 0] = value.T
    contract = (((1,), (1,)), ((), ()))
    total = jnp.zeros((NODES, WIDTH), F32)
    for p in range(2):
        for part in split(kept[p, 0]):
            total = total + lax.dot_general(
                part, weight[:, p * HALF:(p + 1) * HALF], contract, preferred_element_type=F32
            )
    grad_features[...] = total.astype(BF16)

    for s in range(3):
        weight_y(s).wait_recv()
    ygath[y] = (wy[y] + wy_in[0] + wy_in[1] + wy_in[2]).astype(BF16)

    def gather_y(s, spot):
        return copy(ygath.at[spot], ygath.at[spot], gy_s.at[s], gy_r.at[s], ypeer[s])

    for s in range(3):
        gather_y(s, y).start()
    for s in range(3):
        gather_y(s, yspot[s]).wait_recv()
    for s in range(4):
        wfull[core, x, z, :, s * TILE:(s + 1) * TILE] = ygath[s]

    def gather_z(s, spot):
        return copy(wfull.at[core, x, spot], wfull.at[core, x, spot], gz_s.at[s], gz_r.at[s], along("z", s + 1))

    for s in range(3):
        gather_z(s, z).start()
    for s in range(3):
        gather_z(s, (z + 3 - s) % 4).wait_recv()

    def gather_x(s, spot):
        return copy(wfull.at[core, spot], wfull.at[core, spot], gx_s.at[s], gx_r.at[s], along("x", s + 1))

    for s in range(3):
        gather_x(s, x).start()
    for s in range(3):
        gather_x(s, (x + 3 - s) % 4).wait_recv()

    def gather_core(spot):
        return copy(wfull.at[spot], wfull.at[spot], gc_s, gc_r, cores)

    gather_core(core).start()
    gather_core(1 - core).wait_recv()
    grad_weight[...] = wfull[...].reshape(WIDTH, WIDTH).astype(F32)

    gather[0](row).wait_send()
    gather[1](row).wait_send()
    gather[2](row_across).wait_send()

    def sent(o):
        for p in range(2):
            for d in range(2):
                far(p, o, d).wait_send()
                for y in range(2):
                    near(p, o, d, y).wait_send()

    loop(4, sent)
    for p in range(2):
        for d in range(2):
            far2(p, d).wait_send()
            for y in range(2):
                near2(p, d, y).wait_send()
        pairs(p).wait_send()
        own_block(p, low).wait_send()
        for j in (1, 2, 3):
            for y in range(2):
                slot(p, 0, j, y).wait_send()

    def sent_grads(j):
        for p in range(2):
            for i in (1, 2, 3):
                for y in range(2):
                    slot(p, i, j, y).wait_send()

    loop(4, sent_grads)
    for h in range(2):
        cols1(h).wait_send()
    cols2.wait_send()
    weight_core.wait_send()
    for s in range(3):
        weight_x(s).wait_send()
        weight_z(s).wait_send()
        weight_y(s).wait_send()
        gather_y(s, y).wait_send()
        gather_z(s, z).wait_send()
        gather_x(s, x).wait_send()
    gather_core(core).wait_send()


def layer(features, weight, dense, output_grad):
    vmem = pl.BlockSpec(memory_space=pltpu.VMEM)
    dma = pltpu.SemaphoreType.DMA
    block = (NODES, HALF)
    bf = lambda *shape: pltpu.VMEM(shape, BF16)
    f32 = lambda *shape: pltpu.VMEM(shape, F32)
    return pl.pallas_call(
        layer_kernel,
        out_shape=(
            jax.ShapeDtypeStruct((NODES, WIDTH), BF16),
            jax.ShapeDtypeStruct((NODES, WIDTH), BF16),
            jax.ShapeDtypeStruct((WIDTH, WIDTH), F32),
        ),
        in_specs=[vmem, vmem, pl.BlockSpec(memory_space=pl.ANY), vmem],
        out_specs=(vmem, vmem, vmem),
        scratch_shapes=[
            bf(CHUNKS * NODES, COLS),
            bf(PEERS, NODES, WIDTH),
            bf(COLS, WIDTH),
            bf(2, 4, 2, *block),
            bf(2, 4, 2, 2, *block),
            bf(2, 4, 2, *block),
            bf(2, 4, 2, 2, *block),
            bf(2, 2, *block),
            bf(2, 2, 2, *block),
            bf(2, 2, *block),
            bf(2, 2, 2, *block),
            bf(2, *block),
            bf(2, *block),
            f32(2, 2, *block),
            bf(2, 4, 4, 2, HALF, NODES),
            f32(2, PEERS, HALF, NODES),
            bf(2, 2, HALF, NODES),
            bf(2, 2, HALF, NODES),
            bf(2, HALF, NODES),
            bf(2, HALF, NODES),
            bf(HALF, WIDTH),
            bf(HALF, WIDTH),
            f32(4, 64, WIDTH),
            bf(3, 64, WIDTH),
            bf(3, 64, WIDTH),
            f32(4, 16, WIDTH),
            f32(3, 16, WIDTH),
            f32(3, 16, WIDTH),
            f32(4, 16, TILE),
            f32(3, 16, TILE),
            f32(3, 16, TILE),
            bf(4, 16, TILE),
            bf(2, 4, 4, 16, WIDTH),
            dma((LOADS,)),
            dma((3,)), dma((3,)),
            dma((2, 4, 2)), dma((2, 4, 2)),
            dma((2, 4, 2, 2)), dma((2, 4, 2, 2)),
            dma((2, 2)), dma((2, 2)),
            dma((2, 2, 2)), dma((2, 2, 2)),
            dma((2,)), dma((2,)),
            dma((2, 4, 4, 2)), dma((2, 4, 4, 2)),
            dma((2,)), dma((2,)),
            dma, dma,
            dma, dma,
            dma((3,)), dma((3,)),
            dma((3,)), dma((3,)),
            dma((3,)), dma((3,)),
            dma((3,)), dma((3,)),
            dma((3,)), dma((3,)),
            dma((3,)), dma((3,)),
            dma, dma,
        ],
        compiler_params=pltpu.CompilerParams(
            collective_id=0, has_side_effects=True, vmem_limit_bytes=60 * 2**20
        ),
        name="layer",
    )(features, weight, dense, output_grad)


def per_device(features, weight, tile_values, tile_rows, tile_cols, tile_count, output_grad):
    dense = place_tiles(tile_values, tile_rows, tile_cols, tile_count)
    output, grad_features, grad_weight = layer(features, weight, dense, output_grad)
    return output, grad_features, grad_weight.T


def solution(mesh):
    spread = P(("row", "col", "rep"))
    return jax.shard_map(
        per_device,
        mesh=mesh,
        in_specs=(
            P(("row", "col", "rep"), None),
            P(),
            P(("row", "col", "rep"), None, None),
            spread,
            spread,
            spread,
            P(("row", "col", "rep"), None),
        ),
        out_specs=(P(("row", "col", "rep"), None), P(("row", "col", "rep"), None), P()),
        check_vma=False,
    )
```

```python
import math

import jax
import jax.numpy as jnp
from jax import lax
from jax.experimental import pallas as pl
from jax.experimental.pallas import tpu as pltpu
from jax.sharding import PartitionSpec as P

MESH = pl.DeviceIdType.MESH
F32, BF16 = jnp.float32, jnp.bfloat16
TILE = 128
NODES = 256
HALF = 256
WIDTH = 512
PEERS = 4
CHUNKS = 32
COLS = 1024
LOADS = 8
C0 = math.sqrt(2.0 / math.pi)


def place_kernel(rows, cols, count, values, dense, tiles, block, in_sem, out_sem):
    slots = tiles.shape[0]
    load = pltpu.make_async_copy(values, tiles, in_sem)
    load.start()

    def clear(i, carry):
        block[pl.ds(pl.multiple_of(i * 64, 64), 64), :] = jnp.zeros((64, COLS), BF16)
        return carry

    lax.fori_loop(0, block.shape[0] // 64, clear, 0)
    load.wait()

    def place(t, carry):
        row = pl.ds(pl.multiple_of(rows[t] * TILE, TILE), TILE)
        col = pl.ds(pl.multiple_of(cols[t] * TILE, TILE), TILE)
        block[row, col] = block[row, col] + tiles[t]
        return carry

    lax.fori_loop(0, jnp.minimum(count[0], slots), place, 0)
    store = pltpu.make_async_copy(block, dense, out_sem)
    store.start()
    store.wait()


def place_tiles(values, rows, cols, count):
    slots = values.shape[0]
    smem = pl.BlockSpec(memory_space=pltpu.SMEM)
    return pl.pallas_call(
        place_kernel,
        out_shape=jax.ShapeDtypeStruct((CHUNKS * NODES, COLS), BF16),
        in_specs=[smem, smem, smem, pl.BlockSpec(memory_space=pl.ANY)],
        out_specs=pl.BlockSpec(memory_space=pl.ANY),
        scratch_shapes=[
            pltpu.VMEM((slots, TILE, TILE), BF16),
            pltpu.VMEM((CHUNKS * NODES, COLS), BF16),
            pltpu.SemaphoreType.DMA,
            pltpu.SemaphoreType.DMA,
        ],
        cost_estimate=pl.CostEstimate(flops=0, bytes_accessed=30 * 2**20, transcendentals=0),
        compiler_params=pltpu.CompilerParams(vmem_limit_bytes=63 * 2**20),
        name="place_tiles",
    )(rows, cols, count, values)


def dot(a, b):
    return jnp.dot(a, b, preferred_element_type=F32)


def split(v):
    high = v.astype(BF16)
    return high, (v - high.astype(F32)).astype(BF16)


def layer_kernel(
    features, features_across, weight_hbm, dense_hbm, output_grad_hbm, output_hbm, grad_features_hbm, grad_weight_hbm,
    dense, feats, weight, output_grad, output, grad_features, lifted,
    pairs_out, pairs_in, far_out, far_in, near_out, near_in, far2_out, far2_in, near2_out, near2_in, pair_out, pair_in,
    kept, grads, terms, col_out, col_in, col2_out, col2_in,
    wcore_out, wcore_in, wsum, wy_out, wy_in, wgrid, wgrid_in, ggrid, wfull,
    load_sem, in_sem, out_sem, a_s, a_r, pairs_s, pairs_r, far_s, far_r, near_s, near_r, far2_s, far2_r, near2_s, near2_r,
    pair_s, pair_r, g_s, own_r, second_r, first_r, gfar_r, gpair_r, c_s, c_r, c2_s, c2_r, w_s, w_r,
):
    row, z, rep = lax.axis_index("row"), lax.axis_index("col"), lax.axis_index("rep")
    high, core = row // 2, row % 2
    x, low = rep // 2, rep % 2

    def at(high_=None, core_=None, z_=None, x_=None, low_=None):
        pick = lambda v, own: own if v is None else v
        return {
            "row": pick(high_, high) * 2 + pick(core_, core),
            "col": pick(z_, z),
            "rep": pick(x_, x) * 2 + pick(low_, low),
        }

    def along(axis, step):
        return at(x_=(x + step) % 4) if axis == "x" else at(z_=(z + step) % 4)

    def on_grid(s):
        return at(x_=(x + s // 4) % 4, z_=(z + s % 4) % 4)

    axes = (("x", "z"), ("z", "x"))
    spots = ((x, z), (z, x))
    steps = (3, 1)
    mine, other = low, 1 - low

    def chunk(p, first, second, pair_):
        if p == 0:
            return second * 8 + first * 2 + pair_
        return first * 8 + second * 2 + pair_

    def copy(src, dst, s, r, device):
        return pltpu.make_async_remote_copy(
            src_ref=src, dst_ref=dst, send_sem=s, recv_sem=r, device_id=device, device_id_type=MESH
        )

    cores, pair, across = at(core_=1 - core), at(low_=1 - low), at(high_=1 - high)
    ypeer = (pair, across, at(high_=1 - high, low_=1 - low))

    def loop(n, body):
        def step(i, carry):
            body(i)
            return carry

        lax.fori_loop(0, n, step, 0)

    def rows_of(r):
        return pl.ds(pl.multiple_of(r * NODES, NODES), NODES)

    per_load = CHUNKS * NODES // LOADS

    def load(i):
        span = pl.ds(pl.multiple_of(i * per_load, per_load), per_load)
        return pltpu.make_async_copy(dense_hbm.at[span], dense.at[span], load_sem.at[i])

    row_across, row_core, row_last = (1 - high) * 2 + core, high * 2 + 1 - core, (1 - high) * 2 + 1 - core
    takes = (
        pltpu.make_async_copy(features, feats.at[rows_of(row)], in_sem.at[0]),
        pltpu.make_async_copy(features_across, feats.at[rows_of(row_across)], in_sem.at[1]),
        pltpu.make_async_copy(weight_hbm, weight, in_sem.at[2]),
        pltpu.make_async_copy(output_grad_hbm, output_grad, in_sem.at[3]),
    )
    takes[0].start()
    takes[1].start()
    loop(LOADS, lambda i: load(i).start())
    takes[2].start()
    takes[3].start()

    barrier = pltpu.get_barrier_semaphore()

    def greet(s):
        pl.semaphore_signal(barrier, inc=1, device_id=on_grid(s + 1), device_id_type=MESH)

    loop(15, greet)
    for device in (*ypeer, cores):
        pl.semaphore_signal(barrier, inc=1, device_id=device, device_id_type=MESH)
    pl.semaphore_wait(barrier, 19)

    def gather(i, r):
        return copy((features, features_across)[i], feats.at[rows_of(r)], a_s.at[i], a_r.at[i], cores)

    gather(0, row).start()
    gather(1, row_across).start()
    takes[0].wait()
    takes[1].wait()
    gather(0, row_core).wait_recv()
    gather(1, row_last).wait_recv()
    loop(LOADS, lambda i: load(i).wait())

    def partial(p, first, second, pair_):
        start = pl.multiple_of(chunk(p, first, second, pair_) * NODES, NODES)
        return dot(dense[pl.ds(start, NODES), :], feats[:, p * HALF:(p + 1) * HALF])

    def pairs(p, o):
        return copy(pairs_out.at[p, o], pairs_in.at[p, o], pairs_s, pairs_r.at[p, o], pair)

    def far(p, o, d):
        half = pl.ds(d * TILE, TILE)
        return copy(far_out.at[p, o, half], far_in.at[p, o, d], far_s, far_r.at[p, o, d], along(axes[p][0], steps[d]))

    def near(p, o, r, d):
        return copy(near_out.at[p, o, r, d], near_in.at[p, o, r, d], near_s, near_r.at[p, o, r], along(axes[p][0], steps[d]))

    def near_both(p, o, r):
        return copy(near_out.at[p, o, r], near_in.at[p, o, r], near_s, near_r.at[p, o, r], pair)

    def send_other(o):
        for p in range(2):
            first, second = spots[p]
            for d in range(2):
                near_out[p, o, 1, d] = partial(p, (first + steps[d]) % 4, (second + o) % 4, other).astype(BF16)
                near(p, o, 1, d).start()

    def send_pair(o):
        for p in range(2):
            first, second = spots[p]
            pairs_out[p, o] = partial(p, (first + 2) % 4, (second + o) % 4, other).astype(BF16)
            pairs(p, o).start()

    def send_far(o):
        for p in range(2):
            first, second = spots[p]
            value = partial(p, (first + 2) % 4, (second + o) % 4, mine)
            pairs(p, o).wait_recv()
            far_out[p, o] = (value + pairs_in[p, o].astype(F32)).astype(BF16)
            for d in range(2):
                far(p, o, d).start()

    def send_mine(o):
        for p in range(2):
            first, second = spots[p]
            for d in range(2):
                value = partial(p, (first + steps[d]) % 4, (second + o) % 4, mine)
                far(p, o, d).wait_recv()
                half, rest = (slice(0, TILE), slice(TILE, NODES))[::1 - 2 * d]
                near_out[p, o, 0, d, half] = (value[half] + far_in[p, o, d].astype(F32)).astype(BF16)
                near_out[p, o, 0, d, rest] = value[rest].astype(BF16)
                near(p, o, 0, d).start()

    def far2(p, d):
        return copy(far2_out.at[p, d], far2_in.at[p, d], far2_s, far2_r.at[p, d], along(axes[p][1], 3 - 2 * d))

    def near2(p, d, y):
        return copy(near2_out.at[p, y, d], near2_in.at[p, y, d], near2_s, near2_r.at[p, y], along(axes[p][1], 3 - 2 * d))

    def near2_both(p, y):
        return copy(near2_out.at[p, y], near2_in.at[p, y], near2_s, near2_r.at[p, y], pair)

    def first_sum(p, o, y):
        value = partial(p, spots[p][0], (spots[p][1] + o) % 4, y)
        r = (y + low) % 2
        near_both(p, o, r).wait_recv()
        return value + near_in[p, o, r, 0].astype(F32) + near_in[p, o, r, 1].astype(F32)

    def send_far2(d):
        for p in range(2):
            far2_out[p, d] = first_sum(p, 2, d).astype(BF16)
            far2(p, d).start()

    def send_other2(d):
        for p in range(2):
            near2_out[p, 1 - d, d] = first_sum(p, 3 - 2 * d, 1 - d).astype(BF16)
            near2(p, d, 1 - d).start()

    def send_mine2(d):
        for p in range(2):
            value = first_sum(p, 3 - 2 * d, d)
            far2(p, d).wait_recv()
            near2_out[p, d, d] = (value + far2_in[p, d].astype(F32)).astype(BF16)
            near2(p, d, d).start()

    def keep(y):
        for p in range(2):
            kept[p, y] = first_sum(p, 0, y)

    def last_pair(p):
        return copy(pair_out.at[p], pair_in.at[p], pair_s, pair_r.at[p], pair)

    def second_sum(p, y):
        near2_both(p, y).wait_recv()
        return kept[p, y] + near2_in[p, y, 0].astype(F32) + near2_in[p, y, 1].astype(F32)

    def send_last():
        for p in range(2):
            pair_out[p] = second_sum(p, other).astype(BF16)
            last_pair(p).start()

    def keep_last():
        for p in range(2):
            kept[p, mine] = second_sum(p, mine)

    for step in (
        (send_other, 0), (send_pair, 2), (send_other, 2), (send_other, 1), (send_pair, 1), (send_far, 2),
        (send_other, 3), (send_pair, 3), (send_mine, 2), (keep, other), (send_far2, other), (send_pair, 0),
        (send_far, 1), (send_other2, mine), (send_far, 3), (send_far2, mine), (send_mine2, other), (send_mine, 1),
        (send_far, 0), (send_mine, 3), (send_mine, 0), (send_last,), (send_other2, other), (send_mine2, mine),
        (keep, mine), (keep_last,),
    ):
        step[0](*step[1:])

    takes[2].wait()
    takes[3].wait()
    v = jnp.zeros((NODES, WIDTH), F32)
    for p in range(2):
        last_pair(p).wait_recv()
        span = slice(p * HALF, (p + 1) * HALF)
        for i, part in enumerate(split(kept[p, mine] + pair_in[p].astype(F32))):
            lifted[i, :, span] = part
            v = v + dot(part, weight[span, :])
    t = jnp.tanh(C0 * (v + 0.044715 * (v * v * v)))
    slope = 0.5 * (1.0 + t) + 0.5 * v * (1.0 - t * t) * (C0 * (1.0 + 3.0 * 0.044715 * (v * v)))
    grad = (output_grad[...].astype(F32) * slope).astype(BF16).astype(F32)

    def own(p, y):
        return copy(grads.at[p, 0, 0, y], grads.at[p, 0, 0, y], g_s.at[0], own_r.at[p], pair)

    def second(p, j, y):
        step, src = {1: (3, 0), 2: (3 - 2 * y, 1 + 2 * y), 3: (1, 0)}[j]
        return copy(
            grads.at[p, 0, src, y], grads.at[p, 0, j, y], g_s.at[2 if j == 2 else 1], second_r.at[p, j - 1, y],
            along(axes[p][1], step),
        )

    def first(p, i, j, y):
        return copy(
            grads.at[p, 0, j, y], grads.at[p, i, j, y], g_s.at[3], first_r.at[p, i // 2, j, y],
            along(axes[p][0], 3 if i == 1 else 1),
        )

    def onward(p, j, d):
        half = pl.ds(d * TILE, TILE)
        return copy(
            grads.at[p, 1 + 2 * d, j, mine, half], grads.at[p, 2, j, mine, half], g_s.at[4], gfar_r.at[p, j],
            along(axes[p][0], steps[d]),
        )

    def onward_both(p, j):
        return copy(grads.at[p, 2, j, mine], grads.at[p, 2, j, mine], g_s.at[4], gfar_r.at[p, j], pair)

    def far_pair(p, j, y):
        return copy(grads.at[p, 2, j, y], grads.at[p, 2, j, y], g_s.at[5], gpair_r.at[p, j], pair)

    def give_first(p, j, y):
        first(p, 1, j, y).start()
        first(p, 3, j, y).start()

    def give_second(p, y):
        second(p, 1, y).start()
        second(p, 3, y).start()

    for p in range(2):
        grads[p, 0, 0, mine] = grad[:, p * HALF:(p + 1) * HALF].T.astype(BF16)
        give_second(p, mine)
    output[...] = (0.5 * v * (1.0 + t)).astype(BF16)
    gives = (
        pltpu.make_async_copy(output, output_hbm, out_sem.at[0]),
        pltpu.make_async_copy(wfull, grad_weight_hbm, out_sem.at[1]),
        pltpu.make_async_copy(grad_features, grad_features_hbm, out_sem.at[2]),
    )
    gives[0].start()

    def weight_half(p):
        block = grads[p, 0, 0, mine]
        return dot(block, lifted[0]) + dot(block, lifted[1])

    spot = x * 4 + z
    y = high * 2 + low
    yspot = (high * 2 + other, (1 - high) * 2 + low, (1 - high) * 2 + other)
    weight_core = copy(wcore_out, wcore_in, w_s.at[0], w_r.at[0], cores)

    def weight_y(s):
        return copy(wy_out.at[s], wy_in.at[s], w_s.at[1], w_r.at[1], ypeer[s])

    def weight_grid(s):
        part = ((x + s // 4) % 4) * 4 + (z + s % 4) % 4
        return copy(wgrid.at[part], wgrid_in.at[s], w_s.at[2], w_r.at[2], on_grid(s))

    def gather_grid(s):
        return copy(ggrid.at[spot], ggrid.at[spot], w_s.at[3], w_r.at[3], on_grid(s))

    def gather_y(s):
        return copy(wfull.at[core, y], wfull.at[core, y], w_s.at[4], w_r.at[4], ypeer[s])

    def gather_core(half):
        return copy(wfull.at[half], wfull.at[half], w_s.at[5], w_r.at[5], cores)

    weight_all = (
        weight_core,
        copy(wy_out, wy_in, w_s.at[1], w_r.at[1], cores),
        copy(wgrid.at[pl.ds(1, 15)], wgrid_in.at[pl.ds(1, 15)], w_s.at[2], w_r.at[2], cores),
        copy(ggrid.at[pl.ds(1, 15)], ggrid.at[pl.ds(1, 15)], w_s.at[3], w_r.at[3], cores),
        copy(wfull.at[0, pl.ds(0, 3)], wfull.at[0, pl.ds(0, 3)], w_s.at[4], w_r.at[4], cores),
        gather_core(1 - core),
    )

    def weight_step(k):
        if k > 0:
            weight_all[k - 1].wait_recv()
        if k == 0:
            wcore_out[...] = weight_half(1 - core).astype(BF16)
            weight_core.start()
            wsum[...] = weight_half(core).reshape(4, 64, WIDTH)
        elif k == 1:
            wsum[...] = wsum[...] + wcore_in[...].astype(F32).reshape(4, 64, WIDTH)
            for s in range(3):
                wy_out[s] = wsum[yspot[s]].astype(BF16)
                weight_y(s).start()
        elif k == 2:
            total = wsum[y]
            for s in range(3):
                total = total + wy_in[s].astype(F32)
            for s in range(16):
                i, j = s // 4, s % 4
                wgrid[s] = total[i * 16:(i + 1) * 16, j * TILE:(j + 1) * TILE]
            loop(15, lambda s: weight_grid(s + 1).start())
        elif k == 3:
            total = wgrid[spot]
            for s in range(1, 16):
                total = total + wgrid_in[s]
            ggrid[spot] = total.astype(BF16)
            loop(15, lambda s: gather_grid(s + 1).start())
        elif k == 4:
            for s in range(16):
                i, j = s // 4, s % 4
                wfull[core, y, i * 16:(i + 1) * 16, j * TILE:(j + 1) * TILE] = ggrid[s]
            for s in range(3):
                gather_y(s).start()
        elif k == 5:
            gather_core(core).start()
        else:
            gives[1].start()

    def product(p, i, j):
        total = None
        for y_ in range(2):
            start = chunk(p, (spots[p][0] + i) % 4, (spots[p][1] + j) % 4, y_) * NODES
            term = dot(grads[p, i, j, y_], dense[pl.ds(pl.multiple_of(start, NODES), NODES), :])
            total = term if total is None else total + term
        return total

    begun = set()

    def add(p, i, j):
        total, fresh = product(p, i, j), p not in begun
        begun.add(p)
        for r in range(PEERS):
            part = total[:, r * NODES:(r + 1) * NODES]
            terms[p, r] = part if fresh else terms[p, r] + part

    def pass_on(j):
        for p in range(2):
            for d in range(2):
                first(p, 1 + 2 * d, j, mine).wait_recv()
                onward(p, j, d).start()

    def pass_pair(j):
        for p in range(2):
            onward_both(p, j).wait_recv()
            far_pair(p, j, mine).start()

    def use_first(j):
        for p in range(2):
            for i in (1, 3):
                first(p, i, j, other).wait_recv()
                add(p, i, j)

    def use_far(j):
        for p in range(2):
            far_pair(p, j, other).wait_recv()
            add(p, 2, j)

    def give_own():
        for p in range(2):
            own(p, mine).start()

    def take_own():
        for p in range(2):
            own(p, other).wait_recv()
            give_second(p, other)

    def give_firsts(j, y_):
        for p in range(2):
            give_first(p, j, y_)

    def take_second(y_):
        for p in range(2):
            second(p, 1, y_).wait_recv()
            second(p, 3, y_).wait_recv()
            second(p, 2, y_).start()

    def take_second2(y_):
        for p in range(2):
            second(p, 2, y_).wait_recv()

    def use_own(j):
        for p in range(2):
            add(p, 0, j)

    for step in (
        (weight_step, 0), (give_firsts, 0, mine), (give_own,), (take_second, mine), (give_firsts, 3, mine), (pass_on, 0),
        (take_own,), (weight_step, 1), (take_second2, mine), (give_firsts, 2, mine), (pass_on, 3), (weight_step, 2),
        (pass_pair, 0), (give_firsts, 1, mine), (take_second, other), (pass_on, 2), (use_own, 3), (pass_pair, 3),
        (give_firsts, 0, other), (use_own, 1), (weight_step, 3), (pass_on, 1), (pass_pair, 2), (take_second2, other),
        (use_own, 0), (give_firsts, 1, other), (give_firsts, 3, other), (pass_pair, 1), (give_firsts, 2, other),
        (use_first, 0), (use_far, 2), (use_first, 1), (weight_step, 4), (use_far, 3), (use_far, 0), (use_own, 2),
        (use_first, 3), (use_far, 1), (use_first, 2),
    ):
        step[0](*step[1:])

    def cols1(h):
        return copy(col_out.at[h], col_in.at[h], c_s, c_r.at[h], cores)

    cols2 = copy(col2_out, col2_in, c2_s, c2_r, across)

    def give_cols(h):
        for p in range(2):
            col_out[h, p] = terms[p, 2 * h + 1 - core].astype(BF16)
        cols1(h).start()

    give_cols(1 - high)
    give_cols(high)
    cols1(1 - high).wait_recv()
    for p in range(2):
        col2_out[p] = (terms[p, row_across] + col_in[1 - high, p].astype(F32)).astype(BF16)
    cols2.start()
    weight_step(5)
    weight_step(6)

    def sent(ref, sem):
        copy(ref, ref, sem, sem, pair).wait_send()

    for i, r in ((0, row), (1, row_across)):
        gather(i, r).wait_send()
    sent(pairs_out, pairs_s)
    sent(far_out, far_s)
    sent(near_out, near_s)
    sent(far2_out, far2_s)
    sent(near2_out, near2_s)
    sent(pair_out, pair_s)
    sent(grads.at[0, 0, 0], g_s.at[0])
    sent(grads.at[0, 0], g_s.at[1])
    sent(grads.at[0, 0, pl.ds(0, 2)], g_s.at[2])
    sent(grads.at[0], g_s.at[3])
    sent(grads.at[0, 0], g_s.at[4])
    sent(grads.at[0, 0], g_s.at[5])
    for step in weight_all:
        step.wait_send()
    gives[0].wait()
    gives[1].wait()

    cols1(high).wait_recv()
    cols2.wait_recv()
    contract = (((1,), (1,)), ((), ()))
    total = jnp.zeros((NODES, WIDTH), F32)
    for p in range(2):
        value = (terms[p, row] + col_in[high, p].astype(F32) + col2_in[p].astype(F32)).T
        for part in split(value):
            total = total + lax.dot_general(
                part, weight[:, p * HALF:(p + 1) * HALF], contract, preferred_element_type=F32
            )
    grad_features[...] = total.astype(BF16)
    gives[2].start()
    sent(col_out, c_s)
    cols2.wait_send()
    gives[2].wait()


def layer(features, features_across, weight, dense, output_grad):
    anywhere = pl.BlockSpec(memory_space=pl.ANY)
    dma = pltpu.SemaphoreType.DMA
    block = (NODES, HALF)
    bf = lambda *shape: pltpu.VMEM(shape, BF16)
    f32 = lambda *shape: pltpu.VMEM(shape, F32)
    return pl.pallas_call(
        layer_kernel,
        out_shape=(
            jax.ShapeDtypeStruct((NODES, WIDTH), BF16),
            jax.ShapeDtypeStruct((NODES, WIDTH), BF16),
            jax.ShapeDtypeStruct((2, 4, 64, WIDTH), BF16),
        ),
        in_specs=[anywhere] * 5,
        out_specs=(anywhere,) * 3,
        scratch_shapes=[
            bf(CHUNKS * NODES, COLS),
            bf(COLS, WIDTH),
            bf(WIDTH, WIDTH),
            bf(NODES, WIDTH),
            bf(NODES, WIDTH),
            bf(NODES, WIDTH),
            bf(2, NODES, WIDTH),
            bf(2, 4, *block), bf(2, 4, *block),
            bf(2, 4, *block), bf(2, 4, 2, TILE, HALF),
            bf(2, 4, 2, 2, *block), bf(2, 4, 2, 2, *block),
            bf(2, 2, *block), bf(2, 2, *block),
            bf(2, 2, 2, *block), bf(2, 2, 2, *block),
            bf(2, *block), bf(2, *block),
            f32(2, 2, *block),
            bf(2, 4, 4, 2, HALF, NODES),
            f32(2, PEERS, HALF, NODES),
            bf(2, 2, HALF, NODES), bf(2, 2, HALF, NODES),
            bf(2, HALF, NODES), bf(2, HALF, NODES),
            bf(HALF, WIDTH), bf(HALF, WIDTH),
            f32(4, 64, WIDTH),
            bf(3, 64, WIDTH), bf(3, 64, WIDTH),
            f32(16, 16, TILE), f32(16, 16, TILE),
            bf(16, 16, TILE),
            bf(2, 4, 64, WIDTH),
            dma((LOADS,)), dma((4,)), dma((3,)),
            dma((2,)), dma((2,)),
            dma, dma((2, 4)),
            dma, dma((2, 4, 2)),
            dma, dma((2, 4, 2)),
            dma, dma((2, 2)),
            dma, dma((2, 2)),
            dma, dma((2,)),
            dma((6,)), dma((2,)), dma((2, 3, 2)), dma((2, 2, 4, 2)), dma((2, 4)), dma((2, 4)),
            dma, dma((2,)),
            dma, dma,
            dma((6,)), dma((6,)),
        ],
        compiler_params=pltpu.CompilerParams(
            collective_id=0, has_side_effects=True, vmem_limit_bytes=62 * 2**20
        ),
        name="layer",
    )(features, features_across, weight, dense, output_grad)


def finish_kernel(first_in, second_in, weight_in, first, second, weight):
    first[...] = first_in[...]
    second[...] = second_in[...]
    weight[...] = weight_in[...].astype(F32).T


def finish(output, grad_features, grad_weight):
    vmem = pl.BlockSpec(memory_space=pltpu.VMEM)
    return pl.pallas_call(
        finish_kernel,
        out_shape=(
            jax.ShapeDtypeStruct(output.shape, BF16),
            jax.ShapeDtypeStruct(grad_features.shape, BF16),
            jax.ShapeDtypeStruct(grad_weight.shape, F32),
        ),
        in_specs=[vmem] * 3,
        out_specs=(vmem,) * 3,
        compiler_params=pltpu.CompilerParams(vmem_limit_bytes=63 * 2**20),
        name="finish",
    )(output, grad_features, grad_weight)


def per_device(features, weight, tile_values, tile_rows, tile_cols, tile_count, output_grad):
    features_across = lax.ppermute(features, "row", [(r, (r + 2) % PEERS) for r in range(PEERS)])
    dense = place_tiles(tile_values, tile_rows, tile_cols, tile_count)
    output, grad_features, grad_weight = layer(features, features_across, weight, dense, output_grad)
    return finish(output, grad_features, grad_weight.reshape(WIDTH, WIDTH))


def solution(mesh):
    spread = P(("row", "col", "rep"))
    return jax.shard_map(
        per_device,
        mesh=mesh,
        in_specs=(
            P(("row", "col", "rep"), None),
            P(),
            P(("row", "col", "rep"), None, None),
            spread,
            spread,
            spread,
            P(("row", "col", "rep"), None),
        ),
        out_specs=(P(("row", "col", "rep"), None), P(("row", "col", "rep"), None), P()),
        check_vma=False,
    )
```

```python
import math

import jax
import jax.numpy as jnp
from jax import lax
from jax.experimental import pallas as pl
from jax.experimental.pallas import tpu as pltpu
from jax.sharding import PartitionSpec as P

MESH = pl.DeviceIdType.MESH
F32, BF16 = jnp.float32, jnp.bfloat16
TILE = 128
NODES = 256
HALF = 256
WIDTH = 512
PEERS = 4
CHUNKS = 32
COLS = 1024
BANDS = 8
BAND_TILES = 8
PLACE_VMEM, LAYER_VMEM, FINISH_VMEM = 63 * 2**20, 62 * 2**20, 63 * 2**20
C0 = math.sqrt(2.0 / math.pi)


def place_kernel(rows, cols, count, values, dense, tiles, block, listed, filled, in_sem, out_sem):
    slots = tiles.shape[0]
    load = pltpu.make_async_copy(values, tiles, in_sem)
    load.start()

    for g in range(BANDS):
        filled[g] = 0

    def enlist(t, carry):
        g = rows[t] // BAND_TILES
        at = filled[g]
        listed[g, at] = t
        filled[g] = at + 1
        return carry

    lax.fori_loop(0, jnp.minimum(count[0], slots), enlist, 0)

    def clear(i, carry):
        block[pl.ds(pl.multiple_of(i * 64, 64), 64), :] = jnp.zeros((64, COLS), BF16)
        return carry

    lax.fori_loop(0, block.shape[0] // 64, clear, 0)
    load.wait()

    def store(g):
        band = pl.ds(pl.multiple_of(g * BAND_TILES * TILE, BAND_TILES * TILE), BAND_TILES * TILE)
        return pltpu.make_async_copy(block.at[band], dense.at[band], out_sem.at[g])

    for g in range(BANDS):
        def place(i, carry):
            t = listed[g, i]
            row = pl.ds(pl.multiple_of(rows[t] * TILE, TILE), TILE)
            col = pl.ds(pl.multiple_of(cols[t] * TILE, TILE), TILE)
            block[row, col] = block[row, col] + tiles[t]
            return carry

        lax.fori_loop(0, filled[g], place, 0)
        store(g).start()
    for g in range(BANDS):
        store(g).wait()


def place_tiles(values, rows, cols, count):
    slots = values.shape[0]
    smem = pl.BlockSpec(memory_space=pltpu.SMEM)
    return pl.pallas_call(
        place_kernel,
        out_shape=jax.ShapeDtypeStruct((CHUNKS * NODES, COLS), BF16),
        in_specs=[smem, smem, smem, pl.BlockSpec(memory_space=pl.ANY)],
        out_specs=pl.BlockSpec(memory_space=pl.ANY),
        scratch_shapes=[
            pltpu.VMEM((slots, TILE, TILE), BF16),
            pltpu.VMEM((CHUNKS * NODES, COLS), BF16),
            pltpu.SMEM((BANDS, slots), jnp.int32),
            pltpu.SMEM((BANDS,), jnp.int32),
            pltpu.SemaphoreType.DMA,
            pltpu.SemaphoreType.DMA((BANDS,)),
        ],
        cost_estimate=pl.CostEstimate(flops=0, bytes_accessed=30 * 2**20, transcendentals=0),
        compiler_params=pltpu.CompilerParams(vmem_limit_bytes=PLACE_VMEM),
        name="place_tiles",
    )(rows, cols, count, values)


def dot(a, b):
    return jnp.dot(a, b, preferred_element_type=F32)


def split(v):
    high = v.astype(BF16)
    return high, (v - high.astype(F32)).astype(BF16)


def layer_kernel(
    features, features_across, weight_hbm, dense_hbm, output_grad_hbm, output_hbm, grad_features_hbm, grad_weight_hbm,
    dense, feats, weight, output_grad, output, grad_features, lifted,
    pairs_out, pairs_in, far_out, far_in, near_out, near_in, far2_out, far2_in, near2_out, near2_in, pair_out, pair_in,
    kept, grads, terms, col_out, col_in, col2_out, col2_in,
    wcore_out, wcore_in, wsum, wy_in, wgrid, wgrid_in, ggrid, wfull,
    load_sem, in_sem, out_sem, a_s, a_r, pairs_s, pairs_r, far_s, far_r, near_s, near_r, far2_s, far2_r, near2_s, near2_r,
    pair_s, pair_r, g_s, own_r, second_r, first_r, gfar_r, gpair_r, c_s, c_r, c2_s, c2_r, w_s, w_r,
):
    row, z, rep = lax.axis_index("row"), lax.axis_index("col"), lax.axis_index("rep")
    high, core = row // 2, row % 2
    x, low = rep // 2, rep % 2

    def at(high_=None, core_=None, z_=None, x_=None, low_=None):
        pick = lambda v, own: own if v is None else v
        return {
            "row": pick(high_, high) * 2 + pick(core_, core),
            "col": pick(z_, z),
            "rep": pick(x_, x) * 2 + pick(low_, low),
        }

    def along(axis, step):
        return at(x_=(x + step) % 4) if axis == "x" else at(z_=(z + step) % 4)

    def on_grid(s):
        return at(x_=(x + s // 4) % 4, z_=(z + s % 4) % 4)

    axes = (("x", "z"), ("z", "x"))
    spots = ((x, z), (z, x))
    steps = (3, 1)
    mine, other = low, 1 - low

    def chunk(p, first, second, pair_):
        if p == 0:
            return second * 8 + first * 2 + pair_
        return first * 8 + second * 2 + pair_

    def copy(src, dst, s, r, device):
        return pltpu.make_async_remote_copy(
            src_ref=src, dst_ref=dst, send_sem=s, recv_sem=r, device_id=device, device_id_type=MESH
        )

    cores, pair, across = at(core_=1 - core), at(low_=1 - low), at(high_=1 - high)
    ypeer = (pair, across, at(high_=1 - high, low_=1 - low))

    def loop(n, body):
        def step(i, carry):
            body(i)
            return carry

        lax.fori_loop(0, n, step, 0)

    def rows_of(r):
        return pl.ds(pl.multiple_of(r * NODES, NODES), NODES)

    def load(i, j, pair_):
        span = rows_of(chunk(0, (x + i) % 4, (z + j) % 4, pair_))
        sem = load_sem.at[i, j, 0 if pair_ is mine else 1]
        return pltpu.make_async_copy(dense_hbm.at[span], dense.at[span], sem)

    uses = [(steps[d], o, other) for o in (0,) for d in range(2)]
    uses += [(2, 2, other)] + [(steps[d], 2, other) for d in range(2)] + [(steps[d], 1, other) for d in range(2)]
    uses += [(2, 1, other), (2, 2, mine)] + [(steps[d], 3, other) for d in range(2)] + [(2, 3, other)]
    uses += [(steps[d], 2, mine) for d in range(2)]
    waiting = []
    for i, j, pair_ in uses + [(i, j, pair_) for pair_ in (other, mine) for i in range(4) for j in range(4)]:
        for key in ((i, j, pair_), (j, i, pair_)):
            if not any(key[:2] == k[:2] and key[2] is k[2] for k in waiting):
                waiting.append(key)
    loads = list(waiting)

    def need(p, i, j, pair_):
        for key in waiting:
            if key[:2] == ((i, j), (j, i))[p] and key[2] is pair_:
                load(*key).wait()
                waiting.remove(key)
                break

    def need_all():
        while waiting:
            load(*waiting.pop(0)).wait()

    row_across, row_core, row_last = (1 - high) * 2 + core, high * 2 + 1 - core, (1 - high) * 2 + 1 - core
    takes = (
        pltpu.make_async_copy(features, feats.at[rows_of(row)], in_sem.at[0]),
        pltpu.make_async_copy(features_across, feats.at[rows_of(row_across)], in_sem.at[1]),
        pltpu.make_async_copy(weight_hbm, weight, in_sem.at[2]),
        pltpu.make_async_copy(output_grad_hbm, output_grad, in_sem.at[3]),
    )
    takes[0].start()
    takes[1].start()
    for key in loads[:2]:
        load(*key).start()

    barrier = pltpu.get_barrier_semaphore()

    def greet(s):
        pl.semaphore_signal(barrier, inc=1, device_id=on_grid(s + 1), device_id_type=MESH)

    loop(15, greet)
    for device in (*ypeer, cores):
        pl.semaphore_signal(barrier, inc=1, device_id=device, device_id_type=MESH)
    pl.semaphore_wait(barrier, 19)

    def gather(i, r):
        return copy((features, features_across)[i], feats.at[rows_of(r)], a_s.at[i], a_r.at[i], cores)

    gather(0, row).start()
    gather(1, row_across).start()
    takes[0].wait()
    takes[1].wait()
    for key in loads[2:6]:
        load(*key).start()
    gather(0, row_core).wait_recv()
    gather(1, row_last).wait_recv()
    for key in loads[6:]:
        load(*key).start()
    takes[2].start()
    takes[3].start()

    def partial_at(p, i, j, pair_):
        need(p, i, j, pair_)
        return partial(p, (spots[p][0] + i) % 4, (spots[p][1] + j) % 4, pair_)

    def partial(p, first, second, pair_):
        start = pl.multiple_of(chunk(p, first, second, pair_) * NODES, NODES)
        return dot(dense[pl.ds(start, NODES), :], feats[:, p * HALF:(p + 1) * HALF])

    def pairs(p, o):
        return copy(pairs_out.at[p, o], pairs_in.at[p, o], pairs_s, pairs_r.at[p, o], pair)

    def far(p, o, d):
        half = pl.ds(d * TILE, TILE)
        return copy(far_out.at[p, o, half], far_in.at[p, o, d], far_s, far_r.at[p, o, d], along(axes[p][0], steps[d]))

    def near(p, o, r, d):
        return copy(near_out.at[p, o, r, d], near_in.at[p, o, r, d], near_s, near_r.at[p, o, r], along(axes[p][0], steps[d]))

    def near_both(p, o, r):
        return copy(near_out.at[p, o, r], near_in.at[p, o, r], near_s, near_r.at[p, o, r], pair)

    def send_other(p, o):
        for d in range(2):
            near_out[p, o, 1, d] = partial_at(p, steps[d], o, other).astype(BF16)
            near(p, o, 1, d).start()

    def send_pair(p, o):
        pairs_out[p, o] = partial_at(p, 2, o, other).astype(BF16)
        pairs(p, o).start()

    def send_far(p, o):
        value = partial_at(p, 2, o, mine)
        pairs(p, o).wait_recv()
        far_out[p, o] = (value + pairs_in[p, o].astype(F32)).astype(BF16)
        for d in range(2):
            far(p, o, d).start()

    def send_mine(p, o):
        for d in range(2):
            value = partial_at(p, steps[d], o, mine)
            far(p, o, d).wait_recv()
            half, rest = (slice(0, TILE), slice(TILE, NODES))[::1 - 2 * d]
            near_out[p, o, 0, d, half] = (value[half] + far_in[p, o, d].astype(F32)).astype(BF16)
            near_out[p, o, 0, d, rest] = value[rest].astype(BF16)
            near(p, o, 0, d).start()

    def far2(p, d):
        return copy(far2_out.at[p, d], far2_in.at[p, d], far2_s, far2_r.at[p, d], along(axes[p][1], 3 - 2 * d))

    def near2(p, d, y):
        return copy(near2_out.at[p, y, d], near2_in.at[p, y, d], near2_s, near2_r.at[p, y], along(axes[p][1], 3 - 2 * d))

    def near2_both(p, y):
        return copy(near2_out.at[p, y], near2_in.at[p, y], near2_s, near2_r.at[p, y], pair)

    def first_sum(p, o, y):
        need_all()
        value = partial(p, spots[p][0], (spots[p][1] + o) % 4, y)
        r = (y + low) % 2
        near_both(p, o, r).wait_recv()
        return value + near_in[p, o, r, 0].astype(F32) + near_in[p, o, r, 1].astype(F32)

    def send_far2(p, d):
        far2_out[p, d] = first_sum(p, 2, d).astype(BF16)
        far2(p, d).start()

    def send_other2(p, d):
        near2_out[p, 1 - d, d] = first_sum(p, 3 - 2 * d, 1 - d).astype(BF16)
        near2(p, d, 1 - d).start()

    def send_mine2(p, d):
        value = first_sum(p, 3 - 2 * d, d)
        far2(p, d).wait_recv()
        near2_out[p, d, d] = (value + far2_in[p, d].astype(F32)).astype(BF16)
        near2(p, d, d).start()

    def keep(p, y):
        kept[p, y] = first_sum(p, 0, y)

    def last_pair(p):
        return copy(pair_out.at[p], pair_in.at[p], pair_s, pair_r.at[p], pair)

    def second_sum(p, y):
        near2_both(p, y).wait_recv()
        return kept[p, y] + near2_in[p, y, 0].astype(F32) + near2_in[p, y, 1].astype(F32)

    def send_last(p):
        pair_out[p] = second_sum(p, other).astype(BF16)
        last_pair(p).start()

    def keep_last(p):
        kept[p, mine] = second_sum(p, mine)

    for step in (
        (send_other, 0), (send_pair, 2), (send_other, 2), (send_other, 1), (send_pair, 1), (send_far, 2), (send_other, 3),
        (send_pair, 3), (send_mine, 2), (keep, other), (send_far2, other), (send_pair, 0), (send_far, 1), (send_other2, mine),
        (send_far, 3), (send_far2, mine), (send_mine2, other), (send_mine, 1), (send_far, 0), (send_mine, 3), (send_mine, 0),
        (send_last,), (send_other2, other), (send_mine2, mine), (keep, mine), (keep_last,),
    ):
        for p in range(2):
            step[0](p, *step[1:])

    takes[2].wait()
    takes[3].wait()
    v = jnp.zeros((NODES, WIDTH), F32)
    for p in range(2):
        last_pair(p).wait_recv()
        span = slice(p * HALF, (p + 1) * HALF)
        for i, part in enumerate(split(kept[p, mine] + pair_in[p].astype(F32))):
            lifted[i, :, span] = part
            v = v + dot(part, weight[span, :])
    t = jnp.tanh(C0 * (v + 0.044715 * (v * v * v)))
    slope = 0.5 * (1.0 + t) + 0.5 * v * (1.0 - t * t) * (C0 * (1.0 + 3.0 * 0.044715 * (v * v)))
    grad = (output_grad[...].astype(F32) * slope).astype(BF16).astype(F32)

    def own(p, y):
        return copy(grads.at[p, 0, 0, y], grads.at[p, 0, 0, y], g_s.at[0], own_r.at[p], pair)

    def second(p, j, y):
        step, src = {1: (3, 0), 2: (3 - 2 * y, 1 + 2 * y), 3: (1, 0)}[j]
        return copy(
            grads.at[p, 0, src, y], grads.at[p, 0, j, y], g_s.at[2 if j == 2 else 1], second_r.at[p, j - 1, y],
            along(axes[p][1], step),
        )

    def first(p, i, j, y):
        return copy(
            grads.at[p, 0, j, y], grads.at[p, i, j, y], g_s.at[3], first_r.at[p, i // 2, j, y],
            along(axes[p][0], 3 if i == 1 else 1),
        )

    def onward(p, j, d):
        half = pl.ds(d * TILE, TILE)
        return copy(
            grads.at[p, 1 + 2 * d, j, mine, half], grads.at[p, 2, j, mine, half], g_s.at[4], gfar_r.at[p, j],
            along(axes[p][0], steps[d]),
        )

    def onward_both(p, j):
        return copy(grads.at[p, 2, j, mine], grads.at[p, 2, j, mine], g_s.at[4], gfar_r.at[p, j], pair)

    def far_pair(p, j, y):
        return copy(grads.at[p, 2, j, y], grads.at[p, 2, j, y], g_s.at[5], gpair_r.at[p, j], pair)

    def give_first(p, j, y):
        first(p, 1, j, y).start()
        first(p, 3, j, y).start()

    def give_second(p, y):
        second(p, 1, y).start()
        second(p, 3, y).start()

    for p in range(2):
        grads[p, 0, 0, mine] = grad[:, p * HALF:(p + 1) * HALF].T.astype(BF16)
    def weight_half(p):
        block = grads[p, 0, 0, mine]
        return dot(block, lifted[0]) + dot(block, lifted[1])

    spot = x * 4 + z
    y = high * 2 + low
    yspot = (high * 2 + other, (1 - high) * 2 + low, (1 - high) * 2 + other)
    weight_core = copy(wcore_out, wcore_in, w_s.at[0], w_r.at[0], cores)

    def weight_y(s):
        return copy(wsum.at[yspot[s]], wy_in.at[s], w_s.at[1], w_r.at[1], ypeer[s])

    def weight_grid(s):
        part = ((x + s // 4) % 4) * 4 + (z + s % 4) % 4
        return copy(wgrid.at[part], wgrid_in.at[s], w_s.at[2], w_r.at[2], on_grid(s))

    def gather_grid(s):
        return copy(ggrid.at[spot], ggrid.at[spot], w_s.at[3], w_r.at[3], on_grid(s))

    def gather_y(s):
        return copy(wfull.at[core, y], wfull.at[core, y], w_s.at[4], w_r.at[4], ypeer[s])

    def gather_core(half):
        return copy(wfull.at[half], wfull.at[half], w_s.at[5], w_r.at[5], cores)

    weight_all = (
        weight_core,
        copy(wsum.at[pl.ds(0, 3)], wy_in, w_s.at[1], w_r.at[1], cores),
        copy(wgrid.at[pl.ds(1, 15)], wgrid_in.at[pl.ds(1, 15)], w_s.at[2], w_r.at[2], cores),
        copy(ggrid.at[pl.ds(1, 15)], ggrid.at[pl.ds(1, 15)], w_s.at[3], w_r.at[3], cores),
        copy(wfull.at[0, pl.ds(0, 3)], wfull.at[0, pl.ds(0, 3)], w_s.at[4], w_r.at[4], cores),
        gather_core(1 - core),
    )

    def weight_step(k):
        if k > 0:
            weight_all[k - 1].wait_recv()
        if k == 0:
            wcore_out[...] = weight_half(1 - core)
            weight_core.start()
            wsum[...] = weight_half(core).reshape(4, 64, WIDTH)
        elif k == 1:
            wsum[...] = wsum[...] + wcore_in[...].reshape(4, 64, WIDTH)
            for s in range(3):
                weight_y(s).start()
        elif k == 2:
            total = wsum[y]
            for s in range(3):
                total = total + wy_in[s]
            for s in range(16):
                i, j = s // 4, s % 4
                wgrid[s] = total[i * 16:(i + 1) * 16, j * TILE:(j + 1) * TILE]
            loop(15, lambda s: weight_grid(s + 1).start())
        elif k == 3:
            total = wgrid[spot]
            for s in range(1, 16):
                total = total + wgrid_in[s]
            ggrid[spot] = total.astype(BF16)
            loop(15, lambda s: gather_grid(s + 1).start())
        elif k == 4:
            for s in range(16):
                i, j = s // 4, s % 4
                wfull[core, y, i * 16:(i + 1) * 16, j * TILE:(j + 1) * TILE] = ggrid[s]
            for s in range(3):
                gather_y(s).start()
        elif k == 5:
            gather_core(core).start()
        else:
            gives[1].start()

    def product(p, i, j):
        total = None
        for y_ in range(2):
            start = chunk(p, (spots[p][0] + i) % 4, (spots[p][1] + j) % 4, y_) * NODES
            term = dot(grads[p, i, j, y_], dense[pl.ds(pl.multiple_of(start, NODES), NODES), :])
            total = term if total is None else total + term
        return total

    begun = set()

    def add(p, i, j):
        total, fresh = product(p, i, j), p not in begun
        begun.add(p)
        for r in range(PEERS):
            part = total[:, r * NODES:(r + 1) * NODES]
            terms[p, r] = part if fresh else terms[p, r] + part

    def pass_on(p, j):
        for d in range(2):
            first(p, 1 + 2 * d, j, mine).wait_recv()
            onward(p, j, d).start()

    def pass_pair(p, j):
        onward_both(p, j).wait_recv()
        far_pair(p, j, mine).start()

    def use_first(p, j):
        for i in (1, 3):
            first(p, i, j, other).wait_recv()
            add(p, i, j)

    def use_far(p, j):
        far_pair(p, j, other).wait_recv()
        add(p, 2, j)

    gives = (
        pltpu.make_async_copy(output, output_hbm, out_sem.at[0]),
        pltpu.make_async_copy(wfull, grad_weight_hbm, out_sem.at[1]),
        pltpu.make_async_copy(grad_features, grad_features_hbm, out_sem.at[2]),
    )

    def give_output():
        output[...] = (0.5 * v * (1.0 + t)).astype(BF16)
        gives[0].start()

    def give_own():
        for p in range(2):
            own(p, mine).start()

    def take_own(p):
        own(p, other).wait_recv()

    def give_firsts(p, j, y_):
        give_first(p, j, y_)

    def take_second(p, y_):
        second(p, 1, y_).wait_recv()
        second(p, 3, y_).wait_recv()
        second(p, 2, y_).start()

    def take_second2(p, y_):
        second(p, 2, y_).wait_recv()

    def use_own(p, j):
        add(p, 0, j)

    def cols1(p, h):
        return copy(col_out.at[p, h], col_in.at[p, h], c_s, c_r.at[p, h], cores)

    def cols2(p):
        return copy(col2_out.at[p], col2_in.at[p], c2_s, c2_r.at[p], across)

    def give_cols(p):
        for h in (1 - high, high):
            col_out[p, h] = terms[p, 2 * h + 1 - core].astype(BF16)
            cols1(p, h).start()

    def pass_cols(p):
        cols1(p, 1 - high).wait_recv()
        col2_out[p] = (terms[p, row_across] + col_in[p, 1 - high].astype(F32)).astype(BF16)
        cols2(p).start()

    for step in (
        (give_second, 0, mine), (give_second, 1, mine), (give_firsts, 1, 0, mine), (give_own,), (give_output,), (weight_step, 0),
        (give_firsts, 0, 0, mine), (take_own, 0), (take_second, 1, mine), (give_firsts, 1, 3, mine), (take_own, 1),
        (give_second, 1, other), (pass_on, 1, 0), (use_own, 0, 0), (pass_on, 0, 0), (give_second, 0, other),
        (give_firsts, 1, 1, mine), (take_second, 0, mine), (take_second2, 1, mine), (weight_step, 1),
        (give_firsts, 1, 2, mine), (pass_on, 1, 3), (give_firsts, 0, 1, mine), (pass_pair, 1, 0), (take_second, 1, other),
        (take_second, 0, other), (use_own, 1, 1), (use_own, 0, 1), (give_firsts, 0, 3, mine), (take_second2, 1, other),
        (pass_on, 0, 1), (pass_pair, 0, 0), (use_own, 1, 3), (take_second2, 0, mine), (pass_on, 0, 3), (weight_step, 2),
        (pass_on, 1, 1), (pass_pair, 0, 1), (give_firsts, 0, 2, mine), (pass_pair, 0, 3), (give_firsts, 1, 2, other),
        (pass_on, 1, 2), (pass_pair, 1, 3), (take_second2, 0, other), (pass_pair, 1, 1), (give_firsts, 0, 1, other),
        (give_firsts, 0, 3, other), (weight_step, 3), (use_own, 0, 3), (give_firsts, 1, 1, other), (pass_pair, 1, 2),
        (use_far, 1, 0), (give_firsts, 1, 3, other), (pass_on, 0, 2), (use_far, 0, 0), (use_far, 1, 3),
        (give_firsts, 0, 0, other), (give_firsts, 0, 2, other), (use_own, 1, 0), (use_first, 0, 1), (use_far, 0, 3),
        (give_firsts, 1, 0, other), (use_far, 0, 1), (use_far, 1, 1), (use_first, 1, 1), (pass_pair, 0, 2), (use_first, 1, 2),
        (use_first, 0, 3), (use_first, 1, 3), (weight_step, 4), (use_far, 1, 2), (use_own, 1, 2), (use_first, 0, 0),
        (use_first, 1, 0), (give_cols, 1), (use_own, 0, 2), (use_far, 0, 2), (use_first, 0, 2), (pass_cols, 1),
        (give_cols, 0), (pass_cols, 0), (weight_step, 5), (weight_step, 6),
    ):
        step[0](*step[1:])

    def sent(ref, sem):
        copy(ref, ref, sem, sem, pair).wait_send()

    for i, r in ((0, row), (1, row_across)):
        gather(i, r).wait_send()
    sent(pairs_out, pairs_s)
    sent(far_out, far_s)
    sent(near_out, near_s)
    sent(far2_out, far2_s)
    sent(near2_out, near2_s)
    sent(pair_out, pair_s)
    sent(grads.at[0, 0, 0], g_s.at[0])
    sent(grads.at[0, 0], g_s.at[1])
    sent(grads.at[0, 0, pl.ds(0, 2)], g_s.at[2])
    sent(grads.at[0], g_s.at[3])
    sent(grads.at[0, 0], g_s.at[4])
    sent(grads.at[0, 0], g_s.at[5])
    for step in weight_all:
        step.wait_send()

    contract = (((1,), (1,)), ((), ()))
    total = jnp.zeros((NODES, WIDTH), F32)
    for p in (1, 0):
        cols1(p, high).wait_recv()
        cols2(p).wait_recv()
        value = (terms[p, row] + col_in[p, high].astype(F32) + col2_in[p].astype(F32)).T
        for part in split(value):
            total = total + lax.dot_general(
                part, weight[:, p * HALF:(p + 1) * HALF], contract, preferred_element_type=F32
            )
    grad_features[...] = total.astype(BF16)
    gives[2].start()
    sent(col_out, c_s)
    sent(col2_out, c2_s)
    for give in gives:
        give.wait()


def layer(features, features_across, weight, dense, output_grad):
    anywhere = pl.BlockSpec(memory_space=pl.ANY)
    dma = pltpu.SemaphoreType.DMA
    block = (NODES, HALF)
    bf = lambda *shape: pltpu.VMEM(shape, BF16)
    f32 = lambda *shape: pltpu.VMEM(shape, F32)
    return pl.pallas_call(
        layer_kernel,
        out_shape=(
            jax.ShapeDtypeStruct((NODES, WIDTH), BF16),
            jax.ShapeDtypeStruct((NODES, WIDTH), BF16),
            jax.ShapeDtypeStruct((2, 4, 64, WIDTH), BF16),
        ),
        in_specs=[anywhere] * 5,
        out_specs=(anywhere,) * 3,
        scratch_shapes=[
            bf(CHUNKS * NODES, COLS),
            bf(COLS, WIDTH),
            bf(WIDTH, WIDTH),
            bf(NODES, WIDTH),
            bf(NODES, WIDTH),
            bf(NODES, WIDTH),
            bf(2, NODES, WIDTH),
            bf(2, 4, *block), bf(2, 4, *block),
            bf(2, 4, *block), bf(2, 4, 2, TILE, HALF),
            bf(2, 4, 2, 2, *block), bf(2, 4, 2, 2, *block),
            bf(2, 2, *block), bf(2, 2, *block),
            bf(2, 2, 2, *block), bf(2, 2, 2, *block),
            bf(2, *block), bf(2, *block),
            f32(2, 2, *block),
            bf(2, 4, 4, 2, HALF, NODES),
            f32(2, PEERS, HALF, NODES),
            bf(2, 2, HALF, NODES), bf(2, 2, HALF, NODES),
            bf(2, HALF, NODES), bf(2, HALF, NODES),
            f32(HALF, WIDTH), f32(HALF, WIDTH),
            f32(4, 64, WIDTH),
            f32(3, 64, WIDTH),
            f32(16, 16, TILE), f32(16, 16, TILE),
            bf(16, 16, TILE),
            bf(2, 4, 64, WIDTH),
            dma((4, 4, 2)), dma((4,)), dma((3,)),
            dma((2,)), dma((2,)),
            dma, dma((2, 4)),
            dma, dma((2, 4, 2)),
            dma, dma((2, 4, 2)),
            dma, dma((2, 2)),
            dma, dma((2, 2)),
            dma, dma((2,)),
            dma((6,)), dma((2,)), dma((2, 3, 2)), dma((2, 2, 4, 2)), dma((2, 4)), dma((2, 4)),
            dma, dma((2, 2)),
            dma, dma((2,)),
            dma((6,)), dma((6,)),
        ],
        compiler_params=pltpu.CompilerParams(
            collective_id=0, has_side_effects=True, vmem_limit_bytes=LAYER_VMEM
        ),
        name="layer",
    )(features, features_across, weight, dense, output_grad)


def finish_kernel(first_in, second_in, weight_in, first, second, weight):
    first[...] = first_in[...]
    second[...] = second_in[...]
    weight[...] = weight_in[...].astype(F32).T


def finish(output, grad_features, grad_weight):
    vmem = pl.BlockSpec(memory_space=pltpu.VMEM)
    return pl.pallas_call(
        finish_kernel,
        out_shape=(
            jax.ShapeDtypeStruct(output.shape, BF16),
            jax.ShapeDtypeStruct(grad_features.shape, BF16),
            jax.ShapeDtypeStruct(grad_weight.shape, F32),
        ),
        in_specs=[vmem] * 3,
        out_specs=(vmem,) * 3,
        compiler_params=pltpu.CompilerParams(vmem_limit_bytes=FINISH_VMEM),
        name="finish",
    )(output, grad_features, grad_weight)


def per_device(features, weight, tile_values, tile_rows, tile_cols, tile_count, output_grad):
    features_across = lax.ppermute(features, "row", [(r, (r + 2) % PEERS) for r in range(PEERS)])
    dense = place_tiles(tile_values, tile_rows, tile_cols, tile_count)
    output, grad_features, grad_weight = layer(features, features_across, weight, dense, output_grad)
    return finish(output, grad_features, grad_weight.reshape(WIDTH, WIDTH))


def solution(mesh):
    spread = P(("row", "col", "rep"))
    return jax.shard_map(
        per_device,
        mesh=mesh,
        in_specs=(
            P(("row", "col", "rep"), None),
            P(),
            P(("row", "col", "rep"), None, None),
            spread,
            spread,
            spread,
            P(("row", "col", "rep"), None),
        ),
        out_specs=(P(("row", "col", "rep"), None), P(("row", "col", "rep"), None), P()),
        check_vma=False,
    )
```

```python
import math

import jax
import jax.numpy as jnp
from jax import lax
from jax.experimental import pallas as pl
from jax.experimental.pallas import tpu as pltpu
from jax.sharding import PartitionSpec as P

MESH = pl.DeviceIdType.MESH
F32, BF16 = jnp.float32, jnp.bfloat16
TILE = 128
NODES = 256
HALF = 256
WIDTH = 512
PEERS = 4
CHUNKS = 32
COLS = 1024
BANDS = 8
BAND_TILES = 8
PLACE_VMEM, LAYER_VMEM, FINISH_VMEM = 63 * 2**20, 62 * 2**20, 63 * 2**20
C0 = math.sqrt(2.0 / math.pi)


def place_kernel(rows, cols, count, values, dense, tiles, block, listed, filled, in_sem, out_sem):
    slots = tiles.shape[0]
    load = pltpu.make_async_copy(values, tiles, in_sem)
    load.start()

    for g in range(BANDS):
        filled[g] = 0

    def enlist(t, carry):
        g = rows[t] // BAND_TILES
        at = filled[g]
        listed[g, at] = t
        filled[g] = at + 1
        return carry

    lax.fori_loop(0, jnp.minimum(count[0], slots), enlist, 0)

    def clear(i, carry):
        block[pl.ds(pl.multiple_of(i * 64, 64), 64), :] = jnp.zeros((64, COLS), BF16)
        return carry

    lax.fori_loop(0, block.shape[0] // 64, clear, 0)
    load.wait()

    def store(g):
        band = pl.ds(pl.multiple_of(g * BAND_TILES * TILE, BAND_TILES * TILE), BAND_TILES * TILE)
        return pltpu.make_async_copy(block.at[band], dense.at[band], out_sem.at[g])

    def spot_of(t):
        row = pl.multiple_of(rows[t] * TILE, TILE)
        col = pl.multiple_of(cols[t] * TILE, TILE)
        return row, col, (pl.ds(row, TILE), pl.ds(col, TILE))

    for g in range(BANDS):
        def place_two(i, carry):
            t, u = listed[g, 2 * i], listed[g, 2 * i + 1]
            row_t, col_t, at_t = spot_of(t)
            row_u, col_u, at_u = spot_of(u)
            first, second = block[at_t] + tiles[t], block[at_u]
            second = jnp.where((row_t == row_u) & (col_t == col_u), first, second) + tiles[u]
            block[at_t] = first
            block[at_u] = second
            return carry

        def place_last(i, carry):
            t = listed[g, filled[g] - 1]
            at_t = spot_of(t)[2]
            block[at_t] = block[at_t] + tiles[t]
            return carry

        lax.fori_loop(0, filled[g] // 2, place_two, 0)
        lax.fori_loop(0, filled[g] % 2, place_last, 0)
        store(g).start()
    for g in range(BANDS):
        store(g).wait()


def place_tiles(values, rows, cols, count):
    slots = values.shape[0]
    smem = pl.BlockSpec(memory_space=pltpu.SMEM)
    return pl.pallas_call(
        place_kernel,
        out_shape=jax.ShapeDtypeStruct((CHUNKS * NODES, COLS), BF16),
        in_specs=[smem, smem, smem, pl.BlockSpec(memory_space=pl.ANY)],
        out_specs=pl.BlockSpec(memory_space=pl.ANY),
        scratch_shapes=[
            pltpu.VMEM((slots, TILE, TILE), BF16),
            pltpu.VMEM((CHUNKS * NODES, COLS), BF16),
            pltpu.SMEM((BANDS, slots), jnp.int32),
            pltpu.SMEM((BANDS,), jnp.int32),
            pltpu.SemaphoreType.DMA,
            pltpu.SemaphoreType.DMA((BANDS,)),
        ],
        cost_estimate=pl.CostEstimate(flops=0, bytes_accessed=30 * 2**20, transcendentals=0),
        compiler_params=pltpu.CompilerParams(vmem_limit_bytes=PLACE_VMEM),
        name="place_tiles",
    )(rows, cols, count, values)


def dot(a, b):
    return jnp.dot(a, b, preferred_element_type=F32)


def split(v):
    high = v.astype(BF16)
    return high, (v - high.astype(F32)).astype(BF16)


def layer_kernel(
    features, features_across, weight_hbm, dense_hbm, output_grad_hbm, output_hbm, grad_features_hbm, grad_weight_hbm,
    dense, feats, weight, output_grad, output, grad_features, lifted,
    pairs_out, pairs_in, far_out, far_in, near_out, near_in, far2_out, far2_in, near2_out, near2_in, pair_out, pair_in,
    kept, grads, terms, col_out, col_in, col2_out, col2_in,
    wcore_out, wcore_in, wsum, wy_in, wgrid, wgrid_in, ggrid, wfull,
    load_sem, in_sem, out_sem, a_s, a_r, pairs_s, pairs_r, far_s, far_r, near_s, near_r, far2_s, far2_r, near2_s, near2_r,
    pair_s, pair_r, g_s, own_r, second_r, first_r, gfar_r, gpair_r, c_s, c_r, c2_s, c2_r, w_s, w_r,
):
    row, z, rep = lax.axis_index("row"), lax.axis_index("col"), lax.axis_index("rep")
    high, core = row // 2, row % 2
    x, low = rep // 2, rep % 2

    def at(high_=None, core_=None, z_=None, x_=None, low_=None):
        pick = lambda v, own: own if v is None else v
        return {
            "row": pick(high_, high) * 2 + pick(core_, core),
            "col": pick(z_, z),
            "rep": pick(x_, x) * 2 + pick(low_, low),
        }

    def along(axis, step):
        return at(x_=(x + step) % 4) if axis == "x" else at(z_=(z + step) % 4)

    def on_grid(s):
        return at(x_=(x + s // 4) % 4, z_=(z + s % 4) % 4)

    axes = (("x", "z"), ("z", "x"))
    spots = ((x, z), (z, x))
    steps = (3, 1)
    mine, other = low, 1 - low

    def chunk(p, first, second, pair_):
        if p == 0:
            return second * 8 + first * 2 + pair_
        return first * 8 + second * 2 + pair_

    def copy(src, dst, s, r, device):
        return pltpu.make_async_remote_copy(
            src_ref=src, dst_ref=dst, send_sem=s, recv_sem=r, device_id=device, device_id_type=MESH
        )

    cores, pair, across = at(core_=1 - core), at(low_=1 - low), at(high_=1 - high)
    ypeer = (pair, across, at(high_=1 - high, low_=1 - low))

    def loop(n, body):
        def step(i, carry):
            body(i)
            return carry

        lax.fori_loop(0, n, step, 0)

    def rows_of(r):
        return pl.ds(pl.multiple_of(r * NODES, NODES), NODES)

    def load(i, j, pair_):
        span = rows_of(chunk(0, (x + i) % 4, (z + j) % 4, pair_))
        sem = load_sem.at[i, j, 0 if pair_ is mine else 1]
        return pltpu.make_async_copy(dense_hbm.at[span], dense.at[span], sem)

    uses = [(steps[d], o, other) for o in (0,) for d in range(2)]
    uses += [(2, 2, other)] + [(steps[d], 2, other) for d in range(2)] + [(steps[d], 1, other) for d in range(2)]
    uses += [(2, 1, other), (2, 2, mine)] + [(steps[d], 3, other) for d in range(2)] + [(2, 3, other)]
    uses += [(steps[d], 2, mine) for d in range(2)]
    waiting = []
    for i, j, pair_ in uses + [(i, j, pair_) for pair_ in (other, mine) for i in range(4) for j in range(4)]:
        for key in ((i, j, pair_), (j, i, pair_)):
            if not any(key[:2] == k[:2] and key[2] is k[2] for k in waiting):
                waiting.append(key)
    loads = list(waiting)

    def need(p, i, j, pair_):
        for key in waiting:
            if key[:2] == ((i, j), (j, i))[p] and key[2] is pair_:
                load(*key).wait()
                waiting.remove(key)
                break

    def need_all():
        while waiting:
            load(*waiting.pop(0)).wait()

    row_across, row_core, row_last = (1 - high) * 2 + core, high * 2 + 1 - core, (1 - high) * 2 + 1 - core
    takes = (
        pltpu.make_async_copy(features, feats.at[rows_of(row)], in_sem.at[0]),
        pltpu.make_async_copy(features_across, feats.at[rows_of(row_across)], in_sem.at[1]),
        pltpu.make_async_copy(weight_hbm, weight, in_sem.at[2]),
        pltpu.make_async_copy(output_grad_hbm, output_grad, in_sem.at[3]),
    )
    takes[0].start()
    takes[1].start()
    for key in loads[:2]:
        load(*key).start()

    barrier = pltpu.get_barrier_semaphore()

    def greet(s):
        pl.semaphore_signal(barrier, inc=1, device_id=on_grid(s + 1), device_id_type=MESH)

    loop(15, greet)
    for device in (*ypeer, cores):
        pl.semaphore_signal(barrier, inc=1, device_id=device, device_id_type=MESH)
    pl.semaphore_wait(barrier, 19)

    def gather(i, r):
        return copy((features, features_across)[i], feats.at[rows_of(r)], a_s.at[i], a_r.at[i], cores)

    gather(0, row).start()
    gather(1, row_across).start()
    takes[0].wait()
    takes[1].wait()
    for key in loads[2:6]:
        load(*key).start()
    gather(0, row_core).wait_recv()
    gather(1, row_last).wait_recv()
    for key in loads[6:]:
        load(*key).start()
    takes[2].start()
    takes[3].start()

    def partial_at(p, i, j, pair_):
        need(p, i, j, pair_)
        return partial(p, (spots[p][0] + i) % 4, (spots[p][1] + j) % 4, pair_)

    def partial(p, first, second, pair_):
        start = pl.multiple_of(chunk(p, first, second, pair_) * NODES, NODES)
        return dot(dense[pl.ds(start, NODES), :], feats[:, p * HALF:(p + 1) * HALF])

    def pairs(p, o):
        return copy(pairs_out.at[p, o], pairs_in.at[p, o], pairs_s, pairs_r.at[p, o], pair)

    def far(p, o, d):
        half = pl.ds(d * TILE, TILE)
        return copy(far_out.at[p, o, half], far_in.at[p, o, d], far_s, far_r.at[p, o, d], along(axes[p][0], steps[d]))

    def near(p, o, r, d):
        return copy(near_out.at[p, o, r, d], near_in.at[p, o, r, d], near_s, near_r.at[p, o, r], along(axes[p][0], steps[d]))

    def near_both(p, o, r):
        return copy(near_out.at[p, o, r], near_in.at[p, o, r], near_s, near_r.at[p, o, r], pair)

    def send_other(p, o):
        for d in range(2):
            near_out[p, o, 1, d] = partial_at(p, steps[d], o, other).astype(BF16)
            near(p, o, 1, d).start()

    def send_pair(p, o):
        pairs_out[p, o] = partial_at(p, 2, o, other).astype(BF16)
        pairs(p, o).start()

    def send_far(p, o):
        value = partial_at(p, 2, o, mine)
        pairs(p, o).wait_recv()
        far_out[p, o] = (value + pairs_in[p, o].astype(F32)).astype(BF16)
        for d in range(2):
            far(p, o, d).start()

    def send_mine(p, o):
        for d in range(2):
            value = partial_at(p, steps[d], o, mine)
            far(p, o, d).wait_recv()
            half, rest = (slice(0, TILE), slice(TILE, NODES))[::1 - 2 * d]
            near_out[p, o, 0, d, half] = (value[half] + far_in[p, o, d].astype(F32)).astype(BF16)
            near_out[p, o, 0, d, rest] = value[rest].astype(BF16)
            near(p, o, 0, d).start()

    def far2(p, d):
        return copy(far2_out.at[p, d], far2_in.at[p, d], far2_s, far2_r.at[p, d], along(axes[p][1], 3 - 2 * d))

    def near2(p, d, y):
        return copy(near2_out.at[p, y, d], near2_in.at[p, y, d], near2_s, near2_r.at[p, y], along(axes[p][1], 3 - 2 * d))

    def near2_both(p, y):
        return copy(near2_out.at[p, y], near2_in.at[p, y], near2_s, near2_r.at[p, y], pair)

    def first_sum(p, o, y):
        need_all()
        value = partial(p, spots[p][0], (spots[p][1] + o) % 4, y)
        r = (y + low) % 2
        near_both(p, o, r).wait_recv()
        return value + near_in[p, o, r, 0].astype(F32) + near_in[p, o, r, 1].astype(F32)

    def send_far2(p, d):
        far2_out[p, d] = first_sum(p, 2, d).astype(BF16)
        far2(p, d).start()

    def send_other2(p, d):
        near2_out[p, 1 - d, d] = first_sum(p, 3 - 2 * d, 1 - d).astype(BF16)
        near2(p, d, 1 - d).start()

    def send_mine2(p, d):
        value = first_sum(p, 3 - 2 * d, d)
        far2(p, d).wait_recv()
        near2_out[p, d, d] = (value + far2_in[p, d].astype(F32)).astype(BF16)
        near2(p, d, d).start()

    def keep(p, y):
        kept[p, y] = first_sum(p, 0, y)

    def last_pair(p):
        return copy(pair_out.at[p], pair_in.at[p], pair_s, pair_r.at[p], pair)

    def second_sum(p, y):
        near2_both(p, y).wait_recv()
        return kept[p, y] + near2_in[p, y, 0].astype(F32) + near2_in[p, y, 1].astype(F32)

    def send_last(p):
        pair_out[p] = second_sum(p, other).astype(BF16)
        last_pair(p).start()

    def keep_last(p):
        kept[p, mine] = second_sum(p, mine)

    for step in (
        (send_other, 0), (send_pair, 2), (send_other, 2), (send_other, 1), (send_pair, 1), (send_far, 2), (send_other, 3),
        (send_pair, 3), (send_mine, 2), (keep, other), (send_far2, other), (send_pair, 0), (send_far, 1), (send_other2, mine),
        (send_far, 3), (send_far2, mine), (send_mine2, other), (send_mine, 1), (send_far, 0), (send_mine, 3), (send_mine, 0),
        (send_last,), (send_other2, other), (send_mine2, mine), (keep, mine), (keep_last,),
    ):
        for p in range(2):
            step[0](p, *step[1:])

    takes[2].wait()
    takes[3].wait()
    v = jnp.zeros((NODES, WIDTH), F32)
    for p in range(2):
        last_pair(p).wait_recv()
        span = slice(p * HALF, (p + 1) * HALF)
        for i, part in enumerate(split(kept[p, mine] + pair_in[p].astype(F32))):
            lifted[i, :, span] = part
            v = v + dot(part, weight[span, :])
    t = jnp.tanh(C0 * (v + 0.044715 * (v * v * v)))
    slope = 0.5 * (1.0 + t) + 0.5 * v * (1.0 - t * t) * (C0 * (1.0 + 3.0 * 0.044715 * (v * v)))
    grad = (output_grad[...].astype(F32) * slope).astype(BF16).astype(F32)

    def own(p, y):
        return copy(grads.at[p, 0, 0, y], grads.at[p, 0, 0, y], g_s.at[0], own_r.at[p], pair)

    def second(p, j, y):
        step, src = {1: (3, 0), 2: (3 - 2 * y, 1 + 2 * y), 3: (1, 0)}[j]
        return copy(
            grads.at[p, 0, src, y], grads.at[p, 0, j, y], g_s.at[2 if j == 2 else 1], second_r.at[p, j - 1, y],
            along(axes[p][1], step),
        )

    def first(p, i, j, y):
        return copy(
            grads.at[p, 0, j, y], grads.at[p, i, j, y], g_s.at[3], first_r.at[p, i // 2, j, y],
            along(axes[p][0], 3 if i == 1 else 1),
        )

    def onward(p, j, d):
        half = pl.ds(d * TILE, TILE)
        return copy(
            grads.at[p, 1 + 2 * d, j, mine, half], grads.at[p, 2, j, mine, half], g_s.at[4], gfar_r.at[p, j],
            along(axes[p][0], steps[d]),
        )

    def onward_both(p, j):
        return copy(grads.at[p, 2, j, mine], grads.at[p, 2, j, mine], g_s.at[4], gfar_r.at[p, j], pair)

    def far_pair(p, j, y):
        return copy(grads.at[p, 2, j, y], grads.at[p, 2, j, y], g_s.at[5], gpair_r.at[p, j], pair)

    def give_first(p, j, y):
        first(p, 1, j, y).start()
        first(p, 3, j, y).start()

    def give_second(p, y):
        second(p, 1, y).start()
        second(p, 3, y).start()

    for p in range(2):
        grads[p, 0, 0, mine] = grad[:, p * HALF:(p + 1) * HALF].T.astype(BF16)
    def weight_half(p):
        block = grads[p, 0, 0, mine]
        return dot(block, lifted[0]) + dot(block, lifted[1])

    spot = x * 4 + z
    y = high * 2 + low
    yspot = (high * 2 + other, (1 - high) * 2 + low, (1 - high) * 2 + other)
    weight_core = copy(wcore_out, wcore_in, w_s.at[0], w_r.at[0], cores)

    def weight_y(s):
        return copy(wsum.at[yspot[s]], wy_in.at[s], w_s.at[1], w_r.at[1], ypeer[s])

    def weight_grid(s):
        part = ((x + s // 4) % 4) * 4 + (z + s % 4) % 4
        return copy(wgrid.at[part], wgrid_in.at[s], w_s.at[2], w_r.at[2], on_grid(s))

    def gather_grid(s):
        return copy(ggrid.at[spot], ggrid.at[spot], w_s.at[3], w_r.at[3], on_grid(s))

    def gather_y(s):
        return copy(wfull.at[core, y], wfull.at[core, y], w_s.at[4], w_r.at[4], ypeer[s])

    def gather_core(half):
        return copy(wfull.at[half], wfull.at[half], w_s.at[5], w_r.at[5], cores)

    weight_all = (
        weight_core,
        copy(wsum.at[pl.ds(0, 3)], wy_in, w_s.at[1], w_r.at[1], cores),
        copy(wgrid.at[pl.ds(1, 15)], wgrid_in.at[pl.ds(1, 15)], w_s.at[2], w_r.at[2], cores),
        copy(ggrid.at[pl.ds(1, 15)], ggrid.at[pl.ds(1, 15)], w_s.at[3], w_r.at[3], cores),
        copy(wfull.at[0, pl.ds(0, 3)], wfull.at[0, pl.ds(0, 3)], w_s.at[4], w_r.at[4], cores),
        gather_core(1 - core),
    )

    def weight_step(k):
        if k > 0:
            weight_all[k - 1].wait_recv()
        if k == 0:
            wcore_out[...] = weight_half(1 - core)
            weight_core.start()
            wsum[...] = weight_half(core).reshape(4, 64, WIDTH)
        elif k == 1:
            wsum[...] = wsum[...] + wcore_in[...].reshape(4, 64, WIDTH)
            for s in range(3):
                weight_y(s).start()
        elif k == 2:
            total = wsum[y]
            for s in range(3):
                total = total + wy_in[s]
            for s in range(16):
                i, j = s // 4, s % 4
                wgrid[s] = total[i * 16:(i + 1) * 16, j * TILE:(j + 1) * TILE]
            loop(15, lambda s: weight_grid(s + 1).start())
        elif k == 3:
            total = wgrid[spot]
            for s in range(1, 16):
                total = total + wgrid_in[s]
            ggrid[spot] = total.astype(BF16)
            loop(15, lambda s: gather_grid(s + 1).start())
        elif k == 4:
            for s in range(16):
                i, j = s // 4, s % 4
                wfull[core, y, i * 16:(i + 1) * 16, j * TILE:(j + 1) * TILE] = ggrid[s]
            for s in range(3):
                gather_y(s).start()
        elif k == 5:
            gather_core(core).start()
        else:
            gives[1].start()

    def product(p, i, j):
        total = None
        for y_ in range(2):
            start = chunk(p, (spots[p][0] + i) % 4, (spots[p][1] + j) % 4, y_) * NODES
            term = dot(grads[p, i, j, y_], dense[pl.ds(pl.multiple_of(start, NODES), NODES), :])
            total = term if total is None else total + term
        return total

    begun = set()

    def add(p, i, j):
        total, fresh = product(p, i, j), p not in begun
        begun.add(p)
        for r in range(PEERS):
            part = total[:, r * NODES:(r + 1) * NODES]
            terms[p, r] = part if fresh else terms[p, r] + part

    def pass_on(p, j):
        for d in range(2):
            first(p, 1 + 2 * d, j, mine).wait_recv()
            onward(p, j, d).start()

    def pass_pair(p, j):
        onward_both(p, j).wait_recv()
        far_pair(p, j, mine).start()

    def use_first(p, j):
        for i in (1, 3):
            first(p, i, j, other).wait_recv()
            add(p, i, j)

    def use_far(p, j):
        far_pair(p, j, other).wait_recv()
        add(p, 2, j)

    gives = (
        pltpu.make_async_copy(output, output_hbm, out_sem.at[0]),
        pltpu.make_async_copy(wfull, grad_weight_hbm, out_sem.at[1]),
        pltpu.make_async_copy(grad_features, grad_features_hbm, out_sem.at[2]),
    )

    def give_output():
        output[...] = (0.5 * v * (1.0 + t)).astype(BF16)
        gives[0].start()

    def give_own():
        for p in range(2):
            own(p, mine).start()

    def take_own(p):
        own(p, other).wait_recv()

    def give_firsts(p, j, y_):
        give_first(p, j, y_)

    def take_second(p, y_):
        second(p, 1, y_).wait_recv()
        second(p, 3, y_).wait_recv()
        second(p, 2, y_).start()

    def take_second2(p, y_):
        second(p, 2, y_).wait_recv()

    def use_own(p, j):
        add(p, 0, j)

    def cols1(p, h):
        return copy(col_out.at[p, h], col_in.at[p, h], c_s, c_r.at[p, h], cores)

    def cols2(p):
        return copy(col2_out.at[p], col2_in.at[p], c2_s, c2_r.at[p], across)

    def give_cols(p):
        for h in (1 - high, high):
            col_out[p, h] = terms[p, 2 * h + 1 - core].astype(BF16)
            cols1(p, h).start()

    def pass_cols(p):
        cols1(p, 1 - high).wait_recv()
        col2_out[p] = (terms[p, row_across] + col_in[p, 1 - high].astype(F32)).astype(BF16)
        cols2(p).start()

    for step in (
        (give_second, 0, mine), (give_second, 1, mine), (give_firsts, 1, 0, mine), (give_own,), (give_output,), (weight_step, 0),
        (give_firsts, 0, 0, mine), (take_own, 0), (take_second, 1, mine), (give_firsts, 1, 3, mine), (take_own, 1),
        (give_second, 1, other), (pass_on, 1, 0), (use_own, 0, 0), (pass_on, 0, 0), (give_second, 0, other),
        (give_firsts, 1, 1, mine), (take_second, 0, mine), (take_second2, 1, mine), (weight_step, 1),
        (give_firsts, 1, 2, mine), (pass_on, 1, 3), (give_firsts, 0, 1, mine), (pass_pair, 1, 0), (take_second, 1, other),
        (take_second, 0, other), (use_own, 1, 1), (use_own, 0, 1), (give_firsts, 0, 3, mine), (take_second2, 1, other),
        (pass_on, 0, 1), (pass_pair, 0, 0), (use_own, 1, 3), (take_second2, 0, mine), (pass_on, 0, 3), (weight_step, 2),
        (pass_on, 1, 1), (pass_pair, 0, 1), (give_firsts, 0, 2, mine), (pass_pair, 0, 3), (give_firsts, 1, 2, other),
        (pass_on, 1, 2), (pass_pair, 1, 3), (take_second2, 0, other), (pass_pair, 1, 1), (give_firsts, 0, 1, other),
        (give_firsts, 0, 3, other), (weight_step, 3), (use_own, 0, 3), (give_firsts, 1, 1, other), (pass_pair, 1, 2),
        (use_far, 1, 0), (give_firsts, 1, 3, other), (pass_on, 0, 2), (use_far, 0, 0), (use_far, 1, 3),
        (give_firsts, 0, 0, other), (give_firsts, 0, 2, other), (use_own, 1, 0), (use_first, 0, 1), (use_far, 0, 3),
        (give_firsts, 1, 0, other), (use_far, 0, 1), (use_far, 1, 1), (use_first, 1, 1), (pass_pair, 0, 2), (use_first, 1, 2),
        (use_first, 0, 3), (use_first, 1, 3), (weight_step, 4), (use_far, 1, 2), (use_own, 1, 2), (use_first, 0, 0),
        (use_first, 1, 0), (give_cols, 1), (use_own, 0, 2), (use_far, 0, 2), (use_first, 0, 2), (pass_cols, 1),
        (give_cols, 0), (pass_cols, 0), (weight_step, 5), (weight_step, 6),
    ):
        step[0](*step[1:])

    def sent(ref, sem):
        copy(ref, ref, sem, sem, pair).wait_send()

    for i, r in ((0, row), (1, row_across)):
        gather(i, r).wait_send()
    sent(pairs_out, pairs_s)
    sent(far_out, far_s)
    sent(near_out, near_s)
    sent(far2_out, far2_s)
    sent(near2_out, near2_s)
    sent(pair_out, pair_s)
    sent(grads.at[0, 0, 0], g_s.at[0])
    sent(grads.at[0, 0], g_s.at[1])
    sent(grads.at[0, 0, pl.ds(0, 2)], g_s.at[2])
    sent(grads.at[0], g_s.at[3])
    sent(grads.at[0, 0], g_s.at[4])
    sent(grads.at[0, 0], g_s.at[5])
    for step in weight_all:
        step.wait_send()

    contract = (((1,), (1,)), ((), ()))
    total = jnp.zeros((NODES, WIDTH), F32)
    for p in (1, 0):
        cols1(p, high).wait_recv()
        cols2(p).wait_recv()
        value = (terms[p, row] + col_in[p, high].astype(F32) + col2_in[p].astype(F32)).T
        for part in split(value):
            total = total + lax.dot_general(
                part, weight[:, p * HALF:(p + 1) * HALF], contract, preferred_element_type=F32
            )
    grad_features[...] = total.astype(BF16)
    gives[2].start()
    sent(col_out, c_s)
    sent(col2_out, c2_s)
    for give in gives:
        give.wait()


def layer(features, features_across, weight, dense, output_grad):
    anywhere = pl.BlockSpec(memory_space=pl.ANY)
    dma = pltpu.SemaphoreType.DMA
    block = (NODES, HALF)
    bf = lambda *shape: pltpu.VMEM(shape, BF16)
    f32 = lambda *shape: pltpu.VMEM(shape, F32)
    return pl.pallas_call(
        layer_kernel,
        out_shape=(
            jax.ShapeDtypeStruct((NODES, WIDTH), BF16),
            jax.ShapeDtypeStruct((NODES, WIDTH), BF16),
            jax.ShapeDtypeStruct((2, 4, 64, WIDTH), BF16),
        ),
        in_specs=[anywhere] * 5,
        out_specs=(anywhere,) * 3,
        scratch_shapes=[
            bf(CHUNKS * NODES, COLS),
            bf(COLS, WIDTH),
            bf(WIDTH, WIDTH),
            bf(NODES, WIDTH),
            bf(NODES, WIDTH),
            bf(NODES, WIDTH),
            bf(2, NODES, WIDTH),
            bf(2, 4, *block), bf(2, 4, *block),
            bf(2, 4, *block), bf(2, 4, 2, TILE, HALF),
            bf(2, 4, 2, 2, *block), bf(2, 4, 2, 2, *block),
            bf(2, 2, *block), bf(2, 2, *block),
            bf(2, 2, 2, *block), bf(2, 2, 2, *block),
            bf(2, *block), bf(2, *block),
            f32(2, 2, *block),
            bf(2, 4, 4, 2, HALF, NODES),
            f32(2, PEERS, HALF, NODES),
            bf(2, 2, HALF, NODES), bf(2, 2, HALF, NODES),
            bf(2, HALF, NODES), bf(2, HALF, NODES),
            f32(HALF, WIDTH), f32(HALF, WIDTH),
            f32(4, 64, WIDTH),
            f32(3, 64, WIDTH),
            f32(16, 16, TILE), f32(16, 16, TILE),
            bf(16, 16, TILE),
            bf(2, 4, 64, WIDTH),
            dma((4, 4, 2)), dma((4,)), dma((3,)),
            dma((2,)), dma((2,)),
            dma, dma((2, 4)),
            dma, dma((2, 4, 2)),
            dma, dma((2, 4, 2)),
            dma, dma((2, 2)),
            dma, dma((2, 2)),
            dma, dma((2,)),
            dma((6,)), dma((2,)), dma((2, 3, 2)), dma((2, 2, 4, 2)), dma((2, 4)), dma((2, 4)),
            dma, dma((2, 2)),
            dma, dma((2,)),
            dma((6,)), dma((6,)),
        ],
        compiler_params=pltpu.CompilerParams(
            collective_id=0, has_side_effects=True, vmem_limit_bytes=LAYER_VMEM
        ),
        name="layer",
    )(features, features_across, weight, dense, output_grad)


def finish_kernel(first_in, second_in, weight_in, first, second, weight):
    first[...] = first_in[...]
    second[...] = second_in[...]
    weight[...] = weight_in[...].astype(F32).T


def finish(output, grad_features, grad_weight):
    vmem = pl.BlockSpec(memory_space=pltpu.VMEM)
    return pl.pallas_call(
        finish_kernel,
        out_shape=(
            jax.ShapeDtypeStruct(output.shape, BF16),
            jax.ShapeDtypeStruct(grad_features.shape, BF16),
            jax.ShapeDtypeStruct(grad_weight.shape, F32),
        ),
        in_specs=[vmem] * 3,
        out_specs=(vmem,) * 3,
        compiler_params=pltpu.CompilerParams(vmem_limit_bytes=FINISH_VMEM),
        name="finish",
    )(output, grad_features, grad_weight)


def per_device(features, weight, tile_values, tile_rows, tile_cols, tile_count, output_grad):
    features_across = lax.ppermute(features, "row", [(r, (r + 2) % PEERS) for r in range(PEERS)])
    dense = place_tiles(tile_values, tile_rows, tile_cols, tile_count)
    output, grad_features, grad_weight = layer(features, features_across, weight, dense, output_grad)
    return finish(output, grad_features, grad_weight.reshape(WIDTH, WIDTH))


def solution(mesh):
    spread = P(("row", "col", "rep"))
    return jax.shard_map(
        per_device,
        mesh=mesh,
        in_specs=(
            P(("row", "col", "rep"), None),
            P(),
            P(("row", "col", "rep"), None, None),
            spread,
            spread,
            spread,
            P(("row", "col", "rep"), None),
        ),
        out_specs=(P(("row", "col", "rep"), None), P(("row", "col", "rep"), None), P()),
        check_vma=False,
    )
```

```python
import math

import jax
import jax.numpy as jnp
from jax import lax
from jax.experimental import pallas as pl
from jax.experimental.pallas import tpu as pltpu
from jax.sharding import PartitionSpec as P

MESH = pl.DeviceIdType.MESH
F32, BF16 = jnp.float32, jnp.bfloat16
TILE = 128
NODES = 256
HALF = 256
WIDTH = 512
PEERS = 4
CHUNKS = 32
COLS = 1024
BANDS = 8
BAND_TILES = 8
PLACE_VMEM, LAYER_VMEM, FINISH_VMEM = 63 * 2**20, 62 * 2**20, 63 * 2**20
C0 = math.sqrt(2.0 / math.pi)


def place_kernel(rows, cols, count, values, dense, tiles, block, listed, filled, in_sem, out_sem):
    slots = tiles.shape[0]
    load = pltpu.make_async_copy(values, tiles, in_sem)
    load.start()

    for g in range(BANDS):
        filled[g] = 0

    def enlist(t, carry):
        g = rows[t] // BAND_TILES
        at = filled[g]
        listed[g, at] = t
        filled[g] = at + 1
        return carry

    lax.fori_loop(0, jnp.minimum(count[0], slots), enlist, 0)

    def clear(i, carry):
        block[pl.ds(pl.multiple_of(i * 64, 64), 64), :] = jnp.zeros((64, COLS), BF16)
        return carry

    lax.fori_loop(0, block.shape[0] // 64, clear, 0)
    load.wait()

    def store(g):
        band = pl.ds(pl.multiple_of(g * BAND_TILES * TILE, BAND_TILES * TILE), BAND_TILES * TILE)
        return pltpu.make_async_copy(block.at[band], dense.at[band], out_sem.at[g])

    for g in range(BANDS):
        def place(i, carry):
            t = listed[g, i]
            row = pl.ds(pl.multiple_of(rows[t] * TILE, TILE), TILE)
            col = pl.ds(pl.multiple_of(cols[t] * TILE, TILE), TILE)
            block[row, col] = block[row, col] + tiles[t]
            return carry

        lax.fori_loop(0, filled[g], place, 0)
        store(g).start()
    for g in range(BANDS):
        store(g).wait()


def place_tiles(values, rows, cols, count):
    slots = values.shape[0]
    smem = pl.BlockSpec(memory_space=pltpu.SMEM)
    return pl.pallas_call(
        place_kernel,
        out_shape=jax.ShapeDtypeStruct((CHUNKS * NODES, COLS), BF16),
        in_specs=[smem, smem, smem, pl.BlockSpec(memory_space=pl.ANY)],
        out_specs=pl.BlockSpec(memory_space=pl.ANY),
        scratch_shapes=[
            pltpu.VMEM((slots, TILE, TILE), BF16),
            pltpu.VMEM((CHUNKS * NODES, COLS), BF16),
            pltpu.SMEM((BANDS, slots), jnp.int32),
            pltpu.SMEM((BANDS,), jnp.int32),
            pltpu.SemaphoreType.DMA,
            pltpu.SemaphoreType.DMA((BANDS,)),
        ],
        cost_estimate=pl.CostEstimate(flops=0, bytes_accessed=30 * 2**20, transcendentals=0),
        compiler_params=pltpu.CompilerParams(vmem_limit_bytes=PLACE_VMEM),
        name="place_tiles",
    )(rows, cols, count, values)


def dot(a, b):
    return jnp.dot(a, b, preferred_element_type=F32)


def split(v):
    high = v.astype(BF16)
    return high, (v - high.astype(F32)).astype(BF16)


def layer_kernel(
    features, features_across, weight_hbm, dense_hbm, output_grad_hbm, output_hbm, grad_features_hbm, grad_weight_hbm,
    dense, feats, weight, output_grad, output, grad_features, lifted,
    pairs_out, pairs_in, far_out, far_in, near_out, near_in, pairs2_out, pairs2_in, far2_out, far2_in, near2_out, near2_in, pair_out, pair_in,
    kept, grads, terms, col_out, col_in, col2_out, col2_in,
    wcore_out, wcore_in, wsum, wy_in, wgrid, wgrid_in, ggrid, wfull,
    load_sem, in_sem, out_sem, a_s, a_r, pairs_s, pairs_r, far_s, far_r, near_s, near_r, pairs2_s, pairs2_r, far2_s, far2_r, near2_s, near2_r,
    pair_s, pair_r, g_s, own_r, second_r, first_r, gfar_r, gpair_r, c_s, c_r, c2_s, c2_r, w_s, w_r,
):
    row, z, rep = lax.axis_index("row"), lax.axis_index("col"), lax.axis_index("rep")
    high, core = row // 2, row % 2
    x, low = rep // 2, rep % 2

    def at(high_=None, core_=None, z_=None, x_=None, low_=None):
        pick = lambda v, own: own if v is None else v
        return {
            "row": pick(high_, high) * 2 + pick(core_, core),
            "col": pick(z_, z),
            "rep": pick(x_, x) * 2 + pick(low_, low),
        }

    def along(axis, step):
        return at(x_=(x + step) % 4) if axis == "x" else at(z_=(z + step) % 4)

    def on_grid(s):
        return at(x_=(x + s // 4) % 4, z_=(z + s % 4) % 4)

    axes = (("x", "z"), ("z", "x"))
    spots = ((x, z), (z, x))
    steps = (3, 1)
    mine, other = low, 1 - low

    def chunk(p, first, second, pair_):
        if p == 0:
            return second * 8 + first * 2 + pair_
        return first * 8 + second * 2 + pair_

    def copy(src, dst, s, r, device):
        return pltpu.make_async_remote_copy(
            src_ref=src, dst_ref=dst, send_sem=s, recv_sem=r, device_id=device, device_id_type=MESH
        )

    cores, pair, across = at(core_=1 - core), at(low_=1 - low), at(high_=1 - high)
    ypeer = (pair, across, at(high_=1 - high, low_=1 - low))

    def loop(n, body):
        def step(i, carry):
            body(i)
            return carry

        lax.fori_loop(0, n, step, 0)

    def rows_of(r):
        return pl.ds(pl.multiple_of(r * NODES, NODES), NODES)

    def load(i, j, pair_):
        span = rows_of(chunk(0, (x + i) % 4, (z + j) % 4, pair_))
        sem = load_sem.at[i, j, 0 if pair_ is mine else 1]
        return pltpu.make_async_copy(dense_hbm.at[span], dense.at[span], sem)

    uses = [(2, 1, other)] + [(steps[d], 0, other) for d in range(2)] + [(2, 2, other)]
    uses += [(steps[d], o, other) for o in (2, 1) for d in range(2)] + [(2, 3, other), (2, 0, other), (2, 1, mine)]
    waiting = []
    for i, j, pair_ in uses + [(i, j, pair_) for pair_ in (other, mine) for i in range(4) for j in range(4)]:
        for key in ((i, j, pair_), (j, i, pair_)):
            if not any(key[:2] == k[:2] and key[2] is k[2] for k in waiting):
                waiting.append(key)
    loads = list(waiting)

    def need(p, i, j, pair_):
        for key in waiting:
            if key[:2] == ((i, j), (j, i))[p] and key[2] is pair_:
                load(*key).wait()
                waiting.remove(key)
                break

    def need_all():
        while waiting:
            load(*waiting.pop(0)).wait()

    row_across, row_core, row_last = (1 - high) * 2 + core, high * 2 + 1 - core, (1 - high) * 2 + 1 - core
    takes = (
        pltpu.make_async_copy(features, feats.at[rows_of(row)], in_sem.at[0]),
        pltpu.make_async_copy(features_across, feats.at[rows_of(row_across)], in_sem.at[1]),
        pltpu.make_async_copy(weight_hbm, weight, in_sem.at[2]),
        pltpu.make_async_copy(output_grad_hbm, output_grad, in_sem.at[3]),
    )
    takes[0].start()
    takes[1].start()
    for key in loads[:2]:
        load(*key).start()

    barrier = pltpu.get_barrier_semaphore()

    def greet(s):
        pl.semaphore_signal(barrier, inc=1, device_id=on_grid(s + 1), device_id_type=MESH)

    loop(15, greet)
    for device in (*ypeer, cores):
        pl.semaphore_signal(barrier, inc=1, device_id=device, device_id_type=MESH)
    pl.semaphore_wait(barrier, 19)

    def gather(i, r):
        return copy((features, features_across)[i], feats.at[rows_of(r)], a_s.at[i], a_r.at[i], cores)

    gather(0, row).start()
    gather(1, row_across).start()
    takes[0].wait()
    takes[1].wait()
    for key in loads[2:6]:
        load(*key).start()
    gather(0, row_core).wait_recv()
    gather(1, row_last).wait_recv()
    for key in loads[6:]:
        load(*key).start()
    takes[2].start()
    takes[3].start()

    def partial_at(p, i, j, pair_):
        need(p, i, j, pair_)
        return partial(p, (spots[p][0] + i) % 4, (spots[p][1] + j) % 4, pair_)

    def partial(p, first, second, pair_):
        start = pl.multiple_of(chunk(p, first, second, pair_) * NODES, NODES)
        return dot(dense[pl.ds(start, NODES), :], feats[:, p * HALF:(p + 1) * HALF])

    def pairs(p, o):
        return copy(pairs_out.at[p, o], pairs_in.at[p, o], pairs_s, pairs_r.at[p, o], pair)

    def far(p, o, d):
        half = pl.ds(d * TILE, TILE)
        return copy(far_out.at[p, o, half], far_in.at[p, o, d], far_s, far_r.at[p, o, d], along(axes[p][0], steps[d]))

    def near(p, o, r, d):
        return copy(near_out.at[p, o, r, d], near_in.at[p, o, r, d], near_s, near_r.at[p, o, r], along(axes[p][0], steps[d]))

    def near_both(p, o, r):
        return copy(near_out.at[p, o, r], near_in.at[p, o, r], near_s, near_r.at[p, o, r], pair)

    def send_other(p, o):
        for d in range(2):
            near_out[p, o, 1, d] = partial_at(p, steps[d], o, other).astype(BF16)
            near(p, o, 1, d).start()

    def send_pair(p, o):
        pairs_out[p, o] = partial_at(p, 2, o, other).astype(BF16)
        pairs(p, o).start()

    def send_far(p, o):
        value = partial_at(p, 2, o, mine)
        pairs(p, o).wait_recv()
        far_out[p, o] = (value + pairs_in[p, o].astype(F32)).astype(BF16)
        for d in range(2):
            far(p, o, d).start()

    def send_mine(p, o):
        for d in range(2):
            value = partial_at(p, steps[d], o, mine)
            far(p, o, d).wait_recv()
            half, rest = (slice(0, TILE), slice(TILE, NODES))[::1 - 2 * d]
            near_out[p, o, 0, d, half] = (value[half] + far_in[p, o, d].astype(F32)).astype(BF16)
            near_out[p, o, 0, d, rest] = value[rest].astype(BF16)
            near(p, o, 0, d).start()

    def pairs2(p):
        return copy(pairs2_out.at[p], pairs2_in.at[p], pairs2_s, pairs2_r.at[p], pair)

    def far2(p, d):
        half = pl.ds(d * TILE, TILE)
        return copy(far2_out.at[p, half], far2_in.at[p, d], far2_s, far2_r.at[p, d], along(axes[p][1], steps[d]))

    def near2(p, r, d):
        return copy(near2_out.at[p, r, d], near2_in.at[p, r, d], near2_s, near2_r.at[p, r], along(axes[p][1], steps[d]))

    def near2_both(p, r):
        return copy(near2_out.at[p, r], near2_in.at[p, r], near2_s, near2_r.at[p, r], pair)

    def first_sum(p, o, y):
        need_all()
        value = partial(p, spots[p][0], (spots[p][1] + o) % 4, y)
        r = 0 if y is mine else 1
        near_both(p, o, r).wait_recv()
        return value + near_in[p, o, r, 0].astype(F32) + near_in[p, o, r, 1].astype(F32)

    def send_pair2(p):
        pairs2_out[p] = first_sum(p, 2, other).astype(BF16)
        pairs2(p).start()

    def send_far2(p):
        value = first_sum(p, 2, mine)
        pairs2(p).wait_recv()
        far2_out[p] = (value + pairs2_in[p].astype(F32)).astype(BF16)
        for d in range(2):
            far2(p, d).start()

    def send_other2(p, d):
        near2_out[p, 1, d] = first_sum(p, steps[d], other).astype(BF16)
        near2(p, 1, d).start()

    def send_mine2(p, d):
        value = first_sum(p, steps[d], mine)
        far2(p, d).wait_recv()
        half, rest = (slice(0, TILE), slice(TILE, NODES))[::1 - 2 * d]
        near2_out[p, 0, d, half] = (value[half] + far2_in[p, d].astype(F32)).astype(BF16)
        near2_out[p, 0, d, rest] = value[rest].astype(BF16)
        near2(p, 0, d).start()

    def keep(p, y):
        kept[p, y] = first_sum(p, 0, y)

    def last_pair(p):
        return copy(pair_out.at[p], pair_in.at[p], pair_s, pair_r.at[p], pair)

    def second_sum(p, y):
        r = 0 if y is mine else 1
        near2_both(p, r).wait_recv()
        return kept[p, y] + near2_in[p, r, 0].astype(F32) + near2_in[p, r, 1].astype(F32)

    def send_last(p):
        pair_out[p] = second_sum(p, other).astype(BF16)
        last_pair(p).start()

    def keep_last(p):
        kept[p, mine] = second_sum(p, mine)

    for step in (
        (send_pair, 1), (send_other, 0), (send_pair, 2), (send_other, 2), (send_other, 1), (send_pair, 3), (send_pair, 0),
        (send_far, 1), (send_pair2,), (send_other, 3), (send_far, 2), (send_mine, 1), (send_mine, 2), (send_far, 3),
        (send_other2, 1), (send_other2, 0), (send_far, 0), (send_mine, 3), (keep, other), (send_far2,), (send_mine, 0),
        (send_last,), (send_mine2, 0), (send_mine2, 1), (keep, mine), (keep_last,),
    ):
        for p in range(2):
            step[0](p, *step[1:])

    takes[2].wait()
    takes[3].wait()
    v = jnp.zeros((NODES, WIDTH), F32)
    for p in range(2):
        last_pair(p).wait_recv()
        span = slice(p * HALF, (p + 1) * HALF)
        for i, part in enumerate(split(kept[p, mine] + pair_in[p].astype(F32))):
            lifted[i, :, span] = part
            v = v + dot(part, weight[span, :])
    t = jnp.tanh(C0 * (v + 0.044715 * (v * v * v)))
    slope = 0.5 * (1.0 + t) + 0.5 * v * (1.0 - t * t) * (C0 * (1.0 + 3.0 * 0.044715 * (v * v)))
    grad = (output_grad[...].astype(F32) * slope).astype(BF16).astype(F32)

    def own(p, y):
        return copy(grads.at[p, 0, 0, y], grads.at[p, 0, 0, y], g_s.at[0], own_r.at[p], pair)

    def second(p, j, y):
        step, src = {1: (3, 0), 2: (3 - 2 * y, 1 + 2 * y), 3: (1, 0)}[j]
        return copy(
            grads.at[p, 0, src, y], grads.at[p, 0, j, y], g_s.at[2 if j == 2 else 1], second_r.at[p, j - 1, y],
            along(axes[p][1], step),
        )

    def first(p, i, j, y):
        return copy(
            grads.at[p, 0, j, y], grads.at[p, i, j, y], g_s.at[3], first_r.at[p, i // 2, j, y],
            along(axes[p][0], 3 if i == 1 else 1),
        )

    def onward(p, j, d):
        half = pl.ds(d * TILE, TILE)
        return copy(
            grads.at[p, 1 + 2 * d, j, mine, half], grads.at[p, 2, j, mine, half], g_s.at[4], gfar_r.at[p, j],
            along(axes[p][0], steps[d]),
        )

    def onward_both(p, j):
        return copy(grads.at[p, 2, j, mine], grads.at[p, 2, j, mine], g_s.at[4], gfar_r.at[p, j], pair)

    def far_pair(p, j, y):
        return copy(grads.at[p, 2, j, y], grads.at[p, 2, j, y], g_s.at[5], gpair_r.at[p, j], pair)

    def give_first(p, j, y):
        first(p, 1, j, y).start()
        first(p, 3, j, y).start()

    def give_second(p, y):
        second(p, 1, y).start()
        second(p, 3, y).start()

    for p in range(2):
        grads[p, 0, 0, mine] = grad[:, p * HALF:(p + 1) * HALF].T.astype(BF16)
    def weight_half(p):
        block = grads[p, 0, 0, mine]
        return dot(block, lifted[0]) + dot(block, lifted[1])

    spot = x * 4 + z
    y = high * 2 + low
    yspot = (high * 2 + other, (1 - high) * 2 + low, (1 - high) * 2 + other)
    weight_core = copy(wcore_out, wcore_in, w_s.at[0], w_r.at[0], cores)

    def weight_y(s):
        return copy(wsum.at[yspot[s]], wy_in.at[s], w_s.at[1], w_r.at[1], ypeer[s])

    def weight_grid(s):
        part = ((x + s // 4) % 4) * 4 + (z + s % 4) % 4
        return copy(wgrid.at[part], wgrid_in.at[s], w_s.at[2], w_r.at[2], on_grid(s))

    def gather_grid(s):
        return copy(ggrid.at[spot], ggrid.at[spot], w_s.at[3], w_r.at[3], on_grid(s))

    def gather_y(s):
        return copy(wfull.at[core, y], wfull.at[core, y], w_s.at[4], w_r.at[4], ypeer[s])

    def gather_core(half):
        return copy(wfull.at[half], wfull.at[half], w_s.at[5], w_r.at[5], cores)

    weight_all = (
        weight_core,
        copy(wsum.at[pl.ds(0, 3)], wy_in, w_s.at[1], w_r.at[1], cores),
        copy(wgrid.at[pl.ds(1, 15)], wgrid_in.at[pl.ds(1, 15)], w_s.at[2], w_r.at[2], cores),
        copy(ggrid.at[pl.ds(1, 15)], ggrid.at[pl.ds(1, 15)], w_s.at[3], w_r.at[3], cores),
        copy(wfull.at[0, pl.ds(0, 3)], wfull.at[0, pl.ds(0, 3)], w_s.at[4], w_r.at[4], cores),
        gather_core(1 - core),
    )

    def weight_step(k):
        if k > 0:
            weight_all[k - 1].wait_recv()
        if k == 0:
            wcore_out[...] = weight_half(1 - core)
            weight_core.start()
            wsum[...] = weight_half(core).reshape(4, 64, WIDTH)
        elif k == 1:
            wsum[...] = wsum[...] + wcore_in[...].reshape(4, 64, WIDTH)
            for s in range(3):
                weight_y(s).start()
        elif k == 2:
            total = wsum[y]
            for s in range(3):
                total = total + wy_in[s]
            for s in range(16):
                i, j = s // 4, s % 4
                wgrid[s] = total[i * 16:(i + 1) * 16, j * TILE:(j + 1) * TILE]
            loop(15, lambda s: weight_grid(s + 1).start())
        elif k == 3:
            total = wgrid[spot]
            for s in range(1, 16):
                total = total + wgrid_in[s]
            ggrid[spot] = total.astype(BF16)
            loop(15, lambda s: gather_grid(s + 1).start())
        elif k == 4:
            for s in range(16):
                i, j = s // 4, s % 4
                wfull[core, y, i * 16:(i + 1) * 16, j * TILE:(j + 1) * TILE] = ggrid[s]
            for s in range(3):
                gather_y(s).start()
        elif k == 5:
            gather_core(core).start()
        else:
            gives[1].start()

    def product(p, i, j):
        total = None
        for y_ in range(2):
            start = chunk(p, (spots[p][0] + i) % 4, (spots[p][1] + j) % 4, y_) * NODES
            term = dot(grads[p, i, j, y_], dense[pl.ds(pl.multiple_of(start, NODES), NODES), :])
            total = term if total is None else total + term
        return total

    begun = set()

    def add(p, i, j):
        total, fresh = product(p, i, j), p not in begun
        begun.add(p)
        for r in range(PEERS):
            part = total[:, r * NODES:(r + 1) * NODES]
            terms[p, r] = part if fresh else terms[p, r] + part

    def pass_on(p, j):
        for d in range(2):
            first(p, 1 + 2 * d, j, mine).wait_recv()
            onward(p, j, d).start()

    def pass_pair(p, j):
        onward_both(p, j).wait_recv()
        far_pair(p, j, mine).start()

    def use_first(p, j):
        for i in (1, 3):
            first(p, i, j, other).wait_recv()
            add(p, i, j)

    def use_far(p, j):
        far_pair(p, j, other).wait_recv()
        add(p, 2, j)

    gives = (
        pltpu.make_async_copy(output, output_hbm, out_sem.at[0]),
        pltpu.make_async_copy(wfull, grad_weight_hbm, out_sem.at[1]),
        pltpu.make_async_copy(grad_features, grad_features_hbm, out_sem.at[2]),
    )

    def give_output():
        output[...] = (0.5 * v * (1.0 + t)).astype(BF16)
        gives[0].start()

    def give_own():
        for p in range(2):
            own(p, mine).start()

    def take_own(p):
        own(p, other).wait_recv()

    def give_firsts(p, j, y_):
        give_first(p, j, y_)

    def take_second(p, y_):
        second(p, 1, y_).wait_recv()
        second(p, 3, y_).wait_recv()
        second(p, 2, y_).start()

    def take_second2(p, y_):
        second(p, 2, y_).wait_recv()

    def use_own(p, j):
        add(p, 0, j)

    def cols1(p, h):
        return copy(col_out.at[p, h], col_in.at[p, h], c_s, c_r.at[p, h], cores)

    def cols2(p):
        return copy(col2_out.at[p], col2_in.at[p], c2_s, c2_r.at[p], across)

    def give_cols(p):
        for h in (1 - high, high):
            col_out[p, h] = terms[p, 2 * h + 1 - core].astype(BF16)
            cols1(p, h).start()

    def pass_cols(p):
        cols1(p, 1 - high).wait_recv()
        col2_out[p] = (terms[p, row_across] + col_in[p, 1 - high].astype(F32)).astype(BF16)
        cols2(p).start()

    for step in (
        (give_second, 0, mine), (give_second, 1, mine), (give_firsts, 1, 0, mine), (give_own,), (give_output,), (weight_step, 0),
        (give_firsts, 0, 0, mine), (take_own, 0), (take_second, 1, mine), (give_firsts, 1, 3, mine), (take_own, 1),
        (give_second, 1, other), (pass_on, 1, 0), (use_own, 0, 0), (pass_on, 0, 0), (give_second, 0, other),
        (give_firsts, 1, 1, mine), (take_second, 0, mine), (take_second2, 1, mine), (weight_step, 1),
        (give_firsts, 1, 2, mine), (pass_on, 1, 3), (give_firsts, 0, 1, mine), (pass_pair, 1, 0), (take_second, 1, other),
        (take_second, 0, other), (use_own, 1, 1), (use_own, 0, 1), (give_firsts, 0, 3, mine), (take_second2, 1, other),
        (pass_on, 0, 1), (pass_pair, 0, 0), (use_own, 1, 3), (take_second2, 0, mine), (pass_on, 0, 3), (weight_step, 2),
        (pass_on, 1, 1), (pass_pair, 0, 1), (give_firsts, 0, 2, mine), (pass_pair, 0, 3), (give_firsts, 1, 2, other),
        (pass_on, 1, 2), (pass_pair, 1, 3), (take_second2, 0, other), (pass_pair, 1, 1), (give_firsts, 0, 1, other),
        (give_firsts, 0, 3, other), (weight_step, 3), (use_own, 0, 3), (give_firsts, 1, 1, other), (pass_pair, 1, 2),
        (use_far, 1, 0), (give_firsts, 1, 3, other), (pass_on, 0, 2), (use_far, 0, 0), (use_far, 1, 3),
        (give_firsts, 0, 0, other), (give_firsts, 0, 2, other), (use_own, 1, 0), (use_first, 0, 1), (use_far, 0, 3),
        (give_firsts, 1, 0, other), (use_far, 0, 1), (use_far, 1, 1), (use_first, 1, 1), (pass_pair, 0, 2), (use_first, 1, 2),
        (use_first, 0, 3), (use_first, 1, 3), (weight_step, 4), (use_far, 1, 2), (use_own, 1, 2), (use_first, 0, 0),
        (use_first, 1, 0), (give_cols, 1), (use_own, 0, 2), (use_far, 0, 2), (use_first, 0, 2), (pass_cols, 1),
        (give_cols, 0), (pass_cols, 0), (weight_step, 5), (weight_step, 6),
    ):
        step[0](*step[1:])

    def sent(ref, sem):
        copy(ref, ref, sem, sem, pair).wait_send()

    for i, r in ((0, row), (1, row_across)):
        gather(i, r).wait_send()
    sent(pairs_out, pairs_s)
    sent(far_out, far_s)
    sent(near_out, near_s)
    sent(pairs2_out, pairs2_s)
    sent(far2_out, far2_s)
    sent(near2_out, near2_s)
    sent(pair_out, pair_s)
    sent(grads.at[0, 0, 0], g_s.at[0])
    sent(grads.at[0, 0], g_s.at[1])
    sent(grads.at[0, 0, pl.ds(0, 2)], g_s.at[2])
    sent(grads.at[0], g_s.at[3])
    sent(grads.at[0, 0], g_s.at[4])
    sent(grads.at[0, 0], g_s.at[5])
    for step in weight_all:
        step.wait_send()

    contract = (((1,), (1,)), ((), ()))
    total = jnp.zeros((NODES, WIDTH), F32)
    for p in (1, 0):
        cols1(p, high).wait_recv()
        cols2(p).wait_recv()
        value = (terms[p, row] + col_in[p, high].astype(F32) + col2_in[p].astype(F32)).T
        for part in split(value):
            total = total + lax.dot_general(
                part, weight[:, p * HALF:(p + 1) * HALF], contract, preferred_element_type=F32
            )
    grad_features[...] = total.astype(BF16)
    gives[2].start()
    sent(col_out, c_s)
    sent(col2_out, c2_s)
    for give in gives:
        give.wait()


def layer(features, features_across, weight, dense, output_grad):
    anywhere = pl.BlockSpec(memory_space=pl.ANY)
    dma = pltpu.SemaphoreType.DMA
    block = (NODES, HALF)
    bf = lambda *shape: pltpu.VMEM(shape, BF16)
    f32 = lambda *shape: pltpu.VMEM(shape, F32)
    return pl.pallas_call(
        layer_kernel,
        out_shape=(
            jax.ShapeDtypeStruct((NODES, WIDTH), BF16),
            jax.ShapeDtypeStruct((NODES, WIDTH), BF16),
            jax.ShapeDtypeStruct((2, 4, 64, WIDTH), BF16),
        ),
        in_specs=[anywhere] * 5,
        out_specs=(anywhere,) * 3,
        scratch_shapes=[
            bf(CHUNKS * NODES, COLS),
            bf(COLS, WIDTH),
            bf(WIDTH, WIDTH),
            bf(NODES, WIDTH),
            bf(NODES, WIDTH),
            bf(NODES, WIDTH),
            bf(2, NODES, WIDTH),
            bf(2, 4, *block), bf(2, 4, *block),
            bf(2, 4, *block), bf(2, 4, 2, TILE, HALF),
            bf(2, 4, 2, 2, *block), bf(2, 4, 2, 2, *block),
            bf(2, *block), bf(2, *block),
            bf(2, *block), bf(2, 2, TILE, HALF),
            bf(2, 2, 2, *block), bf(2, 2, 2, *block),
            bf(2, *block), bf(2, *block),
            f32(2, 2, *block),
            bf(2, 4, 4, 2, HALF, NODES),
            f32(2, PEERS, HALF, NODES),
            bf(2, 2, HALF, NODES), bf(2, 2, HALF, NODES),
            bf(2, HALF, NODES), bf(2, HALF, NODES),
            f32(HALF, WIDTH), f32(HALF, WIDTH),
            f32(4, 64, WIDTH),
            f32(3, 64, WIDTH),
            f32(16, 16, TILE), f32(16, 16, TILE),
            bf(16, 16, TILE),
            bf(2, 4, 64, WIDTH),
            dma((4, 4, 2)), dma((4,)), dma((3,)),
            dma((2,)), dma((2,)),
            dma, dma((2, 4)),
            dma, dma((2, 4, 2)),
            dma, dma((2, 4, 2)),
            dma, dma((2,)),
            dma, dma((2, 2)),
            dma, dma((2, 2)),
            dma, dma((2,)),
            dma((6,)), dma((2,)), dma((2, 3, 2)), dma((2, 2, 4, 2)), dma((2, 4)), dma((2, 4)),
            dma, dma((2, 2)),
            dma, dma((2,)),
            dma((6,)), dma((6,)),
        ],
        compiler_params=pltpu.CompilerParams(
            collective_id=0, has_side_effects=True, vmem_limit_bytes=LAYER_VMEM
        ),
        name="layer",
    )(features, features_across, weight, dense, output_grad)


def finish_kernel(first_in, second_in, weight_in, first, second, weight):
    first[...] = first_in[...]
    second[...] = second_in[...]
    weight[...] = weight_in[...].astype(F32).T


def finish(output, grad_features, grad_weight):
    vmem = pl.BlockSpec(memory_space=pltpu.VMEM)
    return pl.pallas_call(
        finish_kernel,
        out_shape=(
            jax.ShapeDtypeStruct(output.shape, BF16),
            jax.ShapeDtypeStruct(grad_features.shape, BF16),
            jax.ShapeDtypeStruct(grad_weight.shape, F32),
        ),
        in_specs=[vmem] * 3,
        out_specs=(vmem,) * 3,
        compiler_params=pltpu.CompilerParams(vmem_limit_bytes=FINISH_VMEM),
        name="finish",
    )(output, grad_features, grad_weight)


def per_device(features, weight, tile_values, tile_rows, tile_cols, tile_count, output_grad):
    features_across = lax.ppermute(features, "row", [(r, (r + 2) % PEERS) for r in range(PEERS)])
    dense = place_tiles(tile_values, tile_rows, tile_cols, tile_count)
    output, grad_features, grad_weight = layer(features, features_across, weight, dense, output_grad)
    return finish(output, grad_features, grad_weight.reshape(WIDTH, WIDTH))


def solution(mesh):
    spread = P(("row", "col", "rep"))
    return jax.shard_map(
        per_device,
        mesh=mesh,
        in_specs=(
            P(("row", "col", "rep"), None),
            P(),
            P(("row", "col", "rep"), None, None),
            spread,
            spread,
            spread,
            P(("row", "col", "rep"), None),
        ),
        out_specs=(P(("row", "col", "rep"), None), P(("row", "col", "rep"), None), P()),
        check_vma=False,
    )
```

```python
import math

import jax
import jax.numpy as jnp
from jax import lax
from jax.experimental import pallas as pl
from jax.experimental.pallas import tpu as pltpu
from jax.sharding import PartitionSpec as P

MESH = pl.DeviceIdType.MESH
F32, BF16 = jnp.float32, jnp.bfloat16
TILE = 128
NODES = 256
HALF = 256
WIDTH = 512
PEERS = 4
CHUNKS = 32
COLS = 1024
BANDS = 8
BAND_TILES = 8
PLACE_VMEM, LAYER_VMEM, FINISH_VMEM = 63 * 2**20, 62 * 2**20, 63 * 2**20
C0 = math.sqrt(2.0 / math.pi)


def place_kernel(rows, cols, count, values, dense, tiles, block, listed, filled, in_sem, out_sem):
    slots = tiles.shape[0]
    load = pltpu.make_async_copy(values, tiles, in_sem)
    load.start()

    for g in range(BANDS):
        filled[g] = 0

    def enlist(t, carry):
        g = rows[t] // BAND_TILES
        at = filled[g]
        listed[g, at] = t
        filled[g] = at + 1
        return carry

    lax.fori_loop(0, jnp.minimum(count[0], slots), enlist, 0)

    def clear(i, carry):
        block[pl.ds(pl.multiple_of(i * 64, 64), 64), :] = jnp.zeros((64, COLS), BF16)
        return carry

    lax.fori_loop(0, block.shape[0] // 64, clear, 0)
    load.wait()

    def store(g):
        band = pl.ds(pl.multiple_of(g * BAND_TILES * TILE, BAND_TILES * TILE), BAND_TILES * TILE)
        return pltpu.make_async_copy(block.at[band], dense.at[band], out_sem.at[g])

    for g in range(BANDS):
        def place(i, carry):
            t = listed[g, i]
            row = pl.ds(pl.multiple_of(rows[t] * TILE, TILE), TILE)
            col = pl.ds(pl.multiple_of(cols[t] * TILE, TILE), TILE)
            block[row, col] = block[row, col] + tiles[t]
            return carry

        lax.fori_loop(0, filled[g], place, 0)
        store(g).start()
    for g in range(BANDS):
        store(g).wait()


def place_tiles(values, rows, cols, count):
    slots = values.shape[0]
    smem = pl.BlockSpec(memory_space=pltpu.SMEM)
    return pl.pallas_call(
        place_kernel,
        out_shape=jax.ShapeDtypeStruct((CHUNKS * NODES, COLS), BF16),
        in_specs=[smem, smem, smem, pl.BlockSpec(memory_space=pl.ANY)],
        out_specs=pl.BlockSpec(memory_space=pl.ANY),
        scratch_shapes=[
            pltpu.VMEM((slots, TILE, TILE), BF16),
            pltpu.VMEM((CHUNKS * NODES, COLS), BF16),
            pltpu.SMEM((BANDS, slots), jnp.int32),
            pltpu.SMEM((BANDS,), jnp.int32),
            pltpu.SemaphoreType.DMA,
            pltpu.SemaphoreType.DMA((BANDS,)),
        ],
        cost_estimate=pl.CostEstimate(flops=0, bytes_accessed=30 * 2**20, transcendentals=0),
        compiler_params=pltpu.CompilerParams(vmem_limit_bytes=PLACE_VMEM),
        name="place_tiles",
    )(rows, cols, count, values)


def dot(a, b):
    return jnp.dot(a, b, preferred_element_type=F32)


def split(v):
    high = v.astype(BF16)
    return high, (v - high.astype(F32)).astype(BF16)


def layer_kernel(
    features, features_across, weight_hbm, dense_hbm, output_grad_hbm, output_hbm, grad_features_hbm, grad_weight_hbm,
    dense, feats, weight, output_grad, output, grad_features, lifted,
    pairs_out, pairs_in, far_out, far_in, near_out, near_in, pairs2_out, pairs2_in, far2_out, far2_in, near2_out, near2_in, pair_out, pair_in,
    kept, grads, terms, col_out, col_in, col2_out, col2_in,
    wcore_out, wcore_in, wsum, wy_in, wgrid, wgrid_in, ggrid, wfull,
    load_sem, in_sem, out_sem, a_s, a_r, pairs_s, pairs_r, far_s, far_r, near_s, near_r, pairs2_s, pairs2_r, far2_s, far2_r, near2_s, near2_r,
    pair_s, pair_r, g_s, own_r, second_r, first_r, gfar_r, gpair_r, c_s, c_r, c2_s, c2_r, w_s, w_r,
):
    row, z, rep = lax.axis_index("row"), lax.axis_index("col"), lax.axis_index("rep")
    high, core = row // 2, row % 2
    x, low = rep // 2, rep % 2

    def at(high_=None, core_=None, z_=None, x_=None, low_=None):
        pick = lambda v, own: own if v is None else v
        return {
            "row": pick(high_, high) * 2 + pick(core_, core),
            "col": pick(z_, z),
            "rep": pick(x_, x) * 2 + pick(low_, low),
        }

    def along(axis, step):
        return at(x_=(x + step) % 4) if axis == "x" else at(z_=(z + step) % 4)

    def on_grid(s):
        return at(x_=(x + s // 4) % 4, z_=(z + s % 4) % 4)

    axes = (("x", "z"), ("z", "x"))
    spots = ((x, z), (z, x))
    steps = (3, 1)
    mine, other = low, 1 - low

    def chunk(p, first, second, pair_):
        if p == 0:
            return second * 8 + first * 2 + pair_
        return first * 8 + second * 2 + pair_

    def copy(src, dst, s, r, device):
        return pltpu.make_async_remote_copy(
            src_ref=src, dst_ref=dst, send_sem=s, recv_sem=r, device_id=device, device_id_type=MESH
        )

    cores, pair, across = at(core_=1 - core), at(low_=1 - low), at(high_=1 - high)
    ypeer = (pair, across, at(high_=1 - high, low_=1 - low))

    def loop(n, body):
        def step(i, carry):
            body(i)
            return carry

        lax.fori_loop(0, n, step, 0)

    def rows_of(r):
        return pl.ds(pl.multiple_of(r * NODES, NODES), NODES)

    def load(i, j, pair_):
        span = rows_of(chunk(0, (x + i) % 4, (z + j) % 4, pair_))
        sem = load_sem.at[i, j, 0 if pair_ is mine else 1]
        return pltpu.make_async_copy(dense_hbm.at[span], dense.at[span], sem)

    uses = [(2, 1, other)] + [(steps[d], 0, other) for d in range(2)] + [(2, 2, other)]
    uses += [(steps[d], o, other) for o in (2, 1) for d in range(2)] + [(2, 3, other), (2, 0, other), (2, 1, mine)]
    waiting = []
    for i, j, pair_ in uses + [(i, j, pair_) for pair_ in (other, mine) for i in range(4) for j in range(4)]:
        for key in ((i, j, pair_), (j, i, pair_)):
            if not any(key[:2] == k[:2] and key[2] is k[2] for k in waiting):
                waiting.append(key)
    loads = list(waiting)

    def need(p, i, j, pair_):
        for key in waiting:
            if key[:2] == ((i, j), (j, i))[p] and key[2] is pair_:
                load(*key).wait()
                waiting.remove(key)
                break

    def need_all():
        while waiting:
            load(*waiting.pop(0)).wait()

    row_across, row_core, row_last = (1 - high) * 2 + core, high * 2 + 1 - core, (1 - high) * 2 + 1 - core
    takes = (
        pltpu.make_async_copy(features, feats.at[rows_of(row)], in_sem.at[0]),
        pltpu.make_async_copy(features_across, feats.at[rows_of(row_across)], in_sem.at[1]),
        pltpu.make_async_copy(weight_hbm, weight, in_sem.at[2]),
        pltpu.make_async_copy(output_grad_hbm, output_grad, in_sem.at[3]),
    )
    takes[0].start()
    takes[1].start()
    for key in loads[:2]:
        load(*key).start()

    barrier = pltpu.get_barrier_semaphore()

    def greet(s):
        pl.semaphore_signal(barrier, inc=1, device_id=on_grid(s + 1), device_id_type=MESH)

    loop(15, greet)
    for device in (*ypeer, cores):
        pl.semaphore_signal(barrier, inc=1, device_id=device, device_id_type=MESH)
    pl.semaphore_wait(barrier, 19)

    def gather(i, r):
        return copy((features, features_across)[i], feats.at[rows_of(r)], a_s.at[i], a_r.at[i], cores)

    gather(0, row).start()
    gather(1, row_across).start()
    takes[0].wait()
    takes[1].wait()
    for key in loads[2:6]:
        load(*key).start()
    gather(0, row_core).wait_recv()
    gather(1, row_last).wait_recv()
    for key in loads[6:]:
        load(*key).start()
    takes[2].start()
    takes[3].start()

    def partial_at(p, i, j, pair_):
        need(p, i, j, pair_)
        return partial(p, (spots[p][0] + i) % 4, (spots[p][1] + j) % 4, pair_)

    def partial(p, first, second, pair_):
        start = pl.multiple_of(chunk(p, first, second, pair_) * NODES, NODES)
        return dot(dense[pl.ds(start, NODES), :], feats[:, p * HALF:(p + 1) * HALF])

    def pairs(p, o):
        return copy(pairs_out.at[p, o], pairs_in.at[p, o], pairs_s, pairs_r.at[p, o], pair)

    def far(p, o, d):
        half = pl.ds(d * TILE, TILE)
        return copy(far_out.at[p, o, half], far_in.at[p, o, d], far_s, far_r.at[p, o, d], along(axes[p][0], steps[d]))

    def near(p, o, r, d):
        return copy(near_out.at[p, o, r, d], near_in.at[p, o, r, d], near_s, near_r.at[p, o, r], along(axes[p][0], steps[d]))

    def near_both(p, o, r):
        return copy(near_out.at[p, o, r], near_in.at[p, o, r], near_s, near_r.at[p, o, r], pair)

    def send_other(p, o):
        for d in range(2):
            near_out[p, o, 1, d] = partial_at(p, steps[d], o, other).astype(BF16)
            near(p, o, 1, d).start()

    def send_pair(p, o):
        pairs_out[p, o] = partial_at(p, 2, o, other).astype(BF16)
        pairs(p, o).start()

    def send_far(p, o):
        value = partial_at(p, 2, o, mine)
        pairs(p, o).wait_recv()
        far_out[p, o] = (value + pairs_in[p, o].astype(F32)).astype(BF16)
        for d in range(2):
            far(p, o, d).start()

    def send_mine(p, o):
        for d in range(2):
            value = partial_at(p, steps[d], o, mine)
            far(p, o, d).wait_recv()
            half, rest = (slice(0, TILE), slice(TILE, NODES))[::1 - 2 * d]
            near_out[p, o, 0, d, half] = (value[half] + far_in[p, o, d].astype(F32)).astype(BF16)
            near_out[p, o, 0, d, rest] = value[rest].astype(BF16)
            near(p, o, 0, d).start()

    def pairs2(p):
        return copy(pairs2_out.at[p], pairs2_in.at[p], pairs2_s, pairs2_r.at[p], pair)

    def far2(p, d):
        half = pl.ds(d * TILE, TILE)
        return copy(far2_out.at[p, half], far2_in.at[p, d], far2_s, far2_r.at[p, d], along(axes[p][1], steps[d]))

    def near2(p, r, d):
        return copy(near2_out.at[p, r, d], near2_in.at[p, r, d], near2_s, near2_r.at[p, r], along(axes[p][1], steps[d]))

    def near2_both(p, r):
        return copy(near2_out.at[p, r], near2_in.at[p, r], near2_s, near2_r.at[p, r], pair)

    def first_sum(p, o, y):
        need_all()
        value = partial(p, spots[p][0], (spots[p][1] + o) % 4, y)
        r = 0 if y is mine else 1
        near_both(p, o, r).wait_recv()
        return value + near_in[p, o, r, 0].astype(F32) + near_in[p, o, r, 1].astype(F32)

    def send_pair2(p):
        pairs2_out[p] = first_sum(p, 2, other).astype(BF16)
        pairs2(p).start()

    def send_far2(p):
        value = first_sum(p, 2, mine)
        pairs2(p).wait_recv()
        far2_out[p] = (value + pairs2_in[p].astype(F32)).astype(BF16)
        for d in range(2):
            far2(p, d).start()

    def send_other2(p, d):
        near2_out[p, 1, d] = first_sum(p, steps[d], other).astype(BF16)
        near2(p, 1, d).start()

    def send_mine2(p, d):
        value = first_sum(p, steps[d], mine)
        far2(p, d).wait_recv()
        half, rest = (slice(0, TILE), slice(TILE, NODES))[::1 - 2 * d]
        near2_out[p, 0, d, half] = (value[half] + far2_in[p, d].astype(F32)).astype(BF16)
        near2_out[p, 0, d, rest] = value[rest].astype(BF16)
        near2(p, 0, d).start()

    def keep(p, y):
        kept[p, y] = first_sum(p, 0, y)

    def last_pair(p):
        return copy(pair_out.at[p], pair_in.at[p], pair_s, pair_r.at[p], pair)

    def second_sum(p, y):
        r = 0 if y is mine else 1
        near2_both(p, r).wait_recv()
        return kept[p, y] + near2_in[p, r, 0].astype(F32) + near2_in[p, r, 1].astype(F32)

    def send_last(p):
        pair_out[p] = second_sum(p, other).astype(BF16)
        last_pair(p).start()

    def keep_last(p):
        kept[p, mine] = second_sum(p, mine)

    for step in (
        (send_pair, 1), (send_other, 0), (send_pair, 2), (send_other, 2), (send_other, 1), (send_pair, 3), (send_pair, 0),
        (send_far, 1), (send_pair2,), (send_other, 3), (send_far, 2), (send_mine, 1), (send_mine, 2), (send_far, 3),
        (send_other2, 1), (send_other2, 0), (send_far, 0), (send_mine, 3), (keep, other), (send_far2,), (send_mine, 0),
        (send_last,), (send_mine2, 0), (send_mine2, 1), (keep, mine), (keep_last,),
    ):
        for p in range(2):
            step[0](p, *step[1:])

    takes[2].wait()
    takes[3].wait()
    v = jnp.zeros((NODES, WIDTH), F32)
    for p in range(2):
        last_pair(p).wait_recv()
        span = slice(p * HALF, (p + 1) * HALF)
        for i, part in enumerate(split(kept[p, mine] + pair_in[p].astype(F32))):
            lifted[i, :, span] = part
            v = v + dot(part, weight[span, :])
    t = jnp.tanh(C0 * (v + 0.044715 * (v * v * v)))
    slope = 0.5 * (1.0 + t) + 0.5 * v * (1.0 - t * t) * (C0 * (1.0 + 3.0 * 0.044715 * (v * v)))
    grad = (output_grad[...].astype(F32) * slope).astype(BF16).astype(F32)

    def own(p, y):
        return copy(grads.at[p, 0, 0, y], grads.at[p, 0, 0, y], g_s.at[0], own_r.at[p], pair)

    def second(p, j, y):
        step, src = {1: (3, 0), 2: (3 - 2 * y, 1 + 2 * y), 3: (1, 0)}[j]
        return copy(
            grads.at[p, 0, src, y], grads.at[p, 0, j, y], g_s.at[2 if j == 2 else 1], second_r.at[p, j - 1, y],
            along(axes[p][1], step),
        )

    def first(p, i, j, y):
        return copy(
            grads.at[p, 0, j, y], grads.at[p, i, j, y], g_s.at[3], first_r.at[p, i // 2, j, y],
            along(axes[p][0], 3 if i == 1 else 1),
        )

    def onward(p, j, d):
        half = pl.ds(d * TILE, TILE)
        return copy(
            grads.at[p, 1 + 2 * d, j, mine, half], grads.at[p, 2, j, mine, half], g_s.at[4], gfar_r.at[p, j],
            along(axes[p][0], steps[d]),
        )

    def onward_both(p, j):
        return copy(grads.at[p, 2, j, mine], grads.at[p, 2, j, mine], g_s.at[4], gfar_r.at[p, j], pair)

    def far_pair(p, j, y):
        return copy(grads.at[p, 2, j, y], grads.at[p, 2, j, y], g_s.at[5], gpair_r.at[p, j], pair)

    def give_first(p, j, y):
        first(p, 1, j, y).start()
        first(p, 3, j, y).start()

    def give_second(p, y):
        second(p, 1, y).start()
        second(p, 3, y).start()

    for p in range(2):
        grads[p, 0, 0, mine] = grad[:, p * HALF:(p + 1) * HALF].T.astype(BF16)
    def weight_half(p):
        block = grads[p, 0, 0, mine]
        return dot(block, lifted[0]) + dot(block, lifted[1])

    spot = x * 4 + z
    y = high * 2 + low
    yspot = (high * 2 + other, (1 - high) * 2 + low, (1 - high) * 2 + other)
    weight_core = copy(wcore_out, wcore_in, w_s.at[0], w_r.at[0], cores)

    def weight_y(s):
        return copy(wsum.at[yspot[s]], wy_in.at[s], w_s.at[1], w_r.at[1], ypeer[s])

    def weight_grid(s):
        part = ((x + s // 4) % 4) * 4 + (z + s % 4) % 4
        return copy(wgrid.at[part], wgrid_in.at[s], w_s.at[2], w_r.at[2], on_grid(s))

    def gather_grid(s):
        return copy(ggrid.at[spot], ggrid.at[spot], w_s.at[3], w_r.at[3], on_grid(s))

    def gather_y(s):
        return copy(wfull.at[core, y], wfull.at[core, y], w_s.at[4], w_r.at[4], ypeer[s])

    def gather_core(half):
        return copy(wfull.at[half], wfull.at[half], w_s.at[5], w_r.at[5], cores)

    weight_all = (
        weight_core,
        copy(wsum.at[pl.ds(0, 3)], wy_in, w_s.at[1], w_r.at[1], cores),
        copy(wgrid.at[pl.ds(1, 15)], wgrid_in.at[pl.ds(1, 15)], w_s.at[2], w_r.at[2], cores),
        copy(ggrid.at[pl.ds(1, 15)], ggrid.at[pl.ds(1, 15)], w_s.at[3], w_r.at[3], cores),
        copy(wfull.at[0, pl.ds(0, 3)], wfull.at[0, pl.ds(0, 3)], w_s.at[4], w_r.at[4], cores),
        gather_core(1 - core),
    )

    def weight_step(k):
        if k > 0:
            weight_all[k - 1].wait_recv()
        if k == 0:
            wcore_out[...] = weight_half(1 - core)
            weight_core.start()
            wsum[...] = weight_half(core).reshape(4, 64, WIDTH)
        elif k == 1:
            wsum[...] = wsum[...] + wcore_in[...].reshape(4, 64, WIDTH)
            for s in range(3):
                weight_y(s).start()
        elif k == 2:
            total = wsum[y]
            for s in range(3):
                total = total + wy_in[s]
            for s in range(16):
                i, j = s // 4, s % 4
                wgrid[s] = total[i * 16:(i + 1) * 16, j * TILE:(j + 1) * TILE]
            loop(15, lambda s: weight_grid(s + 1).start())
        elif k == 3:
            total = wgrid[spot]
            for s in range(1, 16):
                total = total + wgrid_in[s]
            ggrid[spot] = total.astype(BF16)
            loop(15, lambda s: gather_grid(s + 1).start())
        elif k == 4:
            for s in range(16):
                i, j = s // 4, s % 4
                wfull[core, y, i * 16:(i + 1) * 16, j * TILE:(j + 1) * TILE] = ggrid[s]
            for s in range(3):
                gather_y(s).start()
        elif k == 5:
            gather_core(core).start()
        else:
            gives[1].start()

    def product(p, i, j):
        total = None
        for y_ in range(2):
            start = chunk(p, (spots[p][0] + i) % 4, (spots[p][1] + j) % 4, y_) * NODES
            term = dot(grads[p, i, j, y_], dense[pl.ds(pl.multiple_of(start, NODES), NODES), :])
            total = term if total is None else total + term
        return total

    begun = set()

    def add(p, i, j):
        total, fresh = product(p, i, j), p not in begun
        begun.add(p)
        for r in range(PEERS):
            part = total[:, r * NODES:(r + 1) * NODES]
            terms[p, r] = part if fresh else terms[p, r] + part

    def pass_on(p, j):
        for d in range(2):
            first(p, 1 + 2 * d, j, mine).wait_recv()
            onward(p, j, d).start()

    def pass_pair(p, j):
        onward_both(p, j).wait_recv()
        far_pair(p, j, mine).start()

    def use_first(p, j):
        for i in (1, 3):
            first(p, i, j, other).wait_recv()
            add(p, i, j)

    def use_far(p, j):
        far_pair(p, j, other).wait_recv()
        add(p, 2, j)

    gives = (
        pltpu.make_async_copy(output, output_hbm, out_sem.at[0]),
        pltpu.make_async_copy(wfull, grad_weight_hbm, out_sem.at[1]),
        pltpu.make_async_copy(grad_features, grad_features_hbm, out_sem.at[2]),
    )

    def give_output():
        output[...] = (0.5 * v * (1.0 + t)).astype(BF16)
        gives[0].start()

    def give_own():
        for p in range(2):
            own(p, mine).start()

    def take_own(p):
        own(p, other).wait_recv()

    def give_firsts(p, j, y_):
        give_first(p, j, y_)

    def take_second(p, y_):
        second(p, 1, y_).wait_recv()
        second(p, 3, y_).wait_recv()
        second(p, 2, y_).start()

    def take_second2(p, y_):
        second(p, 2, y_).wait_recv()

    def use_own(p, j):
        add(p, 0, j)

    def cols1(p, h):
        return copy(col_out.at[p, h], col_in.at[p, h], c_s, c_r.at[p, h], cores)

    def cols2(p):
        return copy(col2_out.at[p], col2_in.at[p], c2_s, c2_r.at[p], across)

    def give_cols(p):
        for h in (1 - high, high):
            col_out[p, h] = terms[p, 2 * h + 1 - core].astype(BF16)
            cols1(p, h).start()

    def pass_cols(p):
        cols1(p, 1 - high).wait_recv()
        col2_out[p] = (terms[p, row_across] + col_in[p, 1 - high].astype(F32)).astype(BF16)
        cols2(p).start()

    for step in (
        (give_second, 0, mine), (give_second, 1, mine), (give_firsts, 1, 0, mine), (give_own,), (give_output,), (weight_step, 0),
        (give_firsts, 0, 0, mine), (take_own, 0), (take_second, 1, mine), (give_firsts, 1, 3, mine), (take_own, 1),
        (give_second, 1, other), (pass_on, 1, 0), (use_own, 0, 0), (pass_on, 0, 0), (give_second, 0, other),
        (give_firsts, 1, 1, mine), (take_second, 0, mine), (take_second2, 1, mine), (weight_step, 1),
        (give_firsts, 1, 2, mine), (pass_on, 1, 3), (give_firsts, 0, 1, mine), (pass_pair, 1, 0), (take_second, 1, other),
        (take_second, 0, other), (use_own, 1, 1), (use_own, 0, 1), (give_firsts, 0, 3, mine), (take_second2, 1, other),
        (pass_on, 0, 1), (pass_pair, 0, 0), (use_own, 1, 3), (take_second2, 0, mine), (pass_on, 0, 3), (weight_step, 2),
        (pass_on, 1, 1), (pass_pair, 0, 1), (give_firsts, 0, 2, mine), (pass_pair, 0, 3), (give_firsts, 1, 2, other),
        (pass_on, 1, 2), (pass_pair, 1, 3), (take_second2, 0, other), (pass_pair, 1, 1), (give_firsts, 0, 1, other),
        (give_firsts, 0, 3, other), (weight_step, 3), (use_own, 0, 3), (give_firsts, 1, 1, other), (pass_pair, 1, 2),
        (use_far, 1, 0), (give_firsts, 1, 3, other), (pass_on, 0, 2), (use_far, 0, 0), (use_far, 1, 3),
        (give_firsts, 0, 0, other), (give_firsts, 0, 2, other), (use_own, 1, 0), (use_first, 0, 1), (use_far, 0, 3),
        (give_firsts, 1, 0, other), (use_far, 0, 1), (use_far, 1, 1), (use_first, 1, 1), (pass_pair, 0, 2), (use_first, 1, 2),
        (use_first, 0, 3), (use_first, 1, 3), (weight_step, 4), (use_far, 1, 2), (use_own, 1, 2), (use_first, 0, 0),
        (use_first, 1, 0), (give_cols, 1), (use_own, 0, 2), (use_far, 0, 2), (use_first, 0, 2), (pass_cols, 1),
        (give_cols, 0), (pass_cols, 0), (weight_step, 5), (weight_step, 6),
    ):
        step[0](*step[1:])

    def sent(ref, sem):
        copy(ref, ref, sem, sem, pair).wait_send()

    for i, r in ((0, row), (1, row_across)):
        gather(i, r).wait_send()
    sent(pairs_out, pairs_s)
    sent(far_out, far_s)
    sent(near_out, near_s)
    sent(pairs2_out, pairs2_s)
    sent(far2_out, far2_s)
    sent(near2_out, near2_s)
    sent(pair_out, pair_s)
    sent(grads.at[0, 0, 0], g_s.at[0])
    sent(grads.at[0, 0], g_s.at[1])
    sent(grads.at[0, 0, pl.ds(0, 2)], g_s.at[2])
    sent(grads.at[0], g_s.at[3])
    sent(grads.at[0, 0], g_s.at[4])
    sent(grads.at[0, 0], g_s.at[5])
    for step in weight_all:
        step.wait_send()

    contract = (((1,), (1,)), ((), ()))
    total = jnp.zeros((NODES, WIDTH), F32)
    for p in (1, 0):
        cols1(p, high).wait_recv()
        cols2(p).wait_recv()
        value = (terms[p, row] + col_in[p, high].astype(F32) + col2_in[p].astype(F32)).T
        for part in split(value):
            total = total + lax.dot_general(
                part, weight[:, p * HALF:(p + 1) * HALF], contract, preferred_element_type=F32
            )
    grad_features[...] = total.astype(BF16)
    gives[2].start()
    sent(col_out, c_s)
    sent(col2_out, c2_s)
    for give in gives:
        give.wait()


def layer(features, features_across, weight, dense, output_grad):
    anywhere = pl.BlockSpec(memory_space=pl.ANY)
    dma = pltpu.SemaphoreType.DMA
    block = (NODES, HALF)
    bf = lambda *shape: pltpu.VMEM(shape, BF16)
    f32 = lambda *shape: pltpu.VMEM(shape, F32)
    return pl.pallas_call(
        layer_kernel,
        out_shape=(
            jax.ShapeDtypeStruct((NODES, WIDTH), BF16),
            jax.ShapeDtypeStruct((NODES, WIDTH), BF16),
            jax.ShapeDtypeStruct((2, 4, 64, WIDTH), BF16),
        ),
        in_specs=[anywhere] * 5,
        out_specs=(anywhere,) * 3,
        scratch_shapes=[
            bf(CHUNKS * NODES, COLS),
            bf(COLS, WIDTH),
            bf(WIDTH, WIDTH),
            bf(NODES, WIDTH),
            bf(NODES, WIDTH),
            bf(NODES, WIDTH),
            bf(2, NODES, WIDTH),
            bf(2, 4, *block), bf(2, 4, *block),
            bf(2, 4, *block), bf(2, 4, 2, TILE, HALF),
            bf(2, 4, 2, 2, *block), bf(2, 4, 2, 2, *block),
            bf(2, *block), bf(2, *block),
            bf(2, *block), bf(2, 2, TILE, HALF),
            bf(2, 2, 2, *block), bf(2, 2, 2, *block),
            bf(2, *block), bf(2, *block),
            f32(2, 2, *block),
            bf(2, 4, 4, 2, HALF, NODES),
            f32(2, PEERS, HALF, NODES),
            bf(2, 2, HALF, NODES), bf(2, 2, HALF, NODES),
            bf(2, HALF, NODES), bf(2, HALF, NODES),
            f32(HALF, WIDTH), f32(HALF, WIDTH),
            f32(4, 64, WIDTH),
            f32(3, 64, WIDTH),
            f32(16, 16, TILE), f32(16, 16, TILE),
            bf(16, 16, TILE),
            bf(2, 4, 64, WIDTH),
            dma((4, 4, 2)), dma((4,)), dma((3,)),
            dma((2,)), dma((2,)),
            dma, dma((2, 4)),
            dma, dma((2, 4, 2)),
            dma, dma((2, 4, 2)),
            dma, dma((2,)),
            dma, dma((2, 2)),
            dma, dma((2, 2)),
            dma, dma((2,)),
            dma((6,)), dma((2,)), dma((2, 3, 2)), dma((2, 2, 4, 2)), dma((2, 4)), dma((2, 4)),
            dma, dma((2, 2)),
            dma, dma((2,)),
            dma((6,)), dma((6,)),
        ],
        compiler_params=pltpu.CompilerParams(
            collective_id=0, has_side_effects=True, vmem_limit_bytes=LAYER_VMEM
        ),
        name="layer",
    )(features, features_across, weight, dense, output_grad)


def finish_kernel(first_in, second_in, weight_in, first, second, weight, first_at, second_at, weight_at, turned, in_sem, out_sem):
    loads = [
        pltpu.make_async_copy(src, dst, in_sem.at[i])
        for i, (src, dst) in enumerate(((weight_in, weight_at), (first_in, first_at), (second_in, second_at)))
    ]
    stores = [
        pltpu.make_async_copy(src, dst, out_sem.at[i])
        for i, (src, dst) in enumerate(((turned, weight), (first_at, first), (second_at, second)))
    ]
    for load in loads:
        load.start()
    loads[0].wait()
    turned[...] = weight_at[...].astype(F32).T
    stores[0].start()
    for load, store in zip(loads[1:], stores[1:]):
        load.wait()
        store.start()
    for store in stores:
        store.wait()


def finish(output, grad_features, grad_weight):
    anywhere = pl.BlockSpec(memory_space=pl.ANY)
    return pl.pallas_call(
        finish_kernel,
        out_shape=(
            jax.ShapeDtypeStruct(output.shape, BF16),
            jax.ShapeDtypeStruct(grad_features.shape, BF16),
            jax.ShapeDtypeStruct(grad_weight.shape, F32),
        ),
        in_specs=[anywhere] * 3,
        out_specs=(anywhere,) * 3,
        scratch_shapes=[
            pltpu.VMEM(output.shape, BF16),
            pltpu.VMEM(grad_features.shape, BF16),
            pltpu.VMEM(grad_weight.shape, BF16),
            pltpu.VMEM(grad_weight.shape, F32),
            pltpu.SemaphoreType.DMA((3,)),
            pltpu.SemaphoreType.DMA((3,)),
        ],
        compiler_params=pltpu.CompilerParams(vmem_limit_bytes=FINISH_VMEM),
        name="finish",
    )(output, grad_features, grad_weight)


def per_device(features, weight, tile_values, tile_rows, tile_cols, tile_count, output_grad):
    features_across = lax.ppermute(features, "row", [(r, (r + 2) % PEERS) for r in range(PEERS)])
    dense = place_tiles(tile_values, tile_rows, tile_cols, tile_count)
    output, grad_features, grad_weight = layer(features, features_across, weight, dense, output_grad)
    return finish(output, grad_features, grad_weight.reshape(WIDTH, WIDTH))


def solution(mesh):
    spread = P(("row", "col", "rep"))
    return jax.shard_map(
        per_device,
        mesh=mesh,
        in_specs=(
            P(("row", "col", "rep"), None),
            P(),
            P(("row", "col", "rep"), None, None),
            spread,
            spread,
            spread,
            P(("row", "col", "rep"), None),
        ),
        out_specs=(P(("row", "col", "rep"), None), P(("row", "col", "rep"), None), P()),
        check_vma=False,
    )
```

```python
import math

import jax
import jax.numpy as jnp
from jax import lax
from jax.experimental import pallas as pl
from jax.experimental.pallas import tpu as pltpu
from jax.sharding import PartitionSpec as P

MESH = pl.DeviceIdType.MESH
F32, BF16 = jnp.float32, jnp.bfloat16
TILE = 128
NODES = 256
HALF = 256
WIDTH = 512
PEERS = 4
CHUNKS = 32
COLS = 1024
BANDS = 8
BAND_TILES = 8
PLACE_VMEM, LAYER_VMEM, FINISH_VMEM = 63 * 2**20, 62 * 2**20, 63 * 2**20
C0 = math.sqrt(2.0 / math.pi)


def place_kernel(rows, cols, count, values, dense, tiles, block, listed, filled, in_sem, out_sem):
    slots = tiles.shape[0]
    load = pltpu.make_async_copy(values, tiles, in_sem)
    load.start()

    for g in range(BANDS):
        filled[g] = 0

    def enlist(t, carry):
        g = rows[t] // BAND_TILES
        at = filled[g]
        listed[g, at] = t
        filled[g] = at + 1
        return carry

    lax.fori_loop(0, jnp.minimum(count[0], slots), enlist, 0)

    def clear(i, carry):
        block[pl.ds(pl.multiple_of(i * 64, 64), 64), :] = jnp.zeros((64, COLS), BF16)
        return carry

    lax.fori_loop(0, block.shape[0] // 64, clear, 0)
    load.wait()

    def store(g):
        band = pl.ds(pl.multiple_of(g * BAND_TILES * TILE, BAND_TILES * TILE), BAND_TILES * TILE)
        return pltpu.make_async_copy(block.at[band], dense.at[band], out_sem.at[g])

    def spot_of(t):
        row = pl.multiple_of(rows[t] * TILE, TILE)
        col = pl.multiple_of(cols[t] * TILE, TILE)
        return row, col, (pl.ds(row, TILE), pl.ds(col, TILE))

    for g in range(BANDS):
        def place_two(i, carry):
            t, u = listed[g, 2 * i], listed[g, 2 * i + 1]
            row_t, col_t, at_t = spot_of(t)
            row_u, col_u, at_u = spot_of(u)
            first, second = block[at_t] + tiles[t], block[at_u]
            second = jnp.where((row_t == row_u) & (col_t == col_u), first, second) + tiles[u]
            block[at_t] = first
            block[at_u] = second
            return carry

        def place_last(i, carry):
            t = listed[g, filled[g] - 1]
            at_t = spot_of(t)[2]
            block[at_t] = block[at_t] + tiles[t]
            return carry

        lax.fori_loop(0, filled[g] // 2, place_two, 0)
        lax.fori_loop(0, filled[g] % 2, place_last, 0)
        store(g).start()
    for g in range(BANDS):
        store(g).wait()


def place_tiles(values, rows, cols, count):
    slots = values.shape[0]
    smem = pl.BlockSpec(memory_space=pltpu.SMEM)
    return pl.pallas_call(
        place_kernel,
        out_shape=jax.ShapeDtypeStruct((CHUNKS * NODES, COLS), BF16),
        in_specs=[smem, smem, smem, pl.BlockSpec(memory_space=pl.ANY)],
        out_specs=pl.BlockSpec(memory_space=pl.ANY),
        scratch_shapes=[
            pltpu.VMEM((slots, TILE, TILE), BF16),
            pltpu.VMEM((CHUNKS * NODES, COLS), BF16),
            pltpu.SMEM((BANDS, slots), jnp.int32),
            pltpu.SMEM((BANDS,), jnp.int32),
            pltpu.SemaphoreType.DMA,
            pltpu.SemaphoreType.DMA((BANDS,)),
        ],
        cost_estimate=pl.CostEstimate(flops=0, bytes_accessed=30 * 2**20, transcendentals=0),
        compiler_params=pltpu.CompilerParams(vmem_limit_bytes=PLACE_VMEM),
        name="place_tiles",
    )(rows, cols, count, values)


def dot(a, b):
    return jnp.dot(a, b, preferred_element_type=F32)


def split(v):
    high = v.astype(BF16)
    return high, (v - high.astype(F32)).astype(BF16)


def layer_kernel(
    features, features_across, weight_hbm, dense_hbm, output_grad_hbm, output_hbm, grad_features_hbm, grad_weight_hbm,
    dense, feats, weight, output_grad, output, grad_features, lifted,
    pairs_out, pairs_in, far_out, far_in, near_out, near_in, pairs2_out, pairs2_in, far2_out, far2_in, near2_out, near2_in, pair_out, pair_in,
    kept, grads, terms, col_out, col_in, col2_out, col2_in,
    wcore_out, wcore_in, wsum, wy_in, wgrid, wgrid_in, ggrid, wfull,
    load_sem, in_sem, out_sem, a_s, a_r, pairs_s, pairs_r, far_s, far_r, near_s, near_r, pairs2_s, pairs2_r, far2_s, far2_r, near2_s, near2_r,
    pair_s, pair_r, g_s, own_r, second_r, first_r, gfar_r, gpair_r, c_s, c_r, c2_s, c2_r, w_s, w_r,
):
    row, z, rep = lax.axis_index("row"), lax.axis_index("col"), lax.axis_index("rep")
    high, core = row // 2, row % 2
    x, low = rep // 2, rep % 2

    def at(high_=None, core_=None, z_=None, x_=None, low_=None):
        pick = lambda v, own: own if v is None else v
        return {
            "row": pick(high_, high) * 2 + pick(core_, core),
            "col": pick(z_, z),
            "rep": pick(x_, x) * 2 + pick(low_, low),
        }

    def along(axis, step):
        return at(x_=(x + step) % 4) if axis == "x" else at(z_=(z + step) % 4)

    def on_grid(s):
        return at(x_=(x + s // 4) % 4, z_=(z + s % 4) % 4)

    axes = (("x", "z"), ("z", "x"))
    spots = ((x, z), (z, x))
    steps = (3, 1)
    mine, other = low, 1 - low

    def chunk(p, first, second, pair_):
        if p == 0:
            return second * 8 + first * 2 + pair_
        return first * 8 + second * 2 + pair_

    def copy(src, dst, s, r, device):
        return pltpu.make_async_remote_copy(
            src_ref=src, dst_ref=dst, send_sem=s, recv_sem=r, device_id=device, device_id_type=MESH
        )

    cores, pair, across = at(core_=1 - core), at(low_=1 - low), at(high_=1 - high)
    ypeer = (pair, across, at(high_=1 - high, low_=1 - low))

    def loop(n, body):
        def step(i, carry):
            body(i)
            return carry

        lax.fori_loop(0, n, step, 0)

    def rows_of(r):
        return pl.ds(pl.multiple_of(r * NODES, NODES), NODES)

    def load(i, j, pair_):
        span = rows_of(chunk(0, (x + i) % 4, (z + j) % 4, pair_))
        sem = load_sem.at[i, j, 0 if pair_ is mine else 1]
        return pltpu.make_async_copy(dense_hbm.at[span], dense.at[span], sem)

    uses = [(2, 1, other)] + [(steps[d], 0, other) for d in range(2)] + [(2, 2, other)]
    uses += [(steps[d], o, other) for o in (2, 1) for d in range(2)] + [(2, 3, other), (2, 0, other), (2, 1, mine)]
    waiting = []
    for i, j, pair_ in uses + [(i, j, pair_) for pair_ in (other, mine) for i in range(4) for j in range(4)]:
        for key in ((i, j, pair_), (j, i, pair_)):
            if not any(key[:2] == k[:2] and key[2] is k[2] for k in waiting):
                waiting.append(key)
    loads = list(waiting)

    def need(p, i, j, pair_):
        for key in waiting:
            if key[:2] == ((i, j), (j, i))[p] and key[2] is pair_:
                load(*key).wait()
                waiting.remove(key)
                break

    def need_all():
        while waiting:
            load(*waiting.pop(0)).wait()

    row_across, row_core, row_last = (1 - high) * 2 + core, high * 2 + 1 - core, (1 - high) * 2 + 1 - core
    takes = (
        pltpu.make_async_copy(features, feats.at[rows_of(row)], in_sem.at[0]),
        pltpu.make_async_copy(features_across, feats.at[rows_of(row_across)], in_sem.at[1]),
        pltpu.make_async_copy(weight_hbm, weight, in_sem.at[2]),
        pltpu.make_async_copy(output_grad_hbm, output_grad, in_sem.at[3]),
    )
    takes[0].start()
    takes[1].start()
    for key in loads[:2]:
        load(*key).start()

    barrier = pltpu.get_barrier_semaphore()

    def greet(s):
        pl.semaphore_signal(barrier, inc=1, device_id=on_grid(s + 1), device_id_type=MESH)

    loop(15, greet)
    for device in (*ypeer, cores):
        pl.semaphore_signal(barrier, inc=1, device_id=device, device_id_type=MESH)
    pl.semaphore_wait(barrier, 19)

    def gather(i, r):
        return copy((features, features_across)[i], feats.at[rows_of(r)], a_s.at[i], a_r.at[i], cores)

    gather(0, row).start()
    gather(1, row_across).start()
    takes[0].wait()
    takes[1].wait()
    for key in loads[2:6]:
        load(*key).start()
    gather(0, row_core).wait_recv()
    gather(1, row_last).wait_recv()
    for key in loads[6:]:
        load(*key).start()
    takes[2].start()
    takes[3].start()

    def partial_at(p, i, j, pair_):
        need(p, i, j, pair_)
        return partial(p, (spots[p][0] + i) % 4, (spots[p][1] + j) % 4, pair_)

    def partial(p, first, second, pair_):
        start = pl.multiple_of(chunk(p, first, second, pair_) * NODES, NODES)
        return dot(dense[pl.ds(start, NODES), :], feats[:, p * HALF:(p + 1) * HALF])

    def pairs(p, o):
        return copy(pairs_out.at[p, o], pairs_in.at[p, o], pairs_s, pairs_r.at[p, o], pair)

    def far(p, o, d):
        half = pl.ds(d * TILE, TILE)
        return copy(far_out.at[p, o, half], far_in.at[p, o, d], far_s, far_r.at[p, o, d], along(axes[p][0], steps[d]))

    def near(p, o, r, d):
        return copy(near_out.at[p, o, r, d], near_in.at[p, o, r, d], near_s, near_r.at[p, o, r], along(axes[p][0], steps[d]))

    def near_both(p, o, r):
        return copy(near_out.at[p, o, r], near_in.at[p, o, r], near_s, near_r.at[p, o, r], pair)

    def send_other(p, o):
        for d in range(2):
            near_out[p, o, 1, d] = partial_at(p, steps[d], o, other).astype(BF16)
            near(p, o, 1, d).start()

    def send_pair(p, o):
        pairs_out[p, o] = partial_at(p, 2, o, other).astype(BF16)
        pairs(p, o).start()

    def send_far(p, o):
        value = partial_at(p, 2, o, mine)
        pairs(p, o).wait_recv()
        far_out[p, o] = (value + pairs_in[p, o].astype(F32)).astype(BF16)
        for d in range(2):
            far(p, o, d).start()

    def send_mine(p, o):
        for d in range(2):
            value = partial_at(p, steps[d], o, mine)
            far(p, o, d).wait_recv()
            half, rest = (slice(0, TILE), slice(TILE, NODES))[::1 - 2 * d]
            near_out[p, o, 0, d, half] = (value[half] + far_in[p, o, d].astype(F32)).astype(BF16)
            near_out[p, o, 0, d, rest] = value[rest].astype(BF16)
            near(p, o, 0, d).start()

    def pairs2(p):
        return copy(pairs2_out.at[p], pairs2_in.at[p], pairs2_s, pairs2_r.at[p], pair)

    def far2(p, d):
        half = pl.ds(d * TILE, TILE)
        return copy(far2_out.at[p, half], far2_in.at[p, d], far2_s, far2_r.at[p, d], along(axes[p][1], steps[d]))

    def near2(p, r, d):
        return copy(near2_out.at[p, r, d], near2_in.at[p, r, d], near2_s, near2_r.at[p, r], along(axes[p][1], steps[d]))

    def near2_both(p, r):
        return copy(near2_out.at[p, r], near2_in.at[p, r], near2_s, near2_r.at[p, r], pair)

    def first_sum(p, o, y):
        need_all()
        value = partial(p, spots[p][0], (spots[p][1] + o) % 4, y)
        r = 0 if y is mine else 1
        near_both(p, o, r).wait_recv()
        return value + near_in[p, o, r, 0].astype(F32) + near_in[p, o, r, 1].astype(F32)

    def send_pair2(p):
        pairs2_out[p] = first_sum(p, 2, other).astype(BF16)
        pairs2(p).start()

    def send_far2(p):
        value = first_sum(p, 2, mine)
        pairs2(p).wait_recv()
        far2_out[p] = (value + pairs2_in[p].astype(F32)).astype(BF16)
        for d in range(2):
            far2(p, d).start()

    def send_other2(p, d):
        near2_out[p, 1, d] = first_sum(p, steps[d], other).astype(BF16)
        near2(p, 1, d).start()

    def send_mine2(p, d):
        value = first_sum(p, steps[d], mine)
        far2(p, d).wait_recv()
        half, rest = (slice(0, TILE), slice(TILE, NODES))[::1 - 2 * d]
        near2_out[p, 0, d, half] = (value[half] + far2_in[p, d].astype(F32)).astype(BF16)
        near2_out[p, 0, d, rest] = value[rest].astype(BF16)
        near2(p, 0, d).start()

    def keep(p, y):
        kept[p, y] = first_sum(p, 0, y)

    def last_pair(p):
        return copy(pair_out.at[p], pair_in.at[p], pair_s, pair_r.at[p], pair)

    def second_sum(p, y):
        r = 0 if y is mine else 1
        near2_both(p, r).wait_recv()
        return kept[p, y] + near2_in[p, r, 0].astype(F32) + near2_in[p, r, 1].astype(F32)

    def send_last(p):
        pair_out[p] = second_sum(p, other).astype(BF16)
        last_pair(p).start()

    def keep_last(p):
        kept[p, mine] = second_sum(p, mine)

    for step in (
        (send_pair, 1), (send_other, 0), (send_pair, 2), (send_other, 2), (send_other, 1), (send_pair, 3), (send_pair, 0),
        (send_far, 1), (send_pair2,), (send_other, 3), (send_far, 2), (send_mine, 1), (send_mine, 2), (send_far, 3),
        (send_other2, 1), (send_other2, 0), (send_far, 0), (send_mine, 3), (keep, other), (send_far2,), (send_mine, 0),
        (send_last,), (send_mine2, 0), (send_mine2, 1), (keep, mine), (keep_last,),
    ):
        for p in range(2):
            step[0](p, *step[1:])

    takes[2].wait()
    takes[3].wait()
    v = jnp.zeros((NODES, WIDTH), F32)
    for p in range(2):
        last_pair(p).wait_recv()
        span = slice(p * HALF, (p + 1) * HALF)
        for i, part in enumerate(split(kept[p, mine] + pair_in[p].astype(F32))):
            lifted[i, :, span] = part
            v = v + dot(part, weight[span, :])
    t = jnp.tanh(C0 * (v + 0.044715 * (v * v * v)))
    slope = 0.5 * (1.0 + t) + 0.5 * v * (1.0 - t * t) * (C0 * (1.0 + 3.0 * 0.044715 * (v * v)))
    grad = (output_grad[...].astype(F32) * slope).astype(BF16).astype(F32)

    def own(p, y):
        return copy(grads.at[p, 0, 0, y], grads.at[p, 0, 0, y], g_s.at[0], own_r.at[p], pair)

    def second(p, j, y):
        step, src = {1: (3, 0), 2: (3 - 2 * y, 1 + 2 * y), 3: (1, 0)}[j]
        return copy(
            grads.at[p, 0, src, y], grads.at[p, 0, j, y], g_s.at[2 if j == 2 else 1], second_r.at[p, j - 1, y],
            along(axes[p][1], step),
        )

    def first(p, i, j, y):
        return copy(
            grads.at[p, 0, j, y], grads.at[p, i, j, y], g_s.at[3], first_r.at[p, i // 2, j, y],
            along(axes[p][0], 3 if i == 1 else 1),
        )

    def onward(p, j, d):
        half = pl.ds(d * TILE, TILE)
        return copy(
            grads.at[p, 1 + 2 * d, j, mine, half], grads.at[p, 2, j, mine, half], g_s.at[4], gfar_r.at[p, j],
            along(axes[p][0], steps[d]),
        )

    def onward_both(p, j):
        return copy(grads.at[p, 2, j, mine], grads.at[p, 2, j, mine], g_s.at[4], gfar_r.at[p, j], pair)

    def far_pair(p, j, y):
        return copy(grads.at[p, 2, j, y], grads.at[p, 2, j, y], g_s.at[5], gpair_r.at[p, j], pair)

    def give_first(p, j, y):
        first(p, 1, j, y).start()
        first(p, 3, j, y).start()

    def give_second(p, y):
        second(p, 1, y).start()
        second(p, 3, y).start()

    for p in range(2):
        grads[p, 0, 0, mine] = grad[:, p * HALF:(p + 1) * HALF].T.astype(BF16)
    def weight_half(p):
        block = grads[p, 0, 0, mine]
        return dot(block, lifted[0]) + dot(block, lifted[1])

    spot = x * 4 + z
    y = high * 2 + low
    yspot = (high * 2 + other, (1 - high) * 2 + low, (1 - high) * 2 + other)
    weight_core = copy(wcore_out, wcore_in, w_s.at[0], w_r.at[0], cores)

    def weight_y(s):
        return copy(wsum.at[yspot[s]], wy_in.at[s], w_s.at[1], w_r.at[1], ypeer[s])

    def weight_grid(s):
        part = ((x + s // 4) % 4) * 4 + (z + s % 4) % 4
        return copy(wgrid.at[part], wgrid_in.at[s], w_s.at[2], w_r.at[2], on_grid(s))

    def gather_grid(s):
        return copy(ggrid.at[spot], ggrid.at[spot], w_s.at[3], w_r.at[3], on_grid(s))

    def gather_y(s):
        return copy(wfull.at[core, y], wfull.at[core, y], w_s.at[4], w_r.at[4], ypeer[s])

    def gather_core(half):
        return copy(wfull.at[half], wfull.at[half], w_s.at[5], w_r.at[5], cores)

    weight_all = (
        weight_core,
        copy(wsum.at[pl.ds(0, 3)], wy_in, w_s.at[1], w_r.at[1], cores),
        copy(wgrid.at[pl.ds(1, 15)], wgrid_in.at[pl.ds(1, 15)], w_s.at[2], w_r.at[2], cores),
        copy(ggrid.at[pl.ds(1, 15)], ggrid.at[pl.ds(1, 15)], w_s.at[3], w_r.at[3], cores),
        copy(wfull.at[0, pl.ds(0, 3)], wfull.at[0, pl.ds(0, 3)], w_s.at[4], w_r.at[4], cores),
        gather_core(1 - core),
    )

    def weight_step(k):
        if k > 0:
            weight_all[k - 1].wait_recv()
        if k == 0:
            wcore_out[...] = weight_half(1 - core)
            weight_core.start()
            wsum[...] = weight_half(core).reshape(4, 64, WIDTH)
        elif k == 1:
            wsum[...] = wsum[...] + wcore_in[...].reshape(4, 64, WIDTH)
            for s in range(3):
                weight_y(s).start()
        elif k == 2:
            total = wsum[y]
            for s in range(3):
                total = total + wy_in[s]
            for s in range(16):
                i, j = s // 4, s % 4
                wgrid[s] = total[i * 16:(i + 1) * 16, j * TILE:(j + 1) * TILE]
            loop(15, lambda s: weight_grid(s + 1).start())
        elif k == 3:
            total = wgrid[spot]
            for s in range(1, 16):
                total = total + wgrid_in[s]
            ggrid[spot] = total.astype(BF16)
            loop(15, lambda s: gather_grid(s + 1).start())
        elif k == 4:
            for s in range(16):
                i, j = s // 4, s % 4
                wfull[core, y, i * 16:(i + 1) * 16, j * TILE:(j + 1) * TILE] = ggrid[s]
            for s in range(3):
                gather_y(s).start()
        elif k == 5:
            gather_core(core).start()
        else:
            gives[1].start()

    def product(p, i, j):
        total = None
        for y_ in range(2):
            start = chunk(p, (spots[p][0] + i) % 4, (spots[p][1] + j) % 4, y_) * NODES
            term = dot(grads[p, i, j, y_], dense[pl.ds(pl.multiple_of(start, NODES), NODES), :])
            total = term if total is None else total + term
        return total

    begun = set()

    def add(p, i, j):
        total, fresh = product(p, i, j), p not in begun
        begun.add(p)
        for r in range(PEERS):
            part = total[:, r * NODES:(r + 1) * NODES]
            terms[p, r] = part if fresh else terms[p, r] + part

    def pass_on(p, j):
        for d in range(2):
            first(p, 1 + 2 * d, j, mine).wait_recv()
            onward(p, j, d).start()

    def pass_pair(p, j):
        onward_both(p, j).wait_recv()
        far_pair(p, j, mine).start()

    def use_first(p, j):
        for i in (1, 3):
            first(p, i, j, other).wait_recv()
            add(p, i, j)

    def use_far(p, j):
        far_pair(p, j, other).wait_recv()
        add(p, 2, j)

    gives = (
        pltpu.make_async_copy(output, output_hbm, out_sem.at[0]),
        pltpu.make_async_copy(wfull, grad_weight_hbm, out_sem.at[1]),
        pltpu.make_async_copy(grad_features, grad_features_hbm, out_sem.at[2]),
    )

    def give_output():
        output[...] = (0.5 * v * (1.0 + t)).astype(BF16)
        gives[0].start()

    def give_own():
        for p in range(2):
            own(p, mine).start()

    def take_own(p):
        own(p, other).wait_recv()

    def give_firsts(p, j, y_):
        give_first(p, j, y_)

    def take_second(p, y_):
        second(p, 1, y_).wait_recv()
        second(p, 3, y_).wait_recv()
        second(p, 2, y_).start()

    def take_second2(p, y_):
        second(p, 2, y_).wait_recv()

    def use_own(p, j):
        add(p, 0, j)

    def cols1(p, h):
        return copy(col_out.at[p, h], col_in.at[p, h], c_s, c_r.at[p, h], cores)

    def cols2(p):
        return copy(col2_out.at[p], col2_in.at[p], c2_s, c2_r.at[p], across)

    def give_cols(p):
        for h in (1 - high, high):
            col_out[p, h] = terms[p, 2 * h + 1 - core].astype(BF16)
            cols1(p, h).start()

    def pass_cols(p):
        cols1(p, 1 - high).wait_recv()
        col2_out[p] = (terms[p, row_across] + col_in[p, 1 - high].astype(F32)).astype(BF16)
        cols2(p).start()

    for step in (
        (give_second, 0, mine), (give_second, 1, mine), (give_firsts, 1, 0, mine), (give_own,), (give_output,), (weight_step, 0),
        (give_firsts, 0, 0, mine), (take_own, 0), (take_second, 1, mine), (give_firsts, 1, 3, mine), (take_own, 1),
        (give_second, 1, other), (pass_on, 1, 0), (use_own, 0, 0), (pass_on, 0, 0), (give_second, 0, other),
        (give_firsts, 1, 1, mine), (take_second, 0, mine), (take_second2, 1, mine), (weight_step, 1),
        (give_firsts, 1, 2, mine), (pass_on, 1, 3), (give_firsts, 0, 1, mine), (pass_pair, 1, 0), (take_second, 1, other),
        (take_second, 0, other), (use_own, 1, 1), (use_own, 0, 1), (give_firsts, 0, 3, mine), (take_second2, 1, other),
        (pass_on, 0, 1), (pass_pair, 0, 0), (use_own, 1, 3), (take_second2, 0, mine), (pass_on, 0, 3), (weight_step, 2),
        (pass_on, 1, 1), (pass_pair, 0, 1), (give_firsts, 0, 2, mine), (pass_pair, 0, 3), (give_firsts, 1, 2, other),
        (pass_on, 1, 2), (pass_pair, 1, 3), (take_second2, 0, other), (pass_pair, 1, 1), (give_firsts, 0, 1, other),
        (give_firsts, 0, 3, other), (weight_step, 3), (use_own, 0, 3), (give_firsts, 1, 1, other), (pass_pair, 1, 2),
        (use_far, 1, 0), (give_firsts, 1, 3, other), (pass_on, 0, 2), (use_far, 0, 0), (use_far, 1, 3),
        (give_firsts, 0, 0, other), (give_firsts, 0, 2, other), (use_own, 1, 0), (use_first, 0, 1), (use_far, 0, 3),
        (give_firsts, 1, 0, other), (use_far, 0, 1), (use_far, 1, 1), (use_first, 1, 1), (pass_pair, 0, 2), (use_first, 1, 2),
        (use_first, 0, 3), (use_first, 1, 3), (weight_step, 4), (use_far, 1, 2), (use_own, 1, 2), (use_first, 0, 0),
        (use_first, 1, 0), (give_cols, 1), (use_own, 0, 2), (use_far, 0, 2), (use_first, 0, 2), (pass_cols, 1),
        (give_cols, 0), (pass_cols, 0), (weight_step, 5), (weight_step, 6),
    ):
        step[0](*step[1:])

    def sent(ref, sem):
        copy(ref, ref, sem, sem, pair).wait_send()

    for i, r in ((0, row), (1, row_across)):
        gather(i, r).wait_send()
    sent(pairs_out, pairs_s)
    sent(far_out, far_s)
    sent(near_out, near_s)
    sent(pairs2_out, pairs2_s)
    sent(far2_out, far2_s)
    sent(near2_out, near2_s)
    sent(pair_out, pair_s)
    sent(grads.at[0, 0, 0], g_s.at[0])
    sent(grads.at[0, 0], g_s.at[1])
    sent(grads.at[0, 0, pl.ds(0, 2)], g_s.at[2])
    sent(grads.at[0], g_s.at[3])
    sent(grads.at[0, 0], g_s.at[4])
    sent(grads.at[0, 0], g_s.at[5])
    for step in weight_all:
        step.wait_send()

    contract = (((1,), (1,)), ((), ()))
    total = jnp.zeros((NODES, WIDTH), F32)
    for p in (1, 0):
        cols1(p, high).wait_recv()
        cols2(p).wait_recv()
        value = (terms[p, row] + col_in[p, high].astype(F32) + col2_in[p].astype(F32)).T
        for part in split(value):
            total = total + lax.dot_general(
                part, weight[:, p * HALF:(p + 1) * HALF], contract, preferred_element_type=F32
            )
    grad_features[...] = total.astype(BF16)
    gives[2].start()
    sent(col_out, c_s)
    sent(col2_out, c2_s)
    for give in gives:
        give.wait()


def layer(features, features_across, weight, dense, output_grad):
    anywhere = pl.BlockSpec(memory_space=pl.ANY)
    dma = pltpu.SemaphoreType.DMA
    block = (NODES, HALF)
    bf = lambda *shape: pltpu.VMEM(shape, BF16)
    f32 = lambda *shape: pltpu.VMEM(shape, F32)
    return pl.pallas_call(
        layer_kernel,
        out_shape=(
            jax.ShapeDtypeStruct((NODES, WIDTH), BF16),
            jax.ShapeDtypeStruct((NODES, WIDTH), BF16),
            jax.ShapeDtypeStruct((2, 4, 64, WIDTH), BF16),
        ),
        in_specs=[anywhere] * 5,
        out_specs=(anywhere,) * 3,
        scratch_shapes=[
            bf(CHUNKS * NODES, COLS),
            bf(COLS, WIDTH),
            bf(WIDTH, WIDTH),
            bf(NODES, WIDTH),
            bf(NODES, WIDTH),
            bf(NODES, WIDTH),
            bf(2, NODES, WIDTH),
            bf(2, 4, *block), bf(2, 4, *block),
            bf(2, 4, *block), bf(2, 4, 2, TILE, HALF),
            bf(2, 4, 2, 2, *block), bf(2, 4, 2, 2, *block),
            bf(2, *block), bf(2, *block),
            bf(2, *block), bf(2, 2, TILE, HALF),
            bf(2, 2, 2, *block), bf(2, 2, 2, *block),
            bf(2, *block), bf(2, *block),
            f32(2, 2, *block),
            bf(2, 4, 4, 2, HALF, NODES),
            f32(2, PEERS, HALF, NODES),
            bf(2, 2, HALF, NODES), bf(2, 2, HALF, NODES),
            bf(2, HALF, NODES), bf(2, HALF, NODES),
            f32(HALF, WIDTH), f32(HALF, WIDTH),
            f32(4, 64, WIDTH),
            f32(3, 64, WIDTH),
            f32(16, 16, TILE), f32(16, 16, TILE),
            bf(16, 16, TILE),
            bf(2, 4, 64, WIDTH),
            dma((4, 4, 2)), dma((4,)), dma((3,)),
            dma((2,)), dma((2,)),
            dma, dma((2, 4)),
            dma, dma((2, 4, 2)),
            dma, dma((2, 4, 2)),
            dma, dma((2,)),
            dma, dma((2, 2)),
            dma, dma((2, 2)),
            dma, dma((2,)),
            dma((6,)), dma((2,)), dma((2, 3, 2)), dma((2, 2, 4, 2)), dma((2, 4)), dma((2, 4)),
            dma, dma((2, 2)),
            dma, dma((2,)),
            dma((6,)), dma((6,)),
        ],
        compiler_params=pltpu.CompilerParams(
            collective_id=0, has_side_effects=True, vmem_limit_bytes=LAYER_VMEM
        ),
        name="layer",
    )(features, features_across, weight, dense, output_grad)


def finish_kernel(first_in, second_in, weight_in, first, second, weight, first_at, second_at, weight_at, turned, in_sem, out_sem):
    loads = [
        pltpu.make_async_copy(src, dst, in_sem.at[i])
        for i, (src, dst) in enumerate(((weight_in, weight_at), (first_in, first_at), (second_in, second_at)))
    ]
    stores = [
        pltpu.make_async_copy(src, dst, out_sem.at[i])
        for i, (src, dst) in enumerate(((turned, weight), (first_at, first), (second_at, second)))
    ]
    for load in loads:
        load.start()
    loads[0].wait()
    turned[...] = weight_at[...].astype(F32).T
    stores[0].start()
    for load, store in zip(loads[1:], stores[1:]):
        load.wait()
        store.start()
    for store in stores:
        store.wait()


def finish(output, grad_features, grad_weight):
    anywhere = pl.BlockSpec(memory_space=pl.ANY)
    return pl.pallas_call(
        finish_kernel,
        out_shape=(
            jax.ShapeDtypeStruct(output.shape, BF16),
            jax.ShapeDtypeStruct(grad_features.shape, BF16),
            jax.ShapeDtypeStruct(grad_weight.shape, F32),
        ),
        in_specs=[anywhere] * 3,
        out_specs=(anywhere,) * 3,
        scratch_shapes=[
            pltpu.VMEM(output.shape, BF16),
            pltpu.VMEM(grad_features.shape, BF16),
            pltpu.VMEM(grad_weight.shape, BF16),
            pltpu.VMEM(grad_weight.shape, F32),
            pltpu.SemaphoreType.DMA((3,)),
            pltpu.SemaphoreType.DMA((3,)),
        ],
        compiler_params=pltpu.CompilerParams(vmem_limit_bytes=FINISH_VMEM),
        name="finish",
    )(output, grad_features, grad_weight)


def per_device(features, weight, tile_values, tile_rows, tile_cols, tile_count, output_grad):
    features_across = lax.ppermute(features, "row", [(r, (r + 2) % PEERS) for r in range(PEERS)])
    dense = place_tiles(tile_values, tile_rows, tile_cols, tile_count)
    output, grad_features, grad_weight = layer(features, features_across, weight, dense, output_grad)
    return finish(output, grad_features, grad_weight.reshape(WIDTH, WIDTH))


def solution(mesh):
    spread = P(("row", "col", "rep"))
    return jax.shard_map(
        per_device,
        mesh=mesh,
        in_specs=(
            P(("row", "col", "rep"), None),
            P(),
            P(("row", "col", "rep"), None, None),
            spread,
            spread,
            spread,
            P(("row", "col", "rep"), None),
        ),
        out_specs=(P(("row", "col", "rep"), None), P(("row", "col", "rep"), None), P()),
        check_vma=False,
    )
```
